256 devices in a mesh: seq: 8 (over x, core), head: 32 (over z, y).
Axes of the slice: x: 4, y: 4, z: 8, core: 2. Of those that a mesh axis runs over, the one named last changes fastest.
Arguments:
- x_rows: bfloat16 [40960, 12288], P('seq', 'head'), may hold values from -16 to 16
- z_rows: bfloat16 [40960, 12288], P('seq', 'head'), may hold values from -6 to 6
- b_rows: bfloat16 [40960, 128], P('seq', 'head'), may hold values from -6 to 6
- c_rows: bfloat16 [40960, 128], P('seq', 'head'), may hold values from -0.5 to 0.5
- step_raw: float32 [40960, 192], P('seq', 'head'), may hold values from -4 to 4
- conv_x: bfloat16 [4, 12288], P(None, 'head'), may hold values from -3 to 3
- conv_b: bfloat16 [4, 128], P(None, 'head'), may hold values from -3 to 3
- conv_c: bfloat16 [4, 128], P(None, 'head'), may hold values from -3 to 3
- decay_rate: float32 [192], P('head'), may hold values from 0 to 1, as said below
- norm_gain: float32 [12288], P('head'), may hold values from 0.5 to 1.5
Outputs:
- normed: bfloat16 [40960, 12288], P('seq', 'head')
The draws below stay inside these ranges and needn't reach their ends.
Inputs may be any that keep to these rules, and one draw needn't show every extreme that they name: `decay_rate`: positive rates.
All inputs are finite; a program needn't handle non-finite values.
Results may differ from the reference program's by a relative error of at most 0.011.
Values may be sent and summed in bfloat16 or wider, within the bound.
A program may use at most 128 MiB of HBM per device.

```python
import jax
import jax.numpy as jnp
from jax import lax

HEAD_SIZE = 64
STATE = 128
CONV = 4
GROUP = 256
HEADS = 192
TOKENS = 40960


def draw_x_rows(key, part):
    key = jax.random.fold_in(key, 11)
    first = jax.random.fold_in(key, 0)
    columns = HEADS * HEAD_SIZE
    heads = (jnp.arange(columns) // HEAD_SIZE).astype(jnp.float32)
    rising = jnp.exp(jnp.log(3.0) * heads / max(HEADS - 1, 1))
    base = jnp.clip(jax.random.normal(first, (TOKENS, columns), jnp.float32), -4.0, 4.0)
    return (base * rising[None, :]).astype(jnp.bfloat16)


def draw_step_raw(key, part):
    key = jax.random.fold_in(key, 23)
    first, second = jax.random.split(key)
    block = max(TOKENS // 16, 1)
    offsets = jax.random.uniform(second, (TOKENS // block + 1, HEADS), jnp.float32, -1.0, 1.0)
    shift = offsets[jnp.arange(TOKENS) // block]
    noise = jnp.clip(0.7 * jax.random.normal(first, (TOKENS, HEADS), jnp.float32), -2.5, 2.5)
    return noise + shift


def draw_decay_rate(key, part):
    key = jax.random.fold_in(key, 37)
    first, second, third = jax.random.split(key, 3)
    pick = jax.random.uniform(first, (HEADS,), jnp.float32)
    slow = jnp.exp(jax.random.uniform(second, (HEADS,), jnp.float32, 1.5, 3.0)) / TOKENS
    fast = jnp.exp(jax.random.uniform(third, (HEADS,), jnp.float32, -3.69, -3.1))
    share = 0.55
    return jnp.where(pick < share, slow, fast)


def block_scale(key, shape, shards, smallest, top_value):
    loudness = 1.0
    for dim, parts in shards:
        draws = jax.random.uniform(jax.random.fold_in(jax.random.fold_in(key, 6), dim), (parts,), jnp.float32, smallest / len(shards), top_value / len(shards))
        loudness = loudness * jnp.repeat(jnp.exp(draws), shape[dim] // parts).reshape((-1,) + (1,) * (len(shape) - 1 - dim))
    return loudness


def normal_values(key, extent, spread, limit, cuts=(), kind=jnp.bfloat16):
    factor_of = block_scale(key, extent, cuts, -0.22, 0.18) if cuts else 1.0
    values = jax.random.normal(key, extent, jnp.float32) * spread * factor_of
    return jnp.minimum(jnp.maximum(values, -limit), limit).astype(kind)


def setup_inputs(seed: int = 0) -> dict:
    keys = jax.random.split(jax.random.key(seed), 11)
    return {
        "x_rows": draw_x_rows(jax.random.fold_in(keys[10], 71), 0),
        "z_rows": normal_values(keys[1], (TOKENS, HEADS * HEAD_SIZE), 1.0, 6.0, ((0, 8), (1, 32))),
        "b_rows": normal_values(keys[2], (TOKENS, STATE), 1.0, 6.0, ((0, 8), (1, 32))),
        "c_rows": normal_values(keys[3], (TOKENS, STATE), STATE ** -0.5, 0.5, ((0, 8), (1, 32))),
        "step_raw": draw_step_raw(jax.random.fold_in(keys[10], 71), 0),
        "conv_x": normal_values(keys[5], (CONV, HEADS * HEAD_SIZE), CONV ** -0.5, 3.0, ((1, 32),)),
        "conv_b": normal_values(keys[6], (CONV, STATE), CONV ** -0.5, 3.0, ((1, 32),)),
        "conv_c": normal_values(keys[7], (CONV, STATE), CONV ** -0.5, 3.0, ((1, 32),)),
        "decay_rate": draw_decay_rate(jax.random.fold_in(keys[10], 71), 0),
        "norm_gain": jnp.clip(1.0 + 0.1 * jax.random.normal(keys[9], (HEADS * HEAD_SIZE,), jnp.float32), 0.5, 1.5),
    }


def conv_valid(padded, weights, length):
    total = jnp.zeros((length, padded.shape[1]), jnp.float32)
    for k in range(weights.shape[0]):
        total = total + weights[k].astype(jnp.float32)[None, :] * padded[k:k + length].astype(jnp.float32)
    return jax.nn.silu(total).astype(jnp.bfloat16)

def causal_conv(rows, weights):
    width = weights.shape[0]
    padded = jnp.concatenate([jnp.zeros((width - 1, rows.shape[1]), rows.dtype), rows], axis=0)
    return conv_valid(padded, weights, rows.shape[0])

def block_parts(x_block, b_block, c_block, step_block, cum_block):
    scores = jnp.dot(c_block, b_block.T, preferred_element_type=jnp.float32)
    order = jnp.arange(x_block.shape[0])
    causal = order[:, None] >= order[None, :]
    gap = cum_block.T[:, :, None] - cum_block.T[:, None, :]
    gap = jnp.where(causal[None], gap, -jnp.inf)
    mixing = (scores[None] * jnp.exp(gap) * step_block.T[:, None, :]).astype(jnp.bfloat16)
    diag = jnp.einsum('hts,shp->thp', mixing.astype(jnp.float32), x_block.astype(jnp.float32))
    tail = jnp.exp(cum_block[-1][None, :] - cum_block) * step_block
    weighted = (tail[:, :, None] * x_block.astype(jnp.float32)).astype(jnp.bfloat16)
    block_state = jnp.einsum('shp,sn->hpn', weighted.astype(jnp.float32), b_block.astype(jnp.float32))
    return (diag, block_state)

def reference(x_rows, z_rows, b_rows, c_rows, step_raw, conv_x, conv_b, conv_c, decay_rate, norm_gain):
    xs = causal_conv(x_rows, conv_x)
    bs = causal_conv(b_rows, conv_b)
    cs = causal_conv(c_rows, conv_c)
    step = jax.nn.softplus(step_raw)
    log_decay = -step * decay_rate[None, :]
    count = TOKENS // GROUP
    pieces = (xs.reshape(count, GROUP, HEADS, HEAD_SIZE), bs.reshape(count, GROUP, STATE), cs.reshape(count, GROUP, STATE), step.reshape(count, GROUP, HEADS), log_decay.reshape(count, GROUP, HEADS))

    def advance(state, piece):
        x_block, b_block, c_block, step_block, decay_block = piece
        cum = jnp.cumsum(decay_block, axis=0)
        diag, block_state = block_parts(x_block, b_block, c_block, step_block, cum)
        carried = jnp.einsum('hpn,tn->thp', state, c_block.astype(jnp.float32), precision=lax.Precision.HIGHEST) * jnp.exp(cum)[:, :, None]
        new_state = jnp.exp(cum[-1])[:, None, None] * state + block_state
        return (new_state, (diag + carried).reshape(GROUP, HEADS * HEAD_SIZE))
    start = jnp.zeros((HEADS, HEAD_SIZE, STATE), jnp.float32)
    _, outputs = lax.scan(advance, start, pieces)
    y_rows = outputs.reshape(TOKENS, HEADS * HEAD_SIZE)
    gated = y_rows * jax.nn.silu(z_rows.astype(jnp.float32))
    mean_sq = lax.optimization_barrier(jnp.sum(gated * gated, axis=1, keepdims=True)) / (HEADS * HEAD_SIZE)
    return (gated * lax.rsqrt(mean_sq + 1e-05) * norm_gain[None, :]).astype(jnp.bfloat16)
```

```python
import functools

import jax
import jax.numpy as jnp
from jax import lax
from jax.experimental import pallas as pl
from jax.experimental.pallas import tpu as pltpu
from jax.sharding import PartitionSpec as P

GROUP = 256
HALF = 128
HEADS = 6
WIDTH = 384
LENGTH = 5120
BLOCKS = 20
CHUNKS = 4
PER = BLOCKS // CHUNKS
NSEQ = 8
NZ = 8
NY = 4
NHEAD = NZ * NY
STATE = 128
PART = STATE // NSEQ
HALO = 16
MASKED = -1e30
F32 = jnp.float32
BF16 = jnp.bfloat16


def remote(src, dst, send, recv, **where):
    return pltpu.make_async_remote_copy(
        src_ref=src,
        dst_ref=dst,
        send_sem=send,
        recv_sem=recv,
        device_id=where,
        device_id_type=pl.DeviceIdType.MESH,
    )


def loop(count, body):
    lax.fori_loop(0, count, lambda i, _: (body(i), 0)[1], 0)


def dot(a, b):
    return jnp.dot(a, b, preferred_element_type=F32)


def layer(
    x_hbm,
    z_hbm,
    b_ref,
    c_ref,
    raw_ref,
    taps_ref,
    small_ref,
    g_hbm,
    total_ref,
    xbuf,
    zbuf,
    xs_even,
    xs_odd,
    near,
    far,
    gath,
    cmat,
    score,
    ydiag,
    local_state,
    colq,
    rowq,
    bq,
    stepq,
    bcx,
    prec,
    state,
    payload,
    got,
    back,
    carry_in,
    ssrow,
    sspart,
    tot,
    x_sem,
    z_sem,
    g_sem,
    halo_send,
    halo_recv,
    zs_send,
    zs_recv,
    ys_send,
    ys_recv,
    yf_send,
    yf_recv,
    st_send,
    st_recv,
    cb_send,
    cb_recv,
    ss_send,
    ss_recv,
    tt_send,
    tt_recv,
):
    seq = lax.axis_index("seq")
    head = lax.axis_index("head")
    my_z = head // NY
    my_y = head % NY
    rows = LENGTH // CHUNKS

    def x_copy(c):
        part = pl.multiple_of(c * rows, rows)
        return pltpu.make_async_copy(
            x_hbm.at[pl.ds(part, rows)], xbuf.at[pl.ds(HALO + part, rows)], x_sem.at[c]
        )

    z_copy = pltpu.make_async_copy(z_hbm, zbuf, z_sem)

    barrier = pltpu.get_barrier_semaphore()

    def greet(r):
        pl.semaphore_signal(
            barrier,
            inc=1,
            device_id={"head": lax.rem(head + 1 + r, NHEAD)},
            device_id_type=pl.DeviceIdType.MESH,
        )

    def greet_seq(r):
        pl.semaphore_signal(
            barrier,
            inc=1,
            device_id={"seq": lax.rem(seq + 1 + r, NSEQ)},
            device_id_type=pl.DeviceIdType.MESH,
        )

    loop(NSEQ - 1, greet_seq)
    loop(NHEAD - 1, greet)
    for c in range(CHUNKS):
        x_copy(c).start()
    z_copy.start()

    bcx[0:4, HALF:] = b_ref[...].astype(F32)
    bcx[4:8, HALF:] = c_ref[...].astype(F32)
    raw = raw_ref[...]
    stepq[...] = jnp.ones_like(stepq)
    step_all = jnp.maximum(raw, 0.0) + jnp.log1p(jnp.exp(-jnp.abs(raw)))
    for i in range(BLOCKS):
        stepq[i, 0:HEADS, :] = step_all[:, GROUP * i : GROUP * (i + 1)]
    small = small_ref[...]

    pl.semaphore_wait(barrier, NHEAD - 1 + NSEQ - 1)

    def halo_bc():
        return remote(
            bcx.at[:, pl.ds(LENGTH, HALF)],
            bcx.at[:, pl.ds(0, HALF)],
            halo_send.at[0],
            halo_recv.at[0],
            seq=lax.rem(seq + 1, NSEQ),
        )

    def halo_x():
        return remote(
            x_hbm.at[pl.ds(LENGTH - HALO, HALO)],
            xbuf.at[pl.ds(0, HALO)],
            halo_send.at[1],
            halo_recv.at[1],
            seq=lax.rem(seq + 1, NSEQ),
        )

    @pl.when(seq < NSEQ - 1)
    def _():
        halo_bc().start()
        halo_x().start()

    step = stepq[...]
    rate = small[:, 4:5]
    decay = -(step * rate[None])
    decay = decay.reshape(BLOCKS * 8, GROUP)
    row = lax.broadcasted_iota(jnp.int32, (GROUP, GROUP), 0)
    col = lax.broadcasted_iota(jnp.int32, (GROUP, GROUP), 1)
    upper = jnp.where(row <= col, 1.0, 0.0).astype(BF16)
    high = decay.astype(BF16)
    rest = decay - high.astype(F32)
    mid = rest.astype(BF16)
    low = (rest - mid.astype(F32)).astype(BF16)
    cum = dot(high, upper) + (dot(mid, upper) + dot(low, upper))
    last = cum[:, GROUP - 1 : GROUP]
    step2 = step.reshape(BLOCKS * 8, GROUP)
    rowq[:, 0:8, :] = cum.reshape(BLOCKS, 8, GROUP)
    rowq[:, 8:16, :] = (jnp.exp(last - cum) * step2).reshape(BLOCKS, 8, GROUP)
    rowq[:, 16:24, :] = jnp.exp(cum).reshape(BLOCKS, 8, GROUP)
    bq[...] = (cum - jnp.log(step2)).reshape(BLOCKS, 8, GROUP)

    @pl.when(seq > 0)
    def _():
        halo_bc().wait_recv()
        halo_x().wait_recv()

    @pl.when(seq == 0)
    def _():
        bcx[:, 0:HALF] = jnp.zeros((8, HALF), F32)
        xbuf[0:HALO, :] = jnp.zeros((HALO, WIDTH), BF16)

    ext = bcx[...]
    acc = ext[:, HALF:] * small[:, 3:4]
    for back_by in (1, 2, 3):
        acc = acc + pltpu.roll(ext, back_by, axis=1)[:, HALF:] * small[:, 3 - back_by : 4 - back_by]
    acc = acc + acc * jnp.tanh(acc)
    for i in range(BLOCKS):
        tile = jnp.concatenate(
            [
                acc[:, GROUP * i : GROUP * i + HALF],
                acc[:, GROUP * i + HALF : GROUP * (i + 1)],
            ],
            axis=0,
        )
        place = HALF * (i % PER)
        gath[i // PER, my_y, my_z, :, place : place + HALF] = tile.astype(BF16)

    def z_send(c, r):
        return remote(
            gath.at[c, my_y, my_z],
            gath.at[c, my_y, my_z],
            zs_send.at[c, r],
            zs_recv.at[c, my_z],
            head=lax.rem(my_z + r, NZ) * NY + my_y,
        )

    def z_arrive(c, r):
        other = lax.rem(my_z + r, NZ)
        return remote(
            gath.at[c, my_y, other],
            gath.at[c, my_y, other],
            zs_send.at[c, r],
            zs_recv.at[c, other],
            head=other * NY + my_y,
        )

    order = (1, 7, 2, 6, 3, 5, 4)
    for c in range(CHUNKS):
        for r in order:
            z_send(c, r).start()

    above = lax.rem(my_y + 1, NY)
    below = lax.rem(my_y + NY - 1, NY)
    across = lax.rem(my_y + 2, NY)
    ups = my_z * NY + above
    downs = my_z * NY + below

    def y_up(c, slot):
        ref = gath.at[c, slot]
        return remote(ref, ref, ys_send.at[c, 0], ys_recv.at[c, 0], head=ups)

    def y_down(c, slot):
        ref = gath.at[c, slot]
        return remote(ref, ref, ys_send.at[c, 1], ys_recv.at[c, 1], head=downs)

    def f_up(c, slot):
        ref = gath.at[c, slot, pl.ds(0, NZ // 2)]
        return remote(ref, ref, yf_send.at[c, 0], yf_recv.at[c, 0], head=ups)

    def f_down(c, slot):
        ref = gath.at[c, slot, pl.ds(NZ // 2, NZ // 2)]
        return remote(ref, ref, yf_send.at[c, 1], yf_recv.at[c, 1], head=downs)

    def event_z(c):
        for r in order:
            z_arrive(c, r).wait_recv()
        y_up(c, my_y).start()
        y_down(c, my_y).start()

    def event_f(c):
        y_up(c, below).wait_recv()
        f_up(c, below).start()
        y_down(c, above).wait_recv()
        f_down(c, above).start()

    def event_d(c):
        f_up(c, across).wait_recv()
        f_down(c, across).wait_recv()

    taps = taps_ref[...].astype(F32) * 0.5
    lanes = lax.broadcasted_iota(jnp.int32, (GROUP, WIDTH), 1)
    even = (lanes & 127) < 64
    row1 = lax.broadcasted_iota(jnp.int32, (HALF, HALF), 0)
    col1 = lax.broadcasted_iota(jnp.int32, (HALF, HALF), 1)
    causal = row1 >= col1

    def phase1(i):
        base = pl.multiple_of(i * GROUP, GROUP)
        wide = xbuf[pl.ds(base, GROUP + HALO), :].astype(F32)
        half = wide[HALO:] * taps[3:4]
        for back_by in (1, 2, 3):
            half = half + pltpu.roll(wide, back_by, axis=0)[HALO:] * taps[3 - back_by : 4 - back_by]
        xs = half + half * jnp.tanh(half)
        xs_even[pl.ds(base, GROUP), :] = jnp.where(even, xs, 0.0).astype(BF16)
        xs_odd[pl.ds(base, GROUP), :] = jnp.where(even, 0.0, xs).astype(BF16)
        cols = rowq[i].T
        colq[i] = cols
        b_all = bq[i]
        for h in range(HEADS):
            a = cols[:, h : h + 1]
            b = b_all[h : h + 1, :]
            near[i, h] = jnp.exp(jnp.where(causal, a[:HALF] - b[:, :HALF], MASKED)).astype(BF16)
            far[i, h, :, 0:HALF] = jnp.exp(a[HALF:] - b[:, :HALF]).astype(BF16)
            far[i, h, :, HALF:] = jnp.exp(
                jnp.where(causal, a[HALF:] - b[:, HALF:], MASKED)
            ).astype(BF16)

    def step1(i):
        @pl.when(lax.rem(i, PER) == 0)
        def _():
            x_copy(i // PER).wait()

        phase1(i)

        @pl.when(i == 6)
        def _():
            event_z(0)

        @pl.when(i == 12)
        def _():
            event_z(1)
            event_f(0)

        @pl.when(i == 18)
        def _():
            event_z(2)
            event_f(1)

    loop(BLOCKS, step1)

    spread_row = lax.broadcasted_iota(jnp.int32, (24, WIDTH), 0)
    spread_col = lax.broadcasted_iota(jnp.int32, (24, WIDTH), 1) >> 6
    spread_w = jnp.where(spread_row == spread_col + 8, 1.0, 0.0).astype(BF16)
    spread_e = jnp.where(spread_row == spread_col + 16, 1.0, 0.0).astype(BF16)
    of_head = lax.broadcasted_iota(jnp.int32, (8, WIDTH), 1) >> 6
    upper4 = lax.broadcasted_iota(jnp.int32, (8, HALF), 0) < 4

    state[...] = jnp.zeros_like(state)
    prec[0] = jnp.ones((8, WIDTH), F32)

    def phase2(i):
        c = i // PER
        lane = pl.multiple_of(lax.rem(i, PER) * HALF, HALF)
        b_rows, c_rows = [], []
        for pair in range(NHEAD // 2):
            y, z = (2 * pair) // NZ, (2 * pair) % NZ
            first = gath[c, y, z, :, pl.ds(lane, HALF)].astype(F32)
            second = gath[c, y, z + 1, :, pl.ds(lane, HALF)].astype(F32)
            b_cols, c_cols = [], []
            for part in range(2):
                one = first[8 * part : 8 * part + 8]
                two = second[8 * part : 8 * part + 8]
                b_cols.append(jnp.where(upper4, one, pltpu.roll(two, 4, axis=0)))
                c_cols.append(jnp.where(upper4, pltpu.roll(one, 4, axis=0), two))
            b_rows.append(jnp.concatenate(b_cols, axis=1))
            c_rows.append(jnp.concatenate(c_cols, axis=1))
        b_t = jnp.concatenate(b_rows, axis=0).astype(BF16)
        c_i = jnp.concatenate(c_rows, axis=0).T.astype(BF16)
        cmat[i] = c_i
        score[i] = dot(c_i, b_t).astype(BF16)
        base = pl.multiple_of(i * GROUP, GROUP)
        xs = (xs_even[pl.ds(base, GROUP), :] + xs_odd[pl.ds(base, GROUP), :]).astype(F32)
        cols = colq[i]
        weight = dot(cols.astype(BF16), spread_w)
        new = dot(b_t, (weight * xs).astype(BF16))
        ends = cols[GROUP - 8 :, 16:24]
        gone = jnp.zeros((8, WIDTH), F32)
        for h in range(HEADS):
            gone = jnp.where(of_head == h, ends[7:8, h : h + 1], gone)
        old = state[...]
        local_state[i] = old
        state[...] = old * gone[0:1] + new
        prec[i + 1] = prec[i] * gone

    def phase3(i):
        base = pl.multiple_of(i * GROUP, GROUP)
        scores = score[i]
        top = scores[:HALF, :HALF]
        low_rows = scores[HALF:, :]
        for pair in range(HEADS // 2):
            span = slice(HALF * pair, HALF * (pair + 1))
            xe = xs_even[pl.ds(base, GROUP), span]
            xo = xs_odd[pl.ds(base, GROUP), span]
            m1 = jnp.concatenate([top * near[i, 2 * pair], top * near[i, 2 * pair + 1]], axis=1)
            x1 = jnp.concatenate([xe[:HALF], xo[:HALF]], axis=0)
            ydiag[pl.ds(base, HALF), span] = dot(m1, x1)
            m2 = jnp.concatenate(
                [low_rows * far[i, 2 * pair], low_rows * far[i, 2 * pair + 1]], axis=1
            )
            x2 = jnp.concatenate([xe, xo], axis=0)
            ydiag[pl.ds(base + HALF, HALF), span] = dot(m2, x2)

    def early(c):
        @pl.when(c == 0)
        def _():
            event_d(0)
            event_z(3)
            event_f(2)

        @pl.when(c == 1)
        def _():
            event_d(1)
            event_f(3)

        loop(PER, lambda j: phase2(c * PER + j))
        loop(PER, lambda j: phase3(c * PER + j))

    loop(2, early)

    def late(c):
        event_d(2 + c)
        loop(PER, lambda j: phase2((2 + c) * PER + j))

    loop(2, late)

    for j in range(NSEQ):
        payload[j, 0:PART, :] = state[PART * j : PART * (j + 1), :]
        payload[j, PART : PART + 8, :] = prec[BLOCKS]

    def st_copy(j, slot):
        return remote(payload.at[j], got.at[slot], st_send.at[j], st_recv.at[slot], seq=j)

    def cb_copy(j, slot):
        place = pl.multiple_of(slot * PART, PART)
        return remote(
            back.at[j], carry_in.at[pl.ds(place, PART)], cb_send.at[j], cb_recv.at[slot], seq=j
        )

    def others(count, me, body):
        loop(count - 1, lambda r: body(lax.rem(me + 1 + r, count)))

    others(NSEQ, seq, lambda j: st_copy(j, seq).start())
    got[seq] = payload[seq]
    loop(PER, lambda j: phase3(2 * PER + j))
    others(NSEQ, seq, lambda j: st_copy(j, j).wait_recv())
    carry = jnp.zeros((PART, WIDTH), F32)
    for j in range(NSEQ):
        back[j] = carry
        carry = carry * got[j, PART : PART + 1, :] + got[j, 0:PART, :]
    others(NSEQ, seq, lambda j: cb_copy(j, seq).start())
    carry_in[pl.ds(pl.multiple_of(seq * PART, PART), PART), :] = back[seq]
    loop(PER, lambda j: phase3(3 * PER + j))
    others(NSEQ, seq, lambda j: cb_copy(j, j).wait_recv())
    z_copy.wait()

    ones = jnp.ones((8, WIDTH), BF16)

    def g_copy(i):
        base = pl.multiple_of(i * GROUP, GROUP)
        return pltpu.make_async_copy(
            xbuf.at[pl.ds(HALO + base, GROUP)], g_hbm.at[pl.ds(base, GROUP)], g_sem.at[i]
        )

    def ss_copy(i):
        return remote(ssrow.at[i], sspart.at[head], ss_send.at[i], ss_recv.at[head], head=i)

    def ss_arrive(j):
        return remote(ssrow.at[0], sspart.at[j], ss_send.at[0], ss_recv.at[j], head=j)

    def tt_copy(j):
        return remote(tot.at[head], tot.at[head], tt_send.at[j], tt_recv.at[head], head=j)

    def tt_arrive(i):
        return remote(tot.at[i], tot.at[i], tt_send.at[0], tt_recv.at[i], head=i)

    def own_total():
        others(NHEAD, head, lambda j: ss_arrive(j).wait_recv())
        tot[head] = jnp.sum(sspart[...], axis=0)
        others(NHEAD, head, lambda j: tt_copy(j).start())

    def phase4(i):
        base = pl.multiple_of(i * GROUP, GROUP)
        whole = local_state[i] + carry_in[...] * prec[i][0:1]
        carried = dot(cmat[i], whole.astype(BF16))
        grown = dot(colq[i].astype(BF16), spread_e)
        y = ydiag[pl.ds(base, GROUP), :] + carried * grown
        half = zbuf[pl.ds(base, GROUP), :].astype(F32) * 0.5
        g = y * (half + half * jnp.tanh(half))
        xbuf[pl.ds(HALO + base, GROUP), :] = g.astype(BF16)
        g_copy(i).start()
        squares = (g * g).astype(BF16)
        sums = lax.dot_general(ones, squares, (((1,), (1,)), ((), ())), preferred_element_type=F32)
        ssrow[i] = sums[0:1]

        @pl.when(head == i)
        def _():
            sspart[head] = sums[0:1]

        @pl.when(head != i)
        def _():
            ss_copy(i).start()

        @pl.when(head == i - 2)
        def _():
            own_total()

    loop(BLOCKS, phase4)

    @pl.when((head == BLOCKS - 2) | (head == BLOCKS - 1))
    def _():
        own_total()

    @pl.when(seq < NSEQ - 1)
    def _():
        halo_bc().wait_send()
        halo_x().wait_send()

    def finish(c):
        for r in order:
            z_send(c, r).wait_send()
        y_up(c, my_y).wait_send()
        y_down(c, my_y).wait_send()
        f_up(c, below).wait_send()
        f_down(c, above).wait_send()

    loop(CHUNKS, finish)
    others(NSEQ, seq, lambda j: st_copy(j, seq).wait_send())
    others(NSEQ, seq, lambda j: cb_copy(j, seq).wait_send())

    def finish_block(i):
        g_copy(i).wait()

        @pl.when(head != i)
        def _():
            ss_copy(i).wait_send()
            tt_arrive(i).wait_recv()

    loop(BLOCKS, finish_block)

    @pl.when(head < BLOCKS)
    def _():
        others(NHEAD, head, lambda j: tt_copy(j).wait_send())

    total_ref[...] = tot[...]


def scale(g_ref, total_ref, gain_ref, out_ref):
    gain = gain_ref[...]
    for j in range(4):
        mean = total_ref[j] * (1.0 / (NHEAD * WIDTH))
        row = lax.rsqrt(mean + 1e-05)
        column = jnp.broadcast_to(row, (8, GROUP)).T[:, 0:1]
        rows = slice(GROUP * j, GROUP * (j + 1))
        out_ref[rows, :] = (g_ref[rows, :].astype(F32) * column * gain).astype(BF16)


def body(x_rows, z_rows, b_rows, c_rows, step_raw, conv_x, conv_b, conv_c, decay_rate, norm_gain):
    small = jnp.concatenate(
        [
            jnp.concatenate([conv_b, conv_c], axis=1).T.astype(F32) * 0.5,
            jnp.pad(decay_rate, (0, 2))[:, None],
            jnp.zeros((8, 3), F32),
        ],
        axis=1,
    )
    vmem = pl.BlockSpec(memory_space=pltpu.VMEM)
    hbm = pl.BlockSpec(memory_space=pl.ANY)
    dma = pltpu.SemaphoreType.DMA
    g, totals = pl.pallas_call(
        layer,
        out_shape=(
            jax.ShapeDtypeStruct((LENGTH, WIDTH), BF16),
            jax.ShapeDtypeStruct((BLOCKS, 1, GROUP), F32),
        ),
        in_specs=[hbm, hbm, vmem, vmem, vmem, vmem, vmem],
        out_specs=(hbm, vmem),
        scratch_shapes=[
            pltpu.VMEM((HALO + LENGTH, WIDTH), BF16),
            pltpu.VMEM((LENGTH, WIDTH), BF16),
            pltpu.VMEM((LENGTH, WIDTH), BF16),
            pltpu.VMEM((LENGTH, WIDTH), BF16),
            pltpu.VMEM((BLOCKS, HEADS, HALF, HALF), BF16),
            pltpu.VMEM((BLOCKS, HEADS, HALF, GROUP), BF16),
            pltpu.VMEM((CHUNKS, NY, NZ, 16, HALF * PER), BF16),
            pltpu.VMEM((BLOCKS, GROUP, STATE), BF16),
            pltpu.VMEM((BLOCKS, GROUP, GROUP), BF16),
            pltpu.VMEM((LENGTH, WIDTH), F32),
            pltpu.VMEM((BLOCKS, STATE, WIDTH), F32),
            pltpu.VMEM((BLOCKS, GROUP, 24), F32),
            pltpu.VMEM((BLOCKS, 24, GROUP), F32),
            pltpu.VMEM((BLOCKS, 8, GROUP), F32),
            pltpu.VMEM((BLOCKS, 8, GROUP), F32),
            pltpu.VMEM((8, HALF + LENGTH), F32),
            pltpu.VMEM((BLOCKS + 1, 8, WIDTH), F32),
            pltpu.VMEM((STATE, WIDTH), F32),
            pltpu.VMEM((NSEQ, PART + 8, WIDTH), F32),
            pltpu.VMEM((NSEQ, PART + 8, WIDTH), F32),
            pltpu.VMEM((NSEQ, PART, WIDTH), F32),
            pltpu.VMEM((STATE, WIDTH), F32),
            pltpu.VMEM((BLOCKS, 1, GROUP), F32),
            pltpu.VMEM((NHEAD, 1, GROUP), F32),
            pltpu.VMEM((BLOCKS, 1, GROUP), F32),
            dma((CHUNKS,)),
            dma,
            dma((BLOCKS,)),
            dma((2,)),
            dma((2,)),
            dma((CHUNKS, NZ)),
            dma((CHUNKS, NZ)),
            dma((CHUNKS, 2)),
            dma((CHUNKS, 2)),
            dma((CHUNKS, 2)),
            dma((CHUNKS, 2)),
            dma((NSEQ,)),
            dma((NSEQ,)),
            dma((NSEQ,)),
            dma((NSEQ,)),
            dma((BLOCKS,)),
            dma((NHEAD,)),
            dma((NHEAD,)),
            dma((BLOCKS,)),
        ],
        compiler_params=pltpu.CompilerParams(
            collective_id=0, has_side_effects=True, vmem_limit_bytes=60 * 2**20
        ),
        name="layer",
    )(x_rows, z_rows, b_rows.T, c_rows.T, step_raw.T, conv_x, small)
    return pl.pallas_call(
        scale,
        out_shape=jax.ShapeDtypeStruct((LENGTH, WIDTH), BF16),
        grid=(5,),
        in_specs=[
            pl.BlockSpec((1024, WIDTH), lambda i: (i, 0)),
            pl.BlockSpec((4, 1, GROUP), lambda i: (i, 0, 0)),
            pl.BlockSpec((1, WIDTH), lambda i: (0, 0)),
        ],
        out_specs=pl.BlockSpec((1024, WIDTH), lambda i: (i, 0)),
        name="scale",
    )(g, totals, norm_gain[None, :])


def solution(mesh):
    placed = (
        P("seq", "head"),
        P("seq", "head"),
        P("seq", "head"),
        P("seq", "head"),
        P("seq", "head"),
        P(None, "head"),
        P(None, "head"),
        P(None, "head"),
        P("head"),
        P("head"),
    )
    return jax.shard_map(
        body, mesh=mesh, in_specs=placed, out_specs=P("seq", "head"), check_vma=False
    )
```

```python
import functools

import jax
import jax.numpy as jnp
from jax import lax
from jax.experimental import pallas as pl
from jax.experimental.pallas import tpu as pltpu
from jax.sharding import PartitionSpec as P

GROUP = 256
HALF = 128
HEADS = 6
WIDTH = 384
LENGTH = 5120
BLOCKS = 20
CHUNKS = 4
PER = BLOCKS // CHUNKS
SIDE = CHUNKS - 1
SCALED = 4
NSEQ = 8
NZ = 8
NY = 4
NHEAD = NZ * NY
STATE = 128
PART = STATE // NSEQ
HALO = 16
MASKED = -1e30
F32 = jnp.float32
BF16 = jnp.bfloat16


def remote(src, dst, send, recv, **where):
    return pltpu.make_async_remote_copy(
        src_ref=src,
        dst_ref=dst,
        send_sem=send,
        recv_sem=recv,
        device_id=where,
        device_id_type=pl.DeviceIdType.MESH,
    )


def loop(count, body):
    lax.fori_loop(0, count, lambda i, _: (body(i), 0)[1], 0)


def dot(a, b):
    return jnp.dot(a, b, preferred_element_type=F32)


def layer(
    x_hbm,
    z_hbm,
    b_ref,
    c_ref,
    raw_ref,
    taps_ref,
    taps_b_ref,
    taps_c_ref,
    rate_ref,
    g_hbm,
    total_ref,
    xbuf,
    zbuf,
    xs_even,
    xs_odd,
    near,
    far,
    gath,
    cmat,
    score,
    ydiag,
    local_state,
    colq,
    rowq,
    bq,
    stepq,
    bcx,
    prec,
    state,
    payload,
    got,
    back,
    carry_in,
    sums_row,
    sums_z,
    half_sums,
    sums_y,
    x_sem,
    z_sem,
    g_sem,
    halo_send,
    halo_recv,
    zs_send,
    zs_recv,
    ys_send,
    ys_recv,
    yf_send,
    yf_recv,
    st_send,
    st_recv,
    cb_send,
    cb_recv,
    side_out,
    side_in,
    ring_out,
    ring_in,
    sz_send,
    sz_recv,
    sy_send,
    sy_recv,
):
    seq = lax.axis_index("seq")
    head = lax.axis_index("head")
    my_z = head // NY
    my_y = head % NY
    rows = LENGTH // CHUNKS

    def x_copy(c):
        part = pl.multiple_of(c * rows, rows)
        return pltpu.make_async_copy(
            x_hbm.at[pl.ds(part, rows)], xbuf.at[pl.ds(HALO + part, rows)], x_sem.at[c]
        )

    z_copy = pltpu.make_async_copy(z_hbm, zbuf, z_sem)

    barrier = pltpu.get_barrier_semaphore()

    def greet(**where):
        pl.semaphore_signal(
            barrier, inc=1, device_id=where, device_id_type=pl.DeviceIdType.MESH
        )

    for r in range(1, NZ):
        greet(head=lax.rem(my_z + r, NZ) * NY + my_y)
    for r in range(1, NY):
        greet(head=my_z * NY + lax.rem(my_y + r, NY))
    for r in range(1, NSEQ):
        greet(seq=lax.rem(seq + r, NSEQ))
    for c in range(CHUNKS):
        x_copy(c).start()
    z_copy.start()

    bcx[0:4, HALF:] = b_ref[...].astype(F32)
    bcx[4:8, HALF:] = c_ref[...].astype(F32)
    raw = raw_ref[...]
    stepq[...] = jnp.ones_like(stepq)
    step_all = jnp.maximum(raw, 0.0) + jnp.log1p(jnp.exp(-jnp.abs(raw)))
    for i in range(BLOCKS):
        stepq[i, 0:HEADS, :] = step_all[:, GROUP * i : GROUP * (i + 1)]
    taps_bc = jnp.concatenate([taps_b_ref[...].astype(F32), taps_c_ref[...].astype(F32)], axis=1)
    taps_bc = taps_bc.T * 0.5
    head_row = lax.broadcasted_iota(jnp.int32, (8, GROUP), 0)
    rate = jnp.zeros((8, GROUP), F32)
    for h in range(HEADS):
        rate = jnp.where(head_row == h, rate_ref[h], rate)
    sums_row[...] = jnp.zeros_like(sums_row)

    pl.semaphore_wait(barrier, NZ - 1 + NY - 1 + NSEQ - 1)

    def halo_bc():
        return remote(
            bcx.at[:, pl.ds(LENGTH, HALF)],
            bcx.at[:, pl.ds(0, HALF)],
            halo_send.at[0],
            halo_recv.at[0],
            seq=lax.rem(seq + 1, NSEQ),
        )

    def halo_x():
        return remote(
            x_hbm.at[pl.ds(LENGTH - HALO, HALO)],
            xbuf.at[pl.ds(0, HALO)],
            halo_send.at[1],
            halo_recv.at[1],
            seq=lax.rem(seq + 1, NSEQ),
        )

    @pl.when(seq < NSEQ - 1)
    def _():
        halo_bc().start()
        halo_x().start()

    step = stepq[...]
    decay = -(step * rate[None])
    decay = decay.reshape(BLOCKS * 8, GROUP)
    row = lax.broadcasted_iota(jnp.int32, (GROUP, GROUP), 0)
    col = lax.broadcasted_iota(jnp.int32, (GROUP, GROUP), 1)
    upper = jnp.where(row <= col, 1.0, 0.0).astype(BF16)
    high = decay.astype(BF16)
    rest = decay - high.astype(F32)
    mid = rest.astype(BF16)
    low = (rest - mid.astype(F32)).astype(BF16)
    cum = dot(high, upper) + (dot(mid, upper) + dot(low, upper))
    last = cum[:, GROUP - 1 : GROUP]
    step2 = step.reshape(BLOCKS * 8, GROUP)
    rowq[:, 0:8, :] = cum.reshape(BLOCKS, 8, GROUP)
    rowq[:, 8:16, :] = (jnp.exp(last - cum) * step2).reshape(BLOCKS, 8, GROUP)
    rowq[:, 16:24, :] = jnp.exp(cum).reshape(BLOCKS, 8, GROUP)
    bq[...] = (cum - jnp.log(step2)).reshape(BLOCKS, 8, GROUP)

    @pl.when(seq > 0)
    def _():
        halo_bc().wait_recv()
        halo_x().wait_recv()

    @pl.when(seq == 0)
    def _():
        bcx[:, 0:HALF] = jnp.zeros((8, HALF), F32)
        xbuf[0:HALO, :] = jnp.zeros((HALO, WIDTH), BF16)

    ext = bcx[...]
    acc = ext[:, HALF:] * taps_bc[:, 3:4]
    for back_by in (1, 2, 3):
        acc = acc + pltpu.roll(ext, back_by, axis=1)[:, HALF:] * taps_bc[:, 3 - back_by : 4 - back_by]
    acc = acc + acc * jnp.tanh(acc)
    for i in range(BLOCKS):
        tile = jnp.concatenate(
            [
                acc[:, GROUP * i : GROUP * i + HALF],
                acc[:, GROUP * i + HALF : GROUP * (i + 1)],
            ],
            axis=0,
        )
        place = HALF * (i % PER)
        gath[i // PER, my_y, my_z, :, place : place + HALF] = tile.astype(BF16)

    def z_send(c, r):
        return remote(
            gath.at[c, my_y, my_z],
            gath.at[c, my_y, my_z],
            zs_send.at[c, r],
            zs_recv.at[c, my_z],
            head=lax.rem(my_z + r, NZ) * NY + my_y,
        )

    def z_arrive(c, r):
        other = lax.rem(my_z + r, NZ)
        return remote(
            gath.at[c, my_y, other],
            gath.at[c, my_y, other],
            zs_send.at[c, r],
            zs_recv.at[c, other],
            head=other * NY + my_y,
        )

    order = (1, 7, 2, 6, 3, 5, 4)
    def side_send(r):
        ref = gath.at[SIDE, my_y, my_z]
        there = my_z * NY + lax.rem(my_y + r, NY)
        return remote(ref, ref, side_out.at[r], side_in.at[my_y], head=there)

    def side_arrive(r):
        other = lax.rem(my_y + r, NY)
        ref = gath.at[SIDE, other, my_z]
        return remote(ref, ref, side_out.at[r], side_in.at[other], head=my_z * NY + other)

    for r in (1, 3, 2):
        side_send(r).start()
    for c in range(SIDE):
        for r in order:
            z_send(c, r).start()

    above = lax.rem(my_y + 1, NY)
    below = lax.rem(my_y + NY - 1, NY)
    across = lax.rem(my_y + 2, NY)
    ups = my_z * NY + above
    downs = my_z * NY + below

    def y_up(c, slot):
        ref = gath.at[c, slot]
        return remote(ref, ref, ys_send.at[c, 0], ys_recv.at[c, 0], head=ups)

    def y_down(c, slot):
        ref = gath.at[c, slot]
        return remote(ref, ref, ys_send.at[c, 1], ys_recv.at[c, 1], head=downs)

    def f_up(c, slot):
        ref = gath.at[c, slot, pl.ds(0, NZ // 2)]
        return remote(ref, ref, yf_send.at[c, 0], yf_recv.at[c, 0], head=ups)

    def f_down(c, slot):
        ref = gath.at[c, slot, pl.ds(NZ // 2, NZ // 2)]
        return remote(ref, ref, yf_send.at[c, 1], yf_recv.at[c, 1], head=downs)

    z_above = lax.rem(my_z + 1, NZ) * NY + my_y
    z_below = lax.rem(my_z + NZ - 1, NZ) * NY + my_y

    def ring(hop, up, block):
        half = NY // 2
        if hop < NZ // 2 - 1:
            ref = gath.at[SIDE, :, block]
        elif up:
            ref = gath.at[SIDE, pl.ds(0, half), block]
        else:
            ref = gath.at[SIDE, pl.ds(half, half), block]
        way = 0 if up else 1
        return remote(
            ref,
            ref,
            ring_out.at[hop, way],
            ring_in.at[hop, way],
            head=z_above if up else z_below,
        )

    def ring_send(hop):
        ring(hop, True, lax.rem(my_z + NZ - hop, NZ)).start()
        ring(hop, False, lax.rem(my_z + hop, NZ)).start()

    def ring_arrive(hop):
        ring(hop, True, lax.rem(my_z + NZ - hop - 1, NZ)).wait_recv()
        ring(hop, False, lax.rem(my_z + hop + 1, NZ)).wait_recv()

    def ring_done(hop):
        ring(hop, True, lax.rem(my_z + NZ - hop, NZ)).wait_send()
        ring(hop, False, lax.rem(my_z + hop, NZ)).wait_send()

    def event_side():
        for r in (1, 3, 2):
            side_arrive(r).wait_recv()
        ring_send(0)

    def event_ring(hop):
        ring_arrive(hop - 1)
        ring_send(hop)

    def event_z(c):
        for r in order:
            z_arrive(c, r).wait_recv()
        y_up(c, my_y).start()
        y_down(c, my_y).start()

    def event_f(c):
        y_up(c, below).wait_recv()
        f_up(c, below).start()
        y_down(c, above).wait_recv()
        f_down(c, above).start()

    def event_d(c):
        f_up(c, across).wait_recv()
        f_down(c, across).wait_recv()

    taps = taps_ref[...].astype(F32) * 0.5
    lanes = lax.broadcasted_iota(jnp.int32, (GROUP, WIDTH), 1)
    even = (lanes & 127) < 64
    row1 = lax.broadcasted_iota(jnp.int32, (HALF, HALF), 0)
    col1 = lax.broadcasted_iota(jnp.int32, (HALF, HALF), 1)
    causal = row1 >= col1

    def phase1(i):
        base = pl.multiple_of(i * GROUP, GROUP)
        wide = xbuf[pl.ds(base, GROUP + HALO), :].astype(F32)
        half = wide[HALO:] * taps[3:4]
        for back_by in (1, 2, 3):
            half = half + pltpu.roll(wide, back_by, axis=0)[HALO:] * taps[3 - back_by : 4 - back_by]
        xs = half + half * jnp.tanh(half)
        xs_even[pl.ds(base, GROUP), :] = jnp.where(even, xs, 0.0).astype(BF16)
        xs_odd[pl.ds(base, GROUP), :] = jnp.where(even, 0.0, xs).astype(BF16)
        cols = rowq[i].T
        colq[i] = cols
        b_all = bq[i]
        for h in range(HEADS):
            a = cols[:, h : h + 1]
            b = b_all[h : h + 1, :]
            near[i, h] = jnp.exp(jnp.where(causal, a[:HALF] - b[:, :HALF], MASKED)).astype(BF16)
            far[i, h, :, 0:HALF] = jnp.exp(a[HALF:] - b[:, :HALF]).astype(BF16)
            far[i, h, :, HALF:] = jnp.exp(
                jnp.where(causal, a[HALF:] - b[:, HALF:], MASKED)
            ).astype(BF16)

    def step1(i):
        @pl.when(lax.rem(i, PER) == 0)
        def _():
            x_copy(i // PER).wait()

        phase1(i)

        @pl.when(i == 4)
        def _():
            event_side()

        @pl.when(i == 9)
        def _():
            event_z(0)

        @pl.when(i == 12)
        def _():
            event_ring(1)

        @pl.when(i == 15)
        def _():
            event_z(1)

        @pl.when(i == 17)
        def _():
            event_f(0)
            event_ring(2)

    loop(BLOCKS, step1)

    spread_row = lax.broadcasted_iota(jnp.int32, (24, WIDTH), 0)
    spread_col = lax.broadcasted_iota(jnp.int32, (24, WIDTH), 1) >> 6
    spread_w = jnp.where(spread_row == spread_col + 8, 1.0, 0.0).astype(BF16)
    spread_e = jnp.where(spread_row == spread_col + 16, 1.0, 0.0).astype(BF16)
    of_head = lax.broadcasted_iota(jnp.int32, (8, WIDTH), 1) >> 6
    upper4 = lax.broadcasted_iota(jnp.int32, (8, HALF), 0) < 4

    state[...] = jnp.zeros_like(state)
    prec[0] = jnp.ones((8, WIDTH), F32)

    def phase2(i):
        c = i // PER
        lane = pl.multiple_of(lax.rem(i, PER) * HALF, HALF)
        b_rows, c_rows = [], []
        for pair in range(NHEAD // 2):
            y, z = (2 * pair) // NZ, (2 * pair) % NZ
            first = gath[c, y, z, :, pl.ds(lane, HALF)].astype(F32)
            second = gath[c, y, z + 1, :, pl.ds(lane, HALF)].astype(F32)
            b_cols, c_cols = [], []
            for part in range(2):
                one = first[8 * part : 8 * part + 8]
                two = second[8 * part : 8 * part + 8]
                b_cols.append(jnp.where(upper4, one, pltpu.roll(two, 4, axis=0)))
                c_cols.append(jnp.where(upper4, pltpu.roll(one, 4, axis=0), two))
            b_rows.append(jnp.concatenate(b_cols, axis=1))
            c_rows.append(jnp.concatenate(c_cols, axis=1))
        b_t = jnp.concatenate(b_rows, axis=0).astype(BF16)
        c_i = jnp.concatenate(c_rows, axis=0).T.astype(BF16)
        cmat[i] = c_i
        score[i] = dot(c_i, b_t).astype(BF16)
        base = pl.multiple_of(i * GROUP, GROUP)
        xs = (xs_even[pl.ds(base, GROUP), :] + xs_odd[pl.ds(base, GROUP), :]).astype(F32)
        cols = colq[i]
        weight = dot(cols.astype(BF16), spread_w)
        new = dot(b_t, (weight * xs).astype(BF16))
        ends = cols[GROUP - 8 :, 16:24]
        gone = jnp.zeros((8, WIDTH), F32)
        for h in range(HEADS):
            gone = jnp.where(of_head == h, ends[7:8, h : h + 1], gone)
        old = state[...]
        local_state[i] = old
        state[...] = old * gone[0:1] + new
        prec[i + 1] = prec[i] * gone

    def phase3(i):
        base = pl.multiple_of(i * GROUP, GROUP)
        scores = score[i]
        top = scores[:HALF, :HALF]
        low_rows = scores[HALF:, :]
        for pair in range(HEADS // 2):
            span = slice(HALF * pair, HALF * (pair + 1))
            xe = xs_even[pl.ds(base, GROUP), span]
            xo = xs_odd[pl.ds(base, GROUP), span]
            m1 = jnp.concatenate([top * near[i, 2 * pair], top * near[i, 2 * pair + 1]], axis=1)
            x1 = jnp.concatenate([xe[:HALF], xo[:HALF]], axis=0)
            ydiag[pl.ds(base, HALF), span] = dot(m1, x1)
            m2 = jnp.concatenate(
                [low_rows * far[i, 2 * pair], low_rows * far[i, 2 * pair + 1]], axis=1
            )
            x2 = jnp.concatenate([xe, xo], axis=0)
            ydiag[pl.ds(base + HALF, HALF), span] = dot(m2, x2)

    def early(c):
        event_d(c)
        loop(PER, lambda j: phase2(c * PER + j))

        @pl.when(c == 0)
        def _():
            event_z(2)
            event_f(1)
            event_ring(3)

        @pl.when(c == 1)
        def _():
            event_f(2)

        loop(PER, lambda j: phase3(c * PER + j))

    loop(2, early)

    def late(c):
        @pl.when(c == 0)
        def _():
            event_d(2)

        @pl.when(c == 1)
        def _():
            ring_arrive(NZ // 2 - 1)

        loop(PER, lambda j: phase2((2 + c) * PER + j))

    loop(2, late)

    for j in range(NSEQ):
        payload[j, 0:PART, :] = state[PART * j : PART * (j + 1), :]
        payload[j, PART : PART + 8, :] = prec[BLOCKS]

    def st_copy(j, slot):
        return remote(payload.at[j], got.at[slot], st_send.at[j], st_recv.at[slot], seq=j)

    def cb_copy(j, slot):
        place = pl.multiple_of(slot * PART, PART)
        return remote(
            back.at[j], carry_in.at[pl.ds(place, PART)], cb_send.at[j], cb_recv.at[slot], seq=j
        )

    def others(count, me, body):
        loop(count - 1, lambda r: body(lax.rem(me + 1 + r, count)))

    others(NSEQ, seq, lambda j: st_copy(j, seq).start())
    got[seq] = payload[seq]
    loop(PER, lambda j: phase3(2 * PER + j))
    others(NSEQ, seq, lambda j: st_copy(j, j).wait_recv())
    carry = jnp.zeros((PART, WIDTH), F32)
    for j in range(NSEQ):
        back[j] = carry
        carry = carry * got[j, PART : PART + 1, :] + got[j, 0:PART, :]
    others(NSEQ, seq, lambda j: cb_copy(j, seq).start())
    carry_in[pl.ds(pl.multiple_of(seq * PART, PART), PART), :] = back[seq]
    loop(PER, lambda j: phase3(3 * PER + j))
    others(NSEQ, seq, lambda j: cb_copy(j, j).wait_recv())
    z_copy.wait()

    ones = jnp.ones((8, WIDTH), BF16)

    def g_copy(i):
        base = pl.multiple_of(i * GROUP, GROUP)
        return pltpu.make_async_copy(
            xbuf.at[pl.ds(HALO + base, GROUP)], g_hbm.at[pl.ds(base, GROUP)], g_sem.at[i]
        )

    parts = (pl.ds(0, 16), pl.ds(16, 8))

    def sz_copy(p, r):
        there = lax.rem(my_z + r, NZ) * NY + my_y
        return remote(
            sums_row.at[parts[p]],
            sums_z.at[my_z, parts[p]],
            sz_send.at[p, r],
            sz_recv.at[p, my_z],
            head=there,
        )

    def sz_arrive(p, r):
        other = lax.rem(my_z + r, NZ)
        return remote(
            sums_row.at[parts[p]],
            sums_z.at[other, parts[p]],
            sz_send.at[p, r],
            sz_recv.at[p, other],
            head=other * NY + my_y,
        )

    def sy_copy(p, r):
        there = my_z * NY + lax.rem(my_y + r, NY)
        return remote(
            half_sums.at[parts[p]],
            sums_y.at[my_y, parts[p]],
            sy_send.at[p, r],
            sy_recv.at[p, my_y],
            head=there,
        )

    def sy_arrive(p, r):
        other = lax.rem(my_y + r, NY)
        return remote(
            half_sums.at[parts[p]],
            sums_y.at[other, parts[p]],
            sy_send.at[p, r],
            sy_recv.at[p, other],
            head=my_z * NY + other,
        )

    def sums_start(p):
        for r in order:
            sz_copy(p, r).start()
        sums_z[my_z, parts[p], :] = sums_row[parts[p], :]

    def sums_turn(p):
        for r in order:
            sz_arrive(p, r).wait_recv()
        added = sums_z[0, parts[p], :]
        for k in range(1, NZ):
            added = added + sums_z[k, parts[p], :]
        half_sums[parts[p], :] = added
        sums_y[my_y, parts[p], :] = added
        for r in (1, 3, 2):
            sy_copy(p, r).start()

    def sums_end(p):
        for r in (1, 3, 2):
            sy_arrive(p, r).wait_recv()
        added = sums_y[0, parts[p], :]
        for k in range(1, NY):
            added = added + sums_y[k, parts[p], :]
        total_ref[parts[p], :] = added

    def phase4(i):
        base = pl.multiple_of(i * GROUP, GROUP)
        whole = local_state[i] + carry_in[...] * prec[i][0:1]
        whole_high = whole.astype(BF16)
        whole_low = (whole - whole_high.astype(F32)).astype(BF16)
        c_i = cmat[i]
        carried = dot(
            jnp.concatenate([c_i, c_i], axis=1),
            jnp.concatenate([whole_high, whole_low], axis=0),
        )
        grown = dot(colq[i].astype(BF16), spread_e)
        y = ydiag[pl.ds(base, GROUP), :] + carried * grown
        half = zbuf[pl.ds(base, GROUP), :].astype(F32) * 0.5
        g = y * (half + half * jnp.tanh(half))
        xbuf[pl.ds(HALO + base, GROUP), :] = g.astype(BF16)
        g_copy(i).start()
        squares = (g * g).astype(BF16)
        sums = lax.dot_general(ones, squares, (((1,), (1,)), ((), ())), preferred_element_type=F32)
        sums_row[pl.ds(jnp.where(i < 12, i, i + 4), 1), :] = sums[0:1]

        @pl.when(i == 11)
        def _():
            sums_start(0)

        @pl.when(i == 17)
        def _():
            sums_turn(0)

    loop(BLOCKS, phase4)
    sums_start(1)
    sums_end(0)
    sums_turn(1)

    @pl.when(seq < NSEQ - 1)
    def _():
        halo_bc().wait_send()
        halo_x().wait_send()

    def finish(c):
        for r in order:
            z_send(c, r).wait_send()
        y_up(c, my_y).wait_send()
        y_down(c, my_y).wait_send()
        f_up(c, below).wait_send()
        f_down(c, above).wait_send()

    loop(SIDE, finish)
    for r in (1, 3, 2):
        side_send(r).wait_send()
    for hop in range(NZ // 2):
        ring_done(hop)
    others(NSEQ, seq, lambda j: st_copy(j, seq).wait_send())
    others(NSEQ, seq, lambda j: cb_copy(j, seq).wait_send())

    loop(BLOCKS, lambda i: g_copy(i).wait())
    for p in range(2):
        for r in order:
            sz_copy(p, r).wait_send()
    sums_end(1)
    for p in range(2):
        for r in (1, 3, 2):
            sy_copy(p, r).wait_send()


def scale(g_hbm, total_ref, gain_ref, out_hbm, g_in, g_out, in_sem, out_sem):
    rows = GROUP * SCALED

    def come(k):
        part = pl.ds(rows * k, rows)
        return pltpu.make_async_copy(g_hbm.at[part], g_in.at[part], in_sem.at[k])

    def go(k):
        part = pl.ds(rows * k, rows)
        return pltpu.make_async_copy(g_out.at[part], out_hbm.at[part], out_sem.at[k])

    for k in range(BLOCKS // SCALED):
        come(k).start()
    gain = gain_ref[...][None, :]
    factor = lax.rsqrt(total_ref[...] * (1.0 / (NHEAD * WIDTH)) + 1e-05).T
    for k in range(BLOCKS // SCALED):
        come(k).wait()
        for j in range(SCALED * k, SCALED * (k + 1)):
            place = j if j < 12 else j + 4
            part = slice(GROUP * j, GROUP * (j + 1))
            scaled = g_in[part, :].astype(F32) * factor[:, place : place + 1] * gain
            g_out[part, :] = scaled.astype(BF16)
        go(k).start()
    for k in range(BLOCKS // SCALED):
        go(k).wait()


def body(x_rows, z_rows, b_rows, c_rows, step_raw, conv_x, conv_b, conv_c, decay_rate, norm_gain):
    vmem = pl.BlockSpec(memory_space=pltpu.VMEM)
    hbm = pl.BlockSpec(memory_space=pl.ANY)
    smem = pl.BlockSpec(memory_space=pltpu.SMEM)
    dma = pltpu.SemaphoreType.DMA
    g, totals = pl.pallas_call(
        layer,
        out_shape=(
            jax.ShapeDtypeStruct((LENGTH, WIDTH), BF16),
            jax.ShapeDtypeStruct((24, GROUP), F32),
        ),
        in_specs=[hbm, hbm, vmem, vmem, vmem, vmem, vmem, vmem, smem],
        out_specs=(hbm, vmem),
        scratch_shapes=[
            pltpu.VMEM((HALO + LENGTH, WIDTH), BF16),
            pltpu.VMEM((LENGTH, WIDTH), BF16),
            pltpu.VMEM((LENGTH, WIDTH), BF16),
            pltpu.VMEM((LENGTH, WIDTH), BF16),
            pltpu.VMEM((BLOCKS, HEADS, HALF, HALF), BF16),
            pltpu.VMEM((BLOCKS, HEADS, HALF, GROUP), BF16),
            pltpu.VMEM((CHUNKS, NY, NZ, 16, HALF * PER), BF16),
            pltpu.VMEM((BLOCKS, GROUP, STATE), BF16),
            pltpu.VMEM((BLOCKS, GROUP, GROUP), BF16),
            pltpu.VMEM((LENGTH, WIDTH), F32),
            pltpu.VMEM((BLOCKS, STATE, WIDTH), F32),
            pltpu.VMEM((BLOCKS, GROUP, 24), F32),
            pltpu.VMEM((BLOCKS, 24, GROUP), F32),
            pltpu.VMEM((BLOCKS, 8, GROUP), F32),
            pltpu.VMEM((BLOCKS, 8, GROUP), F32),
            pltpu.VMEM((8, HALF + LENGTH), F32),
            pltpu.VMEM((BLOCKS + 1, 8, WIDTH), F32),
            pltpu.VMEM((STATE, WIDTH), F32),
            pltpu.VMEM((NSEQ, PART + 8, WIDTH), F32),
            pltpu.VMEM((NSEQ, PART + 8, WIDTH), F32),
            pltpu.VMEM((NSEQ, PART, WIDTH), F32),
            pltpu.VMEM((STATE, WIDTH), F32),
            pltpu.VMEM((24, GROUP), F32),
            pltpu.VMEM((NZ, 24, GROUP), F32),
            pltpu.VMEM((24, GROUP), F32),
            pltpu.VMEM((NY, 24, GROUP), F32),
            dma((CHUNKS,)),
            dma,
            dma((BLOCKS,)),
            dma((2,)),
            dma((2,)),
            dma((CHUNKS, NZ)),
            dma((CHUNKS, NZ)),
            dma((CHUNKS, 2)),
            dma((CHUNKS, 2)),
            dma((CHUNKS, 2)),
            dma((CHUNKS, 2)),
            dma((NSEQ,)),
            dma((NSEQ,)),
            dma((NSEQ,)),
            dma((NSEQ,)),
            dma((NY,)),
            dma((NY,)),
            dma((NZ // 2, 2)),
            dma((NZ // 2, 2)),
            dma((2, NZ)),
            dma((2, NZ)),
            dma((2, NY)),
            dma((2, NY)),
        ],
        compiler_params=pltpu.CompilerParams(
            collective_id=0, has_side_effects=True, vmem_limit_bytes=60 * 2**20
        ),
        name="layer",
    )(x_rows, z_rows, b_rows.T, c_rows.T, step_raw.T, conv_x, conv_b, conv_c, decay_rate)
    return pl.pallas_call(
        scale,
        out_shape=jax.ShapeDtypeStruct((LENGTH, WIDTH), BF16),
        in_specs=[hbm, vmem, vmem],
        out_specs=hbm,
        scratch_shapes=[
            pltpu.VMEM((LENGTH, WIDTH), BF16),
            pltpu.VMEM((LENGTH, WIDTH), BF16),
            dma((BLOCKS // SCALED,)),
            dma((BLOCKS // SCALED,)),
        ],
        compiler_params=pltpu.CompilerParams(vmem_limit_bytes=60 * 2**20),
        name="scale",
    )(g, totals, norm_gain)


def solution(mesh):
    placed = (
        P("seq", "head"),
        P("seq", "head"),
        P("seq", "head"),
        P("seq", "head"),
        P("seq", "head"),
        P(None, "head"),
        P(None, "head"),
        P(None, "head"),
        P("head"),
        P("head"),
    )
    return jax.shard_map(
        body, mesh=mesh, in_specs=placed, out_specs=P("seq", "head"), check_vma=False
    )
```

```python
import functools

import jax
import jax.numpy as jnp
from jax import lax
from jax.experimental import pallas as pl
from jax.experimental.pallas import tpu as pltpu
from jax.sharding import PartitionSpec as P

GROUP = 256
HALF = 128
HEADS = 6
WIDTH = 384
LENGTH = 5120
BLOCKS = 20
PAIRS = BLOCKS // 2
LOADS = 4
PER = BLOCKS // LOADS
SPANS = ((0, 512), (512, 384))
SIDE = (896, 384)
SCALED = 4
NSEQ = 8
NZ = 8
NY = 4
NHEAD = NZ * NY
STATE = 128
PART = STATE // NSEQ
HALO = 16
MASKED = -1e30
F32 = jnp.float32
BF16 = jnp.bfloat16


def remote(src, dst, send, recv, **where):
    return pltpu.make_async_remote_copy(
        src_ref=src,
        dst_ref=dst,
        send_sem=send,
        recv_sem=recv,
        device_id=where,
        device_id_type=pl.DeviceIdType.MESH,
    )


def loop(count, body):
    lax.fori_loop(0, count, lambda i, _: (body(i), 0)[1], 0)


def dot(a, b):
    return jnp.dot(a, b, preferred_element_type=F32)


def layer(
    x_hbm,
    z_hbm,
    b_ref,
    c_ref,
    raw_ref,
    taps_ref,
    taps_b_ref,
    taps_c_ref,
    rate_ref,
    g_hbm,
    total_ref,
    xbuf,
    zbuf,
    xs_even,
    xs_odd,
    near,
    far,
    gath,
    cmat,
    bmat,
    ydiag,
    local_state,
    colq,
    rowq,
    bq,
    stepq,
    bcx,
    prec,
    state,
    payload,
    got,
    back,
    carry_in,
    sums_row,
    sums_z,
    half_sums,
    sums_y,
    x_sem,
    z_sem,
    g_sem,
    halo_send,
    halo_recv,
    zs_send,
    zs_recv,
    ys_send,
    ys_recv,
    yf_send,
    yf_recv,
    st_send,
    st_recv,
    cb_send,
    cb_recv,
    side_out,
    side_in,
    ring_out,
    ring_in,
    sz_send,
    sz_recv,
    sy_send,
    sy_recv,
):
    seq = lax.axis_index("seq")
    head = lax.axis_index("head")
    my_z = head // NY
    my_y = head % NY
    rows = LENGTH // LOADS

    def x_copy(c):
        part = pl.multiple_of(c * rows, rows)
        return pltpu.make_async_copy(
            x_hbm.at[pl.ds(part, rows)], xbuf.at[pl.ds(HALO + part, rows)], x_sem.at[c]
        )

    z_copy = pltpu.make_async_copy(z_hbm, zbuf, z_sem)

    barrier = pltpu.get_barrier_semaphore()

    def greet(**where):
        pl.semaphore_signal(
            barrier, inc=1, device_id=where, device_id_type=pl.DeviceIdType.MESH
        )

    for r in range(1, NZ):
        greet(head=lax.rem(my_z + r, NZ) * NY + my_y)
    for r in range(1, NY):
        greet(head=my_z * NY + lax.rem(my_y + r, NY))
    for r in range(1, NSEQ):
        greet(seq=lax.rem(seq + r, NSEQ))
    for c in range(LOADS):
        x_copy(c).start()
    z_copy.start()

    bcx[0:4, HALF:] = b_ref[...].astype(F32)
    bcx[4:8, HALF:] = c_ref[...].astype(F32)
    raw = raw_ref[...]
    stepq[...] = jnp.ones_like(stepq)
    step_all = jnp.maximum(raw, 0.0) + jnp.log1p(jnp.exp(-jnp.abs(raw)))
    for i in range(BLOCKS):
        stepq[i, 0:HEADS, :] = step_all[:, GROUP * i : GROUP * (i + 1)]
    taps_bc = jnp.concatenate([taps_b_ref[...].astype(F32), taps_c_ref[...].astype(F32)], axis=1)
    taps_bc = taps_bc.T * 0.5
    head_row = lax.broadcasted_iota(jnp.int32, (8, GROUP), 0)
    rate = jnp.zeros((8, GROUP), F32)
    for h in range(HEADS):
        rate = jnp.where(head_row == h, rate_ref[h], rate)
    sums_row[...] = jnp.zeros_like(sums_row)

    def conv_bc(ext):
        acc = ext * taps_bc[:, 3:4]
        for back_by in (1, 2, 3):
            acc = acc + pltpu.roll(ext, back_by, axis=1) * taps_bc[:, 3 - back_by : 4 - back_by]
        return acc + acc * jnp.tanh(acc)

    def put_tile(kind, pair, quarters):
        tile = jnp.concatenate([q[4 * kind : 4 * kind + 4] for q in quarters], axis=0)
        gath[kind, my_y, my_z, :, HALF * pair : HALF * (pair + 1)] = tile.astype(BF16)

    acc = conv_bc(bcx[:, HALF:])
    quarters = [acc[:, HALF * k : HALF * (k + 1)] for k in range(4 * PAIRS)]
    for kind in range(2):
        for pair in range(1, PAIRS):
            put_tile(kind, pair, quarters[4 * pair : 4 * pair + 4])

    pl.semaphore_wait(barrier, NZ - 1 + NY - 1 + NSEQ - 1)

    def halo_bc():
        return remote(
            bcx.at[:, pl.ds(LENGTH, HALF)],
            bcx.at[:, pl.ds(0, HALF)],
            halo_send.at[0],
            halo_recv.at[0],
            seq=lax.rem(seq + 1, NSEQ),
        )

    def halo_x():
        return remote(
            x_hbm.at[pl.ds(LENGTH - HALO, HALO)],
            xbuf.at[pl.ds(0, HALO)],
            halo_send.at[1],
            halo_recv.at[1],
            seq=lax.rem(seq + 1, NSEQ),
        )

    @pl.when(seq < NSEQ - 1)
    def _():
        halo_bc().start()
        halo_x().start()

    def part(kind, y, z, span):
        return gath.at[kind, y, z, :, pl.ds(*span)]

    def z_send(kind, c, r):
        ref = part(kind, my_y, my_z, SPANS[c])
        there = lax.rem(my_z + r, NZ) * NY + my_y
        return remote(ref, ref, zs_send.at[kind, c, r], zs_recv.at[kind, c, my_z], head=there)

    def z_arrive(kind, c, r):
        other = lax.rem(my_z + r, NZ)
        ref = part(kind, my_y, other, SPANS[c])
        return remote(
            ref,
            ref,
            zs_send.at[kind, c, r],
            zs_recv.at[kind, c, other],
            head=other * NY + my_y,
        )

    order = (1, 7, 2, 6, 3, 5, 4)

    def side_send(kind, r):
        ref = part(kind, my_y, my_z, SIDE)
        there = my_z * NY + lax.rem(my_y + r, NY)
        return remote(ref, ref, side_out.at[kind, r], side_in.at[kind, my_y], head=there)

    def side_arrive(kind, r):
        other = lax.rem(my_y + r, NY)
        ref = part(kind, other, my_z, SIDE)
        return remote(
            ref, ref, side_out.at[kind, r], side_in.at[kind, other], head=my_z * NY + other
        )

    y_order = (1, 3, 2)

    def send_z(kind, c):
        for r in order:
            z_send(kind, c, r).start()

    for r in y_order:
        side_send(0, r).start()
    send_z(0, 1)

    step = stepq[...]
    decay = -(step * rate[None])
    decay = decay.reshape(BLOCKS * 8, GROUP)
    row = lax.broadcasted_iota(jnp.int32, (GROUP, GROUP), 0)
    col = lax.broadcasted_iota(jnp.int32, (GROUP, GROUP), 1)
    upper = jnp.where(row <= col, 1.0, 0.0).astype(BF16)
    high = decay.astype(BF16)
    rest = decay - high.astype(F32)
    mid = rest.astype(BF16)
    low = (rest - mid.astype(F32)).astype(BF16)
    cum = dot(high, upper) + (dot(mid, upper) + dot(low, upper))
    last = cum[:, GROUP - 1 : GROUP]
    step2 = step.reshape(BLOCKS * 8, GROUP)
    rowq[:, 0:8, :] = cum.reshape(BLOCKS, 8, GROUP)
    rowq[:, 8:16, :] = (jnp.exp(last - cum) * step2).reshape(BLOCKS, 8, GROUP)
    rowq[:, 16:24, :] = jnp.exp(cum).reshape(BLOCKS, 8, GROUP)
    bq[...] = (cum - jnp.log(step2)).reshape(BLOCKS, 8, GROUP)

    above = lax.rem(my_y + 1, NY)
    below = lax.rem(my_y + NY - 1, NY)
    across = lax.rem(my_y + 2, NY)
    ups = my_z * NY + above
    downs = my_z * NY + below

    def y_copy(kind, c, slot, up):
        ref = gath.at[kind, slot, :, :, pl.ds(*SPANS[c])]
        way = 0 if up else 1
        return remote(
            ref,
            ref,
            ys_send.at[kind, c, way],
            ys_recv.at[kind, c, way],
            head=ups if up else downs,
        )

    def f_copy(kind, c, slot, up):
        first = 0 if up else NZ // 2
        ref = gath.at[kind, slot, pl.ds(first, NZ // 2), :, pl.ds(*SPANS[c])]
        way = 0 if up else 1
        return remote(
            ref,
            ref,
            yf_send.at[kind, c, way],
            yf_recv.at[kind, c, way],
            head=ups if up else downs,
        )

    z_above = lax.rem(my_z + 1, NZ) * NY + my_y
    z_below = lax.rem(my_z + NZ - 1, NZ) * NY + my_y

    def ring(kind, hop, up, block):
        half = NY // 2
        if hop < NZ // 2 - 1:
            ref = gath.at[kind, :, block, :, pl.ds(*SIDE)]
        elif up:
            ref = gath.at[kind, pl.ds(0, half), block, :, pl.ds(*SIDE)]
        else:
            ref = gath.at[kind, pl.ds(half, half), block, :, pl.ds(*SIDE)]
        way = 0 if up else 1
        return remote(
            ref,
            ref,
            ring_out.at[kind, hop, way],
            ring_in.at[kind, hop, way],
            head=z_above if up else z_below,
        )

    def ring_send(kind, hop):
        ring(kind, hop, True, lax.rem(my_z + NZ - hop, NZ)).start()
        ring(kind, hop, False, lax.rem(my_z + hop, NZ)).start()

    def ring_arrive(kind, hop):
        ring(kind, hop, True, lax.rem(my_z + NZ - hop - 1, NZ)).wait_recv()
        ring(kind, hop, False, lax.rem(my_z + hop + 1, NZ)).wait_recv()

    def ring_done(kind, hop):
        ring(kind, hop, True, lax.rem(my_z + NZ - hop, NZ)).wait_send()
        ring(kind, hop, False, lax.rem(my_z + hop, NZ)).wait_send()

    def event_side(kind):
        for r in y_order:
            side_arrive(kind, r).wait_recv()
        ring_send(kind, 0)

    def event_ring(kind, hop):
        ring_arrive(kind, hop - 1)
        ring_send(kind, hop)

    def event_z(kind, c):
        for r in order:
            z_arrive(kind, c, r).wait_recv()
        y_copy(kind, c, my_y, True).start()
        y_copy(kind, c, my_y, False).start()

    def event_f(kind, c):
        y_copy(kind, c, below, True).wait_recv()
        f_copy(kind, c, below, True).start()
        y_copy(kind, c, above, False).wait_recv()
        f_copy(kind, c, above, False).start()

    def event_d(kind, c):
        f_copy(kind, c, across, True).wait_recv()
        f_copy(kind, c, across, False).wait_recv()

    def event_halo():
        @pl.when(seq > 0)
        def _():
            halo_bc().wait_recv()
            halo_x().wait_recv()

        @pl.when(seq == 0)
        def _():
            bcx[:, 0:HALF] = jnp.zeros((8, HALF), F32)
            xbuf[0:HALO, :] = jnp.zeros((HALO, WIDTH), BF16)

        first = conv_bc(bcx[:, 0 : 2 * HALF])[:, HALF:]
        for kind in range(2):
            put_tile(kind, 0, [first] + quarters[1:4])
        send_z(0, 0)
        for r in y_order:
            side_send(1, r).start()

    taps = taps_ref[...].astype(F32) * 0.5
    lanes = lax.broadcasted_iota(jnp.int32, (GROUP, WIDTH), 1)
    even = (lanes & 127) < 64
    row1 = lax.broadcasted_iota(jnp.int32, (HALF, HALF), 0)
    col1 = lax.broadcasted_iota(jnp.int32, (HALF, HALF), 1)
    causal = row1 >= col1

    def phase1(i):
        base = pl.multiple_of(i * GROUP, GROUP)
        wide = xbuf[pl.ds(base, GROUP + HALO), :].astype(F32)
        once = pltpu.roll(wide, 1, axis=0)
        older = pltpu.roll(wide * taps[1:2] + once * taps[0:1], 2, axis=0)
        half = wide[HALO:] * taps[3:4] + once[HALO:] * taps[2:3] + older[HALO:]
        xs = (half + half * jnp.tanh(half)).astype(BF16)
        none = jnp.zeros_like(xs)
        xs_even[pl.ds(base, GROUP), :] = jnp.where(even, xs, none)
        xs_odd[pl.ds(base, GROUP), :] = jnp.where(even, none, xs)
        cols = rowq[i].T
        colq[i] = cols
        b_all = bq[i]
        for h in range(HEADS):
            a = cols[:, h : h + 1]
            b = b_all[h : h + 1, :]
            near[i, h] = jnp.exp(jnp.where(causal, a[:HALF] - b[:, :HALF], MASKED)).astype(BF16)
            far[i, h, :, 0:HALF] = jnp.exp(a[HALF:] - b[:, :HALF]).astype(BF16)
            far[i, h, :, HALF:] = jnp.exp(
                jnp.where(causal, a[HALF:] - b[:, HALF:], MASKED)
            ).astype(BF16)

    def step1(i):
        block = lax.rem(i + 1, BLOCKS)

        @pl.when((i == 0) | ((lax.rem(block, PER) == 0) & (block > 0)))
        def _():
            x_copy(block // PER).wait()

        phase1(block)

        for when, events in during.items():

            @pl.when(i == when)
            def _(events=events):
                for event, *which in events:
                    event(*which)

    during = {
        4: [(event_halo,)],
        5: [(event_side, 0)],
        7: [(event_z, 0, 1), (send_z, 1, 1)],
        11: [(event_ring, 0, 1)],
        12: [(event_z, 0, 0)],
        14: [(event_f, 0, 1)],
        16: [(event_ring, 0, 2), (send_z, 1, 0)],
        17: [(event_side, 1)],
    }
    loop(BLOCKS, step1)

    spread_row = lax.broadcasted_iota(jnp.int32, (24, WIDTH), 0)
    spread_col = lax.broadcasted_iota(jnp.int32, (24, WIDTH), 1) >> 6
    spread_w = jnp.where(spread_row == spread_col + 8, 1.0, 0.0).astype(BF16)
    spread_e = jnp.where(spread_row == spread_col + 16, 1.0, 0.0).astype(BF16)
    of_head = lax.broadcasted_iota(jnp.int32, (8, WIDTH), 1) >> 6
    upper4 = lax.broadcasted_iota(jnp.int32, (8, HALF), 0) < 4

    state[...] = jnp.zeros_like(state)
    prec[0] = jnp.ones((8, WIDTH), F32)

    def assemble(kind, j):
        lane = pl.multiple_of(j * HALF, HALF)
        blocks = ([], [])
        for pair in range(NHEAD // 2):
            y, z = (2 * pair) // NZ, (2 * pair) % NZ
            first = gath[kind, y, z, :, pl.ds(lane, HALF)].astype(F32)
            second = gath[kind, y, z + 1, :, pl.ds(lane, HALF)].astype(F32)
            for e in range(2):
                one = first[8 * e : 8 * e + 8]
                two = second[8 * e : 8 * e + 8]
                left = jnp.where(upper4, one, pltpu.roll(two, 4, axis=0))
                right = jnp.where(upper4, pltpu.roll(one, 4, axis=0), two)
                blocks[e].append(jnp.concatenate([left, right], axis=1))
        return [jnp.concatenate(block, axis=0) for block in blocks]

    def phase2(j):
        for e, b_t in enumerate(assemble(0, j)):
            i = 2 * j + e
            b_t = b_t.astype(BF16)
            bmat[i] = b_t
            base = pl.multiple_of(i * GROUP, GROUP)
            xs = (xs_even[pl.ds(base, GROUP), :] + xs_odd[pl.ds(base, GROUP), :]).astype(F32)
            cols = colq[i]
            weight = dot(cols.astype(BF16), spread_w)
            new = dot(b_t, (weight * xs).astype(BF16))
            ends = cols[GROUP - 8 :, 16:24]
            gone = jnp.zeros((8, WIDTH), F32)
            for h in range(HEADS):
                gone = jnp.where(of_head == h, ends[7:8, h : h + 1], gone)
            old = state[...]
            local_state[i] = old
            state[...] = old * gone[0:1] + new
            prec[i + 1] = prec[i] * gone

    def phase3(j):
        for e, c_t in enumerate(assemble(1, j)):
            i = 2 * j + e
            c_i = c_t.T.astype(BF16)
            cmat[i] = c_i
            base = pl.multiple_of(i * GROUP, GROUP)
            scores = dot(c_i, bmat[i]).astype(BF16)
            top = scores[:HALF, :HALF]
            low_rows = scores[HALF:, :]
            for pair in range(HEADS // 2):
                span = slice(HALF * pair, HALF * (pair + 1))
                xe = xs_even[pl.ds(base, GROUP), span]
                xo = xs_odd[pl.ds(base, GROUP), span]
                m1 = jnp.concatenate(
                    [top * near[i, 2 * pair], top * near[i, 2 * pair + 1]], axis=1
                )
                x1 = jnp.concatenate([xe[:HALF], xo[:HALF]], axis=0)
                ydiag[pl.ds(base, HALF), span] = dot(m1, x1)
                m2 = jnp.concatenate(
                    [low_rows * far[i, 2 * pair], low_rows * far[i, 2 * pair + 1]], axis=1
                )
                x2 = jnp.concatenate([xe, xo], axis=0)
                ydiag[pl.ds(base + HALF, HALF), span] = dot(m2, x2)

    def gates(i):
        base = pl.multiple_of(i * GROUP, GROUP)
        half = zbuf[pl.ds(base, GROUP), :].astype(F32) * 0.5
        zbuf[pl.ds(base, GROUP), :] = (half + half * jnp.tanh(half)).astype(BF16)

    event_f(0, 0)
    event_z(1, 1)
    z_copy.wait()
    loop(BLOCKS // 2, gates)
    event_ring(0, 3)
    loop(BLOCKS // 2, lambda i: gates(BLOCKS // 2 + i))
    event_ring(1, 1)
    event_d(0, 0)
    loop(4, phase2)
    event_z(1, 0)
    event_d(0, 1)
    loop(3, lambda j: phase2(4 + j))
    event_f(1, 1)
    event_ring(1, 2)
    ring_arrive(0, 3)
    loop(3, lambda j: phase2(7 + j))

    for j in range(NSEQ):
        payload[j, 0:PART, :] = state[PART * j : PART * (j + 1), :]
        payload[j, PART : PART + 8, :] = prec[BLOCKS]

    def st_copy(j, slot):
        return remote(payload.at[j], got.at[slot], st_send.at[j], st_recv.at[slot], seq=j)

    def cb_copy(j, slot):
        place = pl.multiple_of(slot * PART, PART)
        return remote(
            back.at[j], carry_in.at[pl.ds(place, PART)], cb_send.at[j], cb_recv.at[slot], seq=j
        )

    def others(count, me, body):
        loop(count - 1, lambda r: body(lax.rem(me + 1 + r, count)))

    others(NSEQ, seq, lambda j: st_copy(j, seq).start())
    got[seq] = payload[seq]
    event_f(1, 0)
    event_ring(1, 3)
    event_d(1, 1)
    loop(3, lambda j: phase3(4 + j))
    others(NSEQ, seq, lambda j: st_copy(j, j).wait_recv())
    carry = jnp.zeros((PART, WIDTH), F32)
    for j in range(NSEQ):
        back[j] = carry
        carry = carry * got[j, PART : PART + 1, :] + got[j, 0:PART, :]
    others(NSEQ, seq, lambda j: cb_copy(j, seq).start())
    carry_in[pl.ds(pl.multiple_of(seq * PART, PART), PART), :] = back[seq]
    event_d(1, 0)
    loop(4, phase3)
    ring_arrive(1, 3)
    loop(3, lambda j: phase3(7 + j))
    others(NSEQ, seq, lambda j: cb_copy(j, j).wait_recv())

    ones = jnp.ones((8, WIDTH), BF16)

    def g_copy(i):
        base = pl.multiple_of(i * GROUP, GROUP)
        return pltpu.make_async_copy(
            xbuf.at[pl.ds(HALO + base, GROUP)], g_hbm.at[pl.ds(base, GROUP)], g_sem.at[i]
        )

    parts = (pl.ds(0, 16), pl.ds(16, 8))

    def sz_copy(p, r):
        there = lax.rem(my_z + r, NZ) * NY + my_y
        return remote(
            sums_row.at[parts[p]],
            sums_z.at[my_z, parts[p]],
            sz_send.at[p, r],
            sz_recv.at[p, my_z],
            head=there,
        )

    def sz_arrive(p, r):
        other = lax.rem(my_z + r, NZ)
        return remote(
            sums_row.at[parts[p]],
            sums_z.at[other, parts[p]],
            sz_send.at[p, r],
            sz_recv.at[p, other],
            head=other * NY + my_y,
        )

    def sy_copy(p, r):
        there = my_z * NY + lax.rem(my_y + r, NY)
        return remote(
            half_sums.at[parts[p]],
            sums_y.at[my_y, parts[p]],
            sy_send.at[p, r],
            sy_recv.at[p, my_y],
            head=there,
        )

    def sy_arrive(p, r):
        other = lax.rem(my_y + r, NY)
        return remote(
            half_sums.at[parts[p]],
            sums_y.at[other, parts[p]],
            sy_send.at[p, r],
            sy_recv.at[p, other],
            head=my_z * NY + other,
        )

    def sums_start(p):
        for r in order:
            sz_copy(p, r).start()
        sums_z[my_z, parts[p], :] = sums_row[parts[p], :]

    def sums_turn(p):
        for r in order:
            sz_arrive(p, r).wait_recv()
        added = sums_z[0, parts[p], :]
        for k in range(1, NZ):
            added = added + sums_z[k, parts[p], :]
        half_sums[parts[p], :] = added
        sums_y[my_y, parts[p], :] = added
        for r in (1, 3, 2):
            sy_copy(p, r).start()

    def sums_end(p):
        for r in (1, 3, 2):
            sy_arrive(p, r).wait_recv()
        added = sums_y[0, parts[p], :]
        for k in range(1, NY):
            added = added + sums_y[k, parts[p], :]
        total_ref[parts[p], :] = added

    def phase4(i):
        base = pl.multiple_of(i * GROUP, GROUP)
        whole = local_state[i] + carry_in[...] * prec[i][0:1]
        whole_high = whole.astype(BF16)
        whole_low = (whole - whole_high.astype(F32)).astype(BF16)
        c_i = cmat[i]
        carried = dot(
            jnp.concatenate([c_i, c_i], axis=1),
            jnp.concatenate([whole_high, whole_low], axis=0),
        )
        grown = dot(colq[i].astype(BF16), spread_e)
        y = ydiag[pl.ds(base, GROUP), :] + carried * grown
        g = y * zbuf[pl.ds(base, GROUP), :].astype(F32)
        xbuf[pl.ds(HALO + base, GROUP), :] = g.astype(BF16)
        g_copy(i).start()
        squares = (g * g).astype(BF16)
        sums = lax.dot_general(ones, squares, (((1,), (1,)), ((), ())), preferred_element_type=F32)
        sums_row[pl.ds(jnp.where(i < 12, i, i + 4), 1), :] = sums[0:1]

        @pl.when(i == 11)
        def _():
            sums_start(0)

    loop(BLOCKS, phase4)
    sums_start(1)
    sums_turn(0)
    sums_turn(1)
    sums_end(0)

    @pl.when(seq < NSEQ - 1)
    def _():
        halo_bc().wait_send()
        halo_x().wait_send()

    for kind in range(2):
        for c in range(len(SPANS)):
            for r in order:
                z_send(kind, c, r).wait_send()
            y_copy(kind, c, my_y, True).wait_send()
            y_copy(kind, c, my_y, False).wait_send()
            f_copy(kind, c, below, True).wait_send()
            f_copy(kind, c, above, False).wait_send()
        for r in y_order:
            side_send(kind, r).wait_send()
        for hop in range(NZ // 2):
            ring_done(kind, hop)
    others(NSEQ, seq, lambda j: st_copy(j, seq).wait_send())
    others(NSEQ, seq, lambda j: cb_copy(j, seq).wait_send())

    loop(BLOCKS, lambda i: g_copy(i).wait())
    for p in range(2):
        for r in order:
            sz_copy(p, r).wait_send()
    sums_end(1)
    for p in range(2):
        for r in (1, 3, 2):
            sy_copy(p, r).wait_send()


def scale(g_hbm, total_ref, gain_ref, out_hbm, g_in, g_out, in_sem, out_sem):
    rows = GROUP * SCALED

    def come(k):
        part = pl.ds(rows * k, rows)
        return pltpu.make_async_copy(g_hbm.at[part], g_in.at[part], in_sem.at[k])

    def go(k):
        part = pl.ds(rows * k, rows)
        return pltpu.make_async_copy(g_out.at[part], out_hbm.at[part], out_sem.at[k])

    for k in range(BLOCKS // SCALED):
        come(k).start()
    gain = gain_ref[...][None, :]
    factor = lax.rsqrt(total_ref[...] * (1.0 / (NHEAD * WIDTH)) + 1e-05).T
    for k in range(BLOCKS // SCALED):
        come(k).wait()
        for j in range(SCALED * k, SCALED * (k + 1)):
            place = j if j < 12 else j + 4
            part = slice(GROUP * j, GROUP * (j + 1))
            scaled = g_in[part, :].astype(F32) * factor[:, place : place + 1] * gain
            g_out[part, :] = scaled.astype(BF16)
        go(k).start()
    for k in range(BLOCKS // SCALED):
        go(k).wait()


def body(x_rows, z_rows, b_rows, c_rows, step_raw, conv_x, conv_b, conv_c, decay_rate, norm_gain):
    vmem = pl.BlockSpec(memory_space=pltpu.VMEM)
    hbm = pl.BlockSpec(memory_space=pl.ANY)
    smem = pl.BlockSpec(memory_space=pltpu.SMEM)
    dma = pltpu.SemaphoreType.DMA
    g, totals = pl.pallas_call(
        layer,
        out_shape=(
            jax.ShapeDtypeStruct((LENGTH, WIDTH), BF16),
            jax.ShapeDtypeStruct((24, GROUP), F32),
        ),
        in_specs=[hbm, hbm, vmem, vmem, vmem, vmem, vmem, vmem, smem],
        out_specs=(hbm, vmem),
        scratch_shapes=[
            pltpu.VMEM((HALO + LENGTH, WIDTH), BF16),
            pltpu.VMEM((LENGTH, WIDTH), BF16),
            pltpu.VMEM((LENGTH, WIDTH), BF16),
            pltpu.VMEM((LENGTH, WIDTH), BF16),
            pltpu.VMEM((BLOCKS, HEADS, HALF, HALF), BF16),
            pltpu.VMEM((BLOCKS, HEADS, HALF, GROUP), BF16),
            pltpu.VMEM((2, NY, NZ, 16, HALF * PAIRS), BF16),
            pltpu.VMEM((BLOCKS, GROUP, STATE), BF16),
            pltpu.VMEM((BLOCKS, STATE, GROUP), BF16),
            pltpu.VMEM((LENGTH, WIDTH), F32),
            pltpu.VMEM((BLOCKS, STATE, WIDTH), F32),
            pltpu.VMEM((BLOCKS, GROUP, 24), F32),
            pltpu.VMEM((BLOCKS, 24, GROUP), F32),
            pltpu.VMEM((BLOCKS, 8, GROUP), F32),
            pltpu.VMEM((BLOCKS, 8, GROUP), F32),
            pltpu.VMEM((8, HALF + LENGTH), F32),
            pltpu.VMEM((BLOCKS + 1, 8, WIDTH), F32),
            pltpu.VMEM((STATE, WIDTH), F32),
            pltpu.VMEM((NSEQ, PART + 8, WIDTH), F32),
            pltpu.VMEM((NSEQ, PART + 8, WIDTH), F32),
            pltpu.VMEM((NSEQ, PART, WIDTH), F32),
            pltpu.VMEM((STATE, WIDTH), F32),
            pltpu.VMEM((24, GROUP), F32),
            pltpu.VMEM((NZ, 24, GROUP), F32),
            pltpu.VMEM((24, GROUP), F32),
            pltpu.VMEM((NY, 24, GROUP), F32),
            dma((LOADS,)),
            dma,
            dma((BLOCKS,)),
            dma((2,)),
            dma((2,)),
            dma((2, len(SPANS), NZ)),
            dma((2, len(SPANS), NZ)),
            dma((2, len(SPANS), 2)),
            dma((2, len(SPANS), 2)),
            dma((2, len(SPANS), 2)),
            dma((2, len(SPANS), 2)),
            dma((NSEQ,)),
            dma((NSEQ,)),
            dma((NSEQ,)),
            dma((NSEQ,)),
            dma((2, NY)),
            dma((2, NY)),
            dma((2, NZ // 2, 2)),
            dma((2, NZ // 2, 2)),
            dma((2, NZ)),
            dma((2, NZ)),
            dma((2, NY)),
            dma((2, NY)),
        ],
        compiler_params=pltpu.CompilerParams(
            collective_id=0, has_side_effects=True, vmem_limit_bytes=60 * 2**20
        ),
        name="layer",
    )(x_rows, z_rows, b_rows.T, c_rows.T, step_raw.T, conv_x, conv_b, conv_c, decay_rate)
    return pl.pallas_call(
        scale,
        out_shape=jax.ShapeDtypeStruct((LENGTH, WIDTH), BF16),
        in_specs=[hbm, vmem, vmem],
        out_specs=hbm,
        scratch_shapes=[
            pltpu.VMEM((LENGTH, WIDTH), BF16),
            pltpu.VMEM((LENGTH, WIDTH), BF16),
            dma((BLOCKS // SCALED,)),
            dma((BLOCKS // SCALED,)),
        ],
        compiler_params=pltpu.CompilerParams(vmem_limit_bytes=60 * 2**20),
        name="scale",
    )(g, totals, norm_gain)


def solution(mesh):
    placed = (
        P("seq", "head"),
        P("seq", "head"),
        P("seq", "head"),
        P("seq", "head"),
        P("seq", "head"),
        P(None, "head"),
        P(None, "head"),
        P(None, "head"),
        P("head"),
        P("head"),
    )
    return jax.shard_map(
        body, mesh=mesh, in_specs=placed, out_specs=P("seq", "head"), check_vma=False
    )
```

```python
import functools

import jax
import jax.numpy as jnp
from jax import lax
from jax.experimental import pallas as pl
from jax.experimental.pallas import tpu as pltpu
from jax.sharding import PartitionSpec as P

GROUP = 256
HALF = 128
HEADS = 6
WIDTH = 384
LENGTH = 5120
BLOCKS = 20
PAIRS = BLOCKS // 2
LOADS = 4
PER = BLOCKS // LOADS
FIRST = (0, 128)
SPANS = (((128, 384), (512, 384)), ((128, 384), (512, 384)))
SIDE = ((896, 384), (896, 384))
SCALED = 2
NSEQ = 8
NZ = 8
NY = 4
NHEAD = NZ * NY
STATE = 128
PART = STATE // NSEQ
HALO = 16
MASKED = -1e30
F32 = jnp.float32
BF16 = jnp.bfloat16


def remote(src, dst, send, recv, **where):
    return pltpu.make_async_remote_copy(
        src_ref=src,
        dst_ref=dst,
        send_sem=send,
        recv_sem=recv,
        device_id=where,
        device_id_type=pl.DeviceIdType.MESH,
    )


def loop(count, body):
    lax.fori_loop(0, count, lambda i, _: (body(i), 0)[1], 0)


def dot(a, b):
    return jnp.dot(a, b, preferred_element_type=F32)


def layer(
    x_hbm,
    z_hbm,
    b_ref,
    c_ref,
    raw_ref,
    taps_ref,
    taps_b_ref,
    taps_c_ref,
    rate_ref,
    g_hbm,
    total_ref,
    xbuf,
    zbuf,
    egate,
    xs_even,
    xs_odd,
    near,
    far,
    gath,
    cmat,
    bmat,
    ydiag,
    local_state,
    colq,
    rowq,
    bq,
    stepq,
    bcx,
    prec,
    state,
    gones,
    got_decay,
    got,
    back,
    carry_in,
    sums_row,
    sums_z,
    half_sums,
    sums_y,
    x_sem,
    z_sem,
    g_sem,
    halo_send,
    halo_recv,
    zs_send,
    zs_recv,
    ys_send,
    ys_recv,
    yf_send,
    yf_recv,
    st_send,
    st_recv,
    cb_send,
    cb_recv,
    tz_send,
    tz_recv,
    ty_send,
    ty_recv,
    sd_send,
    sd_recv,
    side_out,
    side_in,
    ring_out,
    ring_in,
    sz_send,
    sz_recv,
    sy_send,
    sy_recv,
):
    seq = lax.axis_index("seq")
    head = lax.axis_index("head")
    my_z = head // NY
    my_y = head % NY
    rows = LENGTH // LOADS

    def x_copy(c):
        part = pl.multiple_of(c * rows, rows)
        return pltpu.make_async_copy(
            x_hbm.at[pl.ds(part, rows)], xbuf.at[pl.ds(HALO + part, rows)], x_sem.at[c]
        )

    z_copy = pltpu.make_async_copy(z_hbm, zbuf, z_sem)

    barrier = pltpu.get_barrier_semaphore()

    def greet(**where):
        pl.semaphore_signal(
            barrier, inc=1, device_id=where, device_id_type=pl.DeviceIdType.MESH
        )

    for r in range(1, NZ):
        greet(head=lax.rem(my_z + r, NZ) * NY + my_y)
    for r in range(1, NY):
        greet(head=my_z * NY + lax.rem(my_y + r, NY))
    for r in range(1, NSEQ):
        greet(seq=lax.rem(seq + r, NSEQ))
    for c in range(LOADS):
        x_copy(c).start()
    z_copy.start()

    bcx[0:4, HALF:] = b_ref[...].astype(F32)
    bcx[4:8, HALF:] = c_ref[...].astype(F32)
    taps_bc = jnp.concatenate([taps_b_ref[...].astype(F32), taps_c_ref[...].astype(F32)], axis=1)
    taps_bc = taps_bc.T * 0.5
    head_row = lax.broadcasted_iota(jnp.int32, (8, GROUP), 0)
    rate = jnp.zeros((8, GROUP), F32)
    for h in range(HEADS):
        rate = jnp.where(head_row == h, rate_ref[h], rate)
    sums_row[...] = jnp.zeros_like(sums_row)

    def conv_bc(ext):
        acc = ext * taps_bc[:, 3:4]
        for back_by in (1, 2, 3):
            acc = acc + pltpu.roll(ext, back_by, axis=1) * taps_bc[:, 3 - back_by : 4 - back_by]
        return acc + acc * jnp.tanh(acc)

    def put_tile(kind, pair, quarters):
        tile = jnp.concatenate([q[4 * kind : 4 * kind + 4] for q in quarters], axis=0)
        gath[kind, my_y, my_z, :, HALF * pair : HALF * (pair + 1)] = tile.astype(BF16)

    acc = conv_bc(bcx[:, HALF:])
    quarters = [acc[:, HALF * k : HALF * (k + 1)] for k in range(4 * PAIRS)]
    for kind in range(2):
        for pair in range(1, PAIRS):
            put_tile(kind, pair, quarters[4 * pair : 4 * pair + 4])

    pl.semaphore_wait(barrier, NZ - 1 + NY - 1 + NSEQ - 1)

    def halo_bc():
        return remote(
            bcx.at[:, pl.ds(LENGTH, HALF)],
            bcx.at[:, pl.ds(0, HALF)],
            halo_send.at[0],
            halo_recv.at[0],
            seq=lax.rem(seq + 1, NSEQ),
        )

    def halo_x():
        return remote(
            x_hbm.at[pl.ds(LENGTH - HALO, HALO)],
            xbuf.at[pl.ds(0, HALO)],
            halo_send.at[1],
            halo_recv.at[1],
            seq=lax.rem(seq + 1, NSEQ),
        )

    @pl.when(seq < NSEQ - 1)
    def _():
        halo_bc().start()
        halo_x().start()

    def part(kind, y, z, span):
        return gath.at[kind, y, z, :, pl.ds(*span)]

    def z_send(kind, c, r):
        ref = part(kind, my_y, my_z, SPANS[kind][c])
        there = lax.rem(my_z + r, NZ) * NY + my_y
        return remote(ref, ref, zs_send.at[kind, c, r], zs_recv.at[kind, c, my_z], head=there)

    def z_arrive(kind, c, r):
        other = lax.rem(my_z + r, NZ)
        ref = part(kind, my_y, other, SPANS[kind][c])
        return remote(
            ref,
            ref,
            zs_send.at[kind, c, r],
            zs_recv.at[kind, c, other],
            head=other * NY + my_y,
        )

    order = (1, 7, 2, 6, 3, 5, 4)

    def side_send(kind, r):
        ref = part(kind, my_y, my_z, SIDE[kind])
        there = my_z * NY + lax.rem(my_y + r, NY)
        return remote(ref, ref, side_out.at[kind, r], side_in.at[kind, my_y], head=there)

    def side_arrive(kind, r):
        other = lax.rem(my_y + r, NY)
        ref = part(kind, other, my_z, SIDE[kind])
        return remote(
            ref, ref, side_out.at[kind, r], side_in.at[kind, other], head=my_z * NY + other
        )

    y_order = (1, 3, 2)

    def send_z(kind, c):
        for r in order:
            z_send(kind, c, r).start()

    send_z(0, 0)
    for r in y_order:
        side_send(0, r).start()
    send_z(0, 1)
    for r in y_order:
        side_send(1, r).start()

    raw = raw_ref[...]
    stepq[...] = jnp.ones_like(stepq)
    step_all = jnp.maximum(raw, 0.0) + jnp.log1p(jnp.exp(-jnp.abs(raw)))
    for i in range(BLOCKS):
        stepq[i, 0:HEADS, :] = step_all[:, GROUP * i : GROUP * (i + 1)]
    step = stepq[...]
    decay = -(step * rate[None])
    decay = decay.reshape(BLOCKS * 8, GROUP)
    row = lax.broadcasted_iota(jnp.int32, (GROUP, GROUP), 0)
    col = lax.broadcasted_iota(jnp.int32, (GROUP, GROUP), 1)
    upper = jnp.where(row <= col, 1.0, 0.0).astype(BF16)
    high = decay.astype(BF16)
    rest = decay - high.astype(F32)
    mid = rest.astype(BF16)
    low = (rest - mid.astype(F32)).astype(BF16)
    cum = dot(high, upper) + (dot(mid, upper) + dot(low, upper))
    last = cum[:, GROUP - 1 : GROUP]
    step2 = step.reshape(BLOCKS * 8, GROUP)
    rowq[:, 0:8, :] = cum.reshape(BLOCKS, 8, GROUP)
    rowq[:, 8:16, :] = (jnp.exp(last - cum) * step2).reshape(BLOCKS, 8, GROUP)
    rowq[:, 16:24, :] = jnp.exp(cum).reshape(BLOCKS, 8, GROUP)
    bq[...] = (cum - jnp.log(step2)).reshape(BLOCKS, 8, GROUP)

    above = lax.rem(my_y + 1, NY)
    below = lax.rem(my_y + NY - 1, NY)
    across = lax.rem(my_y + 2, NY)
    ups = my_z * NY + above
    downs = my_z * NY + below

    def y_copy(kind, c, slot, up):
        ref = gath.at[kind, slot, :, :, pl.ds(*SPANS[kind][c])]
        way = 0 if up else 1
        return remote(
            ref,
            ref,
            ys_send.at[kind, c, way],
            ys_recv.at[kind, c, way],
            head=ups if up else downs,
        )

    def f_copy(kind, c, slot, up):
        first = 0 if up else NZ // 2
        ref = gath.at[kind, slot, pl.ds(first, NZ // 2), :, pl.ds(*SPANS[kind][c])]
        way = 0 if up else 1
        return remote(
            ref,
            ref,
            yf_send.at[kind, c, way],
            yf_recv.at[kind, c, way],
            head=ups if up else downs,
        )

    z_above = lax.rem(my_z + 1, NZ) * NY + my_y
    z_below = lax.rem(my_z + NZ - 1, NZ) * NY + my_y

    def ring(kind, hop, up, block):
        half = NY // 2
        if hop < NZ // 2 - 1:
            ref = gath.at[kind, :, block, :, pl.ds(*SIDE[kind])]
        elif up:
            ref = gath.at[kind, pl.ds(0, half), block, :, pl.ds(*SIDE[kind])]
        else:
            ref = gath.at[kind, pl.ds(half, half), block, :, pl.ds(*SIDE[kind])]
        way = 0 if up else 1
        return remote(
            ref,
            ref,
            ring_out.at[kind, hop, way],
            ring_in.at[kind, hop, way],
            head=z_above if up else z_below,
        )

    def ring_send(kind, hop):
        ring(kind, hop, True, lax.rem(my_z + NZ - hop, NZ)).start()
        ring(kind, hop, False, lax.rem(my_z + hop, NZ)).start()

    def ring_arrive(kind, hop):
        ring(kind, hop, True, lax.rem(my_z + NZ - hop - 1, NZ)).wait_recv()
        ring(kind, hop, False, lax.rem(my_z + hop + 1, NZ)).wait_recv()

    def ring_done(kind, hop):
        ring(kind, hop, True, lax.rem(my_z + NZ - hop, NZ)).wait_send()
        ring(kind, hop, False, lax.rem(my_z + hop, NZ)).wait_send()

    def event_side(kind):
        for r in y_order:
            side_arrive(kind, r).wait_recv()
        ring_send(kind, 0)

    def event_ring(kind, hop):
        ring_arrive(kind, hop - 1)
        ring_send(kind, hop)

    def event_z(kind, c):
        for r in order:
            z_arrive(kind, c, r).wait_recv()
        y_copy(kind, c, my_y, True).start()
        y_copy(kind, c, my_y, False).start()

    def event_f(kind, c):
        y_copy(kind, c, below, True).wait_recv()
        f_copy(kind, c, below, True).start()
        y_copy(kind, c, above, False).wait_recv()
        f_copy(kind, c, above, False).start()

    def event_d(kind, c):
        f_copy(kind, c, across, True).wait_recv()
        f_copy(kind, c, across, False).wait_recv()

    def first_part(y, z):
        return gath.at[:, y, z, :, pl.ds(*FIRST)]

    def first_z(r):
        ref = first_part(my_y, my_z)
        there = lax.rem(my_z + r, NZ) * NY + my_y
        return remote(ref, ref, tz_send.at[r], tz_recv.at[my_z], head=there)

    def first_z_arrive(r):
        other = lax.rem(my_z + r, NZ)
        ref = first_part(my_y, other)
        return remote(ref, ref, tz_send.at[r], tz_recv.at[other], head=other * NY + my_y)

    def first_y(r):
        ref = gath.at[:, my_y, :, :, pl.ds(*FIRST)]
        there = my_z * NY + lax.rem(my_y + r, NY)
        return remote(ref, ref, ty_send.at[r], ty_recv.at[my_y], head=there)

    def first_y_arrive(r):
        other = lax.rem(my_y + r, NY)
        ref = gath.at[:, other, :, :, pl.ds(*FIRST)]
        return remote(ref, ref, ty_send.at[r], ty_recv.at[other], head=my_z * NY + other)

    def event_first():
        for r in order:
            first_z_arrive(r).wait_recv()
        for r in y_order:
            first_y(r).start()

    def event_first_done():
        for r in y_order:
            first_y_arrive(r).wait_recv()

    def event_halo():
        @pl.when(seq > 0)
        def _():
            halo_bc().wait_recv()
            halo_x().wait_recv()

        @pl.when(seq == 0)
        def _():
            bcx[:, 0:HALF] = jnp.zeros((8, HALF), F32)
            xbuf[0:HALO, :] = jnp.zeros((HALO, WIDTH), BF16)

        first = conv_bc(bcx[:, 0 : 2 * HALF])[:, HALF:]
        for kind in range(2):
            put_tile(kind, 0, [first] + quarters[1:4])
        for r in order:
            first_z(r).start()

    taps = taps_ref[...].astype(F32) * 0.5
    even = lax.broadcasted_iota(jnp.int32, (HALF, HALF), 1) < 64
    row1 = lax.broadcasted_iota(jnp.int32, (HALF, HALF), 0)
    col1 = lax.broadcasted_iota(jnp.int32, (HALF, HALF), 1)
    causal = row1 >= col1
    of_head = lax.broadcasted_iota(jnp.int32, (8, WIDTH), 1) >> 6

    def phase1(i):
        base = pl.multiple_of(i * GROUP, GROUP)
        for low in (0, HALF):
            for lane in range(0, WIDTH, HALF):
                span = slice(lane, lane + HALF)
                wide = xbuf[pl.ds(base + low, HALF + HALO), span].astype(F32)
                once = pltpu.roll(wide, 1, axis=0)
                older = pltpu.roll(wide * taps[1:2, span] + once * taps[0:1, span], 2, axis=0)
                half = (
                    wide[HALO:] * taps[3:4, span] + once[HALO:] * taps[2:3, span] + older[HALO:]
                )
                xs = (half + half * jnp.tanh(half)).astype(BF16)
                none = jnp.zeros_like(xs)
                xs_even[pl.ds(base + low, HALF), span] = jnp.where(even, xs, none)
                xs_odd[pl.ds(base + low, HALF), span] = jnp.where(even, none, xs)
        cols = rowq[i].T
        colq[i] = cols
        ends = cols[GROUP - 8 :, 16:24]
        gone = jnp.zeros((8, WIDTH), F32)
        for h in range(HEADS):
            gone = jnp.where(of_head == h, ends[7:8, h : h + 1], gone)
        gones[i] = gone
        b_all = bq[i]
        for h in range(HEADS):
            a = cols[:, h : h + 1]
            b = b_all[h : h + 1, :]
            gap1 = jnp.where(causal, a[:HALF] - b[:, :HALF], MASKED)
            gap2 = a[HALF:] - b[:, :HALF]
            gap3 = jnp.where(causal, a[HALF:] - b[:, HALF:], MASKED)
            near[i, h] = jnp.exp(gap1.astype(BF16))
            far[i, h, :, 0:HALF] = jnp.exp(gap2.astype(BF16))
            far[i, h, :, HALF:] = jnp.exp(gap3.astype(BF16))

    def step1(i):
        block = lax.rem(i + 1, BLOCKS)

        @pl.when((i == 0) | ((lax.rem(block, PER) == 0) & (block > 0)))
        def _():
            x_copy(block // PER).wait()

        phase1(block)

    def run(count, unit, before):
        def step(i):
            for when, events in before.items():

                @pl.when(i == when)
                def _(events=events):
                    for event, *which in events:
                        event(*which)

            unit(i)

        loop(count, step)

    run(
        BLOCKS,
        step1,
        {
            5: [(event_side, 0), (event_side, 1), (event_halo,), (send_z, 1, 0)],
            9: [(event_z, 0, 0)],
            12: [(event_ring, 0, 1), (event_z, 0, 1), (send_z, 1, 1)],
            14: [(event_ring, 1, 1), (event_first,)],
            15: [(event_f, 0, 0)],
            18: [(event_f, 0, 1), (event_ring, 0, 2)],
        },
    )

    spread_row = lax.broadcasted_iota(jnp.int32, (24, WIDTH), 0)
    spread_col = lax.broadcasted_iota(jnp.int32, (24, WIDTH), 1) >> 6
    spread_w = jnp.where(spread_row == spread_col + 8, 1.0, 0.0).astype(BF16)
    spread_e = jnp.where(spread_row == spread_col + 16, 1.0, 0.0).astype(BF16)
    upper4 = lax.broadcasted_iota(jnp.int32, (8, HALF), 0) < 4

    state[...] = jnp.zeros_like(state)

    so_far = jnp.ones((8, WIDTH), F32)
    prec[0] = so_far
    for i in range(BLOCKS):
        so_far = so_far * gones[i]
        prec[i + 1] = so_far
    got_decay[seq] = so_far

    def others(count, me, body):
        loop(count - 1, lambda r: body(lax.rem(me + 1 + r, count)))

    def sd_copy(j, slot):
        return remote(
            prec.at[BLOCKS], got_decay.at[slot], sd_send.at[j], sd_recv.at[slot], seq=j
        )

    others(NSEQ, seq, lambda j: sd_copy(j, seq).start())

    def assemble(kind, j):
        lane = pl.multiple_of(j * HALF, HALF)
        blocks = ([], [])
        for pair in range(NHEAD // 2):
            y, z = (2 * pair) // NZ, (2 * pair) % NZ
            first = gath[kind, y, z, :, pl.ds(lane, HALF)].astype(F32)
            second = gath[kind, y, z + 1, :, pl.ds(lane, HALF)].astype(F32)
            for e in range(2):
                one = first[8 * e : 8 * e + 8]
                two = second[8 * e : 8 * e + 8]
                left = jnp.where(upper4, one, pltpu.roll(two, 4, axis=0))
                right = jnp.where(upper4, pltpu.roll(one, 4, axis=0), two)
                blocks[e].append(jnp.concatenate([left, right], axis=1))
        return [jnp.concatenate(block, axis=0) for block in blocks]

    def phase2(j):
        news, goes = [], []
        for e, b_t in enumerate(assemble(0, j)):
            i = 2 * j + e
            b_t = b_t.astype(BF16)
            bmat[i] = b_t
            base = pl.multiple_of(i * GROUP, GROUP)
            xs = (xs_even[pl.ds(base, GROUP), :] + xs_odd[pl.ds(base, GROUP), :]).astype(F32)
            cols = colq[i]
            weight = dot(cols.astype(BF16), spread_w)
            news.append(dot(b_t, (weight * xs).astype(BF16)))
            goes.append(gones[i])
        old = state[...]
        local_state[2 * j] = old
        old = old * goes[0][0:1] + news[0]
        local_state[2 * j + 1] = old
        state[...] = old * goes[1][0:1] + news[1]

    def phase3(j):
        for e, c_t in enumerate(assemble(1, j)):
            i = 2 * j + e
            c_i = c_t.T.astype(BF16)
            cmat[i] = c_i
            base = pl.multiple_of(i * GROUP, GROUP)
            scores = dot(c_i, bmat[i]).astype(BF16)
            top = scores[:HALF, :HALF]
            low_rows = scores[HALF:, :]
            for pair in range(HEADS // 2):
                span = slice(HALF * pair, HALF * (pair + 1))
                xe = xs_even[pl.ds(base, GROUP), span]
                xo = xs_odd[pl.ds(base, GROUP), span]
                m1 = jnp.concatenate(
                    [top * near[i, 2 * pair], top * near[i, 2 * pair + 1]], axis=1
                )
                x1 = jnp.concatenate([xe[:HALF], xo[:HALF]], axis=0)
                gate1 = zbuf[pl.ds(base, HALF), span].astype(F32)
                ydiag[pl.ds(base, HALF), span] = dot(m1, x1) * gate1
                m2 = jnp.concatenate(
                    [low_rows * far[i, 2 * pair], low_rows * far[i, 2 * pair + 1]], axis=1
                )
                x2 = jnp.concatenate([xe, xo], axis=0)
                gate2 = zbuf[pl.ds(base + HALF, HALF), span].astype(F32)
                ydiag[pl.ds(base + HALF, HALF), span] = dot(m2, x2) * gate2

    def gates(i):
        base = pl.multiple_of(i * GROUP, GROUP)
        half = zbuf[pl.ds(base, GROUP), :].astype(F32) * 0.5
        gate = half + half * jnp.tanh(half)
        zbuf[pl.ds(base, GROUP), :] = gate.astype(BF16)
        grown = dot(colq[i].astype(BF16), spread_e)
        egate[pl.ds(base, GROUP), :] = (gate * grown).astype(BF16)

    z_copy.wait()
    run(BLOCKS // 2, gates, {0: [(event_z, 1, 0)]})
    run(
        PAIRS,
        phase2,
        {
            0: [(event_ring, 1, 2), (event_first_done,)],
            1: [(event_d, 0, 0)],
            2: [(event_ring, 0, 3), (event_z, 1, 1)],
            4: [(event_d, 0, 1)],
            6: [(event_ring, 1, 3)],
            7: [(ring_arrive, 0, 3)],
            8: [(event_f, 1, 0)],
        },
    )

    def st_copy(j, slot):
        place = pl.multiple_of(j * PART, PART)
        return remote(
            state.at[pl.ds(place, PART)], got.at[slot], st_send.at[j], st_recv.at[slot], seq=j
        )

    def cb_copy(j, slot):
        place = pl.multiple_of(slot * PART, PART)
        return remote(
            back.at[j], carry_in.at[pl.ds(place, PART)], cb_send.at[j], cb_recv.at[slot], seq=j
        )

    others(NSEQ, seq, lambda j: st_copy(j, seq).start())
    got[seq] = state[pl.ds(pl.multiple_of(seq * PART, PART), PART), :]
    run(BLOCKS // 2, lambda i: gates(BLOCKS // 2 + i), {6: [(event_f, 1, 1)]})

    def event_states():
        others(NSEQ, seq, lambda j: sd_copy(j, j).wait_recv())
        others(NSEQ, seq, lambda j: st_copy(j, j).wait_recv())
        carry = jnp.zeros((PART, WIDTH), F32)
        for j in range(NSEQ):
            back[j] = carry
            carry = carry * got_decay[j, 0:1, :] + got[j]
        others(NSEQ, seq, lambda j: cb_copy(j, seq).start())
        carry_in[pl.ds(pl.multiple_of(seq * PART, PART), PART), :] = back[seq]

    run(
        PAIRS,
        lambda i: phase3(lax.rem(i + 7, PAIRS)),
        {
            0: [(ring_arrive, 1, 3)],
            4: [(event_d, 1, 0), (event_states,)],
            7: [(event_d, 1, 1)],
        },
    )
    others(NSEQ, seq, lambda j: cb_copy(j, j).wait_recv())

    ones = jnp.ones((8, WIDTH), BF16)

    def g_copy(i):
        base = pl.multiple_of(i * GROUP, GROUP)
        return pltpu.make_async_copy(
            xbuf.at[pl.ds(HALO + base, GROUP)], g_hbm.at[pl.ds(base, GROUP)], g_sem.at[i]
        )

    parts = (pl.ds(0, 16), pl.ds(16, 8))

    def sz_copy(p, r):
        there = lax.rem(my_z + r, NZ) * NY + my_y
        return remote(
            sums_row.at[parts[p]],
            sums_z.at[my_z, parts[p]],
            sz_send.at[p, r],
            sz_recv.at[p, my_z],
            head=there,
        )

    def sz_arrive(p, r):
        other = lax.rem(my_z + r, NZ)
        return remote(
            sums_row.at[parts[p]],
            sums_z.at[other, parts[p]],
            sz_send.at[p, r],
            sz_recv.at[p, other],
            head=other * NY + my_y,
        )

    def sy_copy(p, r):
        there = my_z * NY + lax.rem(my_y + r, NY)
        return remote(
            half_sums.at[parts[p]],
            sums_y.at[my_y, parts[p]],
            sy_send.at[p, r],
            sy_recv.at[p, my_y],
            head=there,
        )

    def sy_arrive(p, r):
        other = lax.rem(my_y + r, NY)
        return remote(
            half_sums.at[parts[p]],
            sums_y.at[other, parts[p]],
            sy_send.at[p, r],
            sy_recv.at[p, other],
            head=my_z * NY + other,
        )

    def sums_start(p):
        for r in order:
            sz_copy(p, r).start()
        sums_z[my_z, parts[p], :] = sums_row[parts[p], :]

    def sums_turn(p):
        for r in order:
            sz_arrive(p, r).wait_recv()
        added = sums_z[0, parts[p], :]
        for k in range(1, NZ):
            added = added + sums_z[k, parts[p], :]
        half_sums[parts[p], :] = added
        sums_y[my_y, parts[p], :] = added
        for r in (1, 3, 2):
            sy_copy(p, r).start()

    def sums_end(p):
        for r in (1, 3, 2):
            sy_arrive(p, r).wait_recv()
        added = sums_y[0, parts[p], :]
        for k in range(1, NY):
            added = added + sums_y[k, parts[p], :]
        total_ref[parts[p], :] = added

    def phase4(j):
        for e in range(2):
            i = 2 * j + e
            base = pl.multiple_of(i * GROUP, GROUP)
            whole = local_state[i] + carry_in[...] * prec[i][0:1]
            whole_high = whole.astype(BF16)
            whole_low = (whole - whole_high.astype(F32)).astype(BF16)
            c_i = cmat[i]
            carried = dot(
                jnp.concatenate([c_i, c_i], axis=1),
                jnp.concatenate([whole_high, whole_low], axis=0),
            )
            g = ydiag[pl.ds(base, GROUP), :] + carried * egate[pl.ds(base, GROUP), :].astype(F32)
            g = g.astype(BF16)
            xbuf[pl.ds(HALO + base, GROUP), :] = g
            squares = g * g
            sums = lax.dot_general(
                ones, squares, (((1,), (1,)), ((), ())), preferred_element_type=F32
            )
            sums_row[pl.ds(jnp.where(i < 12, i, i + 4), 1), :] = sums[0:1]
        g_copy(2 * j).start()
        g_copy(2 * j + 1).start()

        @pl.when(j == 5)
        def _():
            sums_start(0)

    loop(PAIRS, phase4)
    sums_start(1)
    sums_turn(0)
    sums_turn(1)
    sums_end(0)

    @pl.when(seq < NSEQ - 1)
    def _():
        halo_bc().wait_send()
        halo_x().wait_send()

    for r in order:
        first_z(r).wait_send()
    for r in y_order:
        first_y(r).wait_send()
    others(NSEQ, seq, lambda j: sd_copy(j, seq).wait_send())
    for kind in range(2):
        for c in range(2):
            for r in order:
                z_send(kind, c, r).wait_send()
            y_copy(kind, c, my_y, True).wait_send()
            y_copy(kind, c, my_y, False).wait_send()
            f_copy(kind, c, below, True).wait_send()
            f_copy(kind, c, above, False).wait_send()
        for r in y_order:
            side_send(kind, r).wait_send()
        for hop in range(NZ // 2):
            ring_done(kind, hop)
    others(NSEQ, seq, lambda j: st_copy(j, seq).wait_send())
    others(NSEQ, seq, lambda j: cb_copy(j, seq).wait_send())

    loop(BLOCKS, lambda i: g_copy(i).wait())
    for p in range(2):
        for r in order:
            sz_copy(p, r).wait_send()
    sums_end(1)
    for p in range(2):
        for r in (1, 3, 2):
            sy_copy(p, r).wait_send()


def scale(g_hbm, total_hbm, gain_hbm, out_hbm, g_in, g_out, total, gain_in, in_sem, out_sem, sem):
    rows = GROUP * SCALED

    def come(k):
        part = pl.ds(rows * k, rows)
        return pltpu.make_async_copy(g_hbm.at[part], g_in.at[part], in_sem.at[k])

    def go(k):
        part = pl.ds(rows * k, rows)
        return pltpu.make_async_copy(g_out.at[part], out_hbm.at[part], out_sem.at[k])

    total_copy = pltpu.make_async_copy(total_hbm, total, sem.at[0])
    gain_copy = pltpu.make_async_copy(gain_hbm, gain_in, sem.at[1])
    total_copy.start()
    gain_copy.start()
    for k in range(BLOCKS // SCALED):
        come(k).start()
    total_copy.wait()
    gain_copy.wait()
    gain = gain_in[...][None, :]
    factor = lax.rsqrt(total[...] * (1.0 / (NHEAD * WIDTH)) + 1e-05).T
    for k in range(BLOCKS // SCALED):
        come(k).wait()
        for j in range(SCALED * k, SCALED * (k + 1)):
            place = j if j < 12 else j + 4
            part = slice(GROUP * j, GROUP * (j + 1))
            scaled = g_in[part, :].astype(F32) * factor[:, place : place + 1] * gain
            g_out[part, :] = scaled.astype(BF16)
        go(k).start()
    for k in range(BLOCKS // SCALED):
        go(k).wait()


def body(x_rows, z_rows, b_rows, c_rows, step_raw, conv_x, conv_b, conv_c, decay_rate, norm_gain):
    vmem = pl.BlockSpec(memory_space=pltpu.VMEM)
    hbm = pl.BlockSpec(memory_space=pl.ANY)
    smem = pl.BlockSpec(memory_space=pltpu.SMEM)
    dma = pltpu.SemaphoreType.DMA
    g, totals = pl.pallas_call(
        layer,
        out_shape=(
            jax.ShapeDtypeStruct((LENGTH, WIDTH), BF16),
            jax.ShapeDtypeStruct((24, GROUP), F32),
        ),
        in_specs=[hbm, hbm, vmem, vmem, vmem, vmem, vmem, vmem, smem],
        out_specs=(hbm, vmem),
        scratch_shapes=[
            pltpu.VMEM((HALO + LENGTH, WIDTH), BF16),
            pltpu.VMEM((LENGTH, WIDTH), BF16),
            pltpu.VMEM((LENGTH, WIDTH), BF16),
            pltpu.VMEM((LENGTH, WIDTH), BF16),
            pltpu.VMEM((LENGTH, WIDTH), BF16),
            pltpu.VMEM((BLOCKS, HEADS, HALF, HALF), BF16),
            pltpu.VMEM((BLOCKS, HEADS, HALF, GROUP), BF16),
            pltpu.VMEM((2, NY, NZ, 16, HALF * PAIRS), BF16),
            pltpu.VMEM((BLOCKS, GROUP, STATE), BF16),
            pltpu.VMEM((BLOCKS, STATE, GROUP), BF16),
            pltpu.VMEM((LENGTH, WIDTH), F32),
            pltpu.VMEM((BLOCKS, STATE, WIDTH), F32),
            pltpu.VMEM((BLOCKS, GROUP, 24), F32),
            pltpu.VMEM((BLOCKS, 24, GROUP), F32),
            pltpu.VMEM((BLOCKS, 8, GROUP), F32),
            pltpu.VMEM((BLOCKS, 8, GROUP), F32),
            pltpu.VMEM((8, HALF + LENGTH), F32),
            pltpu.VMEM((BLOCKS + 1, 8, WIDTH), F32),
            pltpu.VMEM((STATE, WIDTH), F32),
            pltpu.VMEM((BLOCKS, 8, WIDTH), F32),
            pltpu.VMEM((NSEQ, 8, WIDTH), F32),
            pltpu.VMEM((NSEQ, PART, WIDTH), F32),
            pltpu.VMEM((NSEQ, PART, WIDTH), F32),
            pltpu.VMEM((STATE, WIDTH), F32),
            pltpu.VMEM((24, GROUP), F32),
            pltpu.VMEM((NZ, 24, GROUP), F32),
            pltpu.VMEM((24, GROUP), F32),
            pltpu.VMEM((NY, 24, GROUP), F32),
            dma((LOADS,)),
            dma,
            dma((BLOCKS,)),
            dma((2,)),
            dma((2,)),
            dma((2, 2, NZ)),
            dma((2, 2, NZ)),
            dma((2, 2, 2)),
            dma((2, 2, 2)),
            dma((2, 2, 2)),
            dma((2, 2, 2)),
            dma((NSEQ,)),
            dma((NSEQ,)),
            dma((NSEQ,)),
            dma((NSEQ,)),
            dma((NZ,)),
            dma((NZ,)),
            dma((NY,)),
            dma((NY,)),
            dma((NSEQ,)),
            dma((NSEQ,)),
            dma((2, NY)),
            dma((2, NY)),
            dma((2, NZ // 2, 2)),
            dma((2, NZ // 2, 2)),
            dma((2, NZ)),
            dma((2, NZ)),
            dma((2, NY)),
            dma((2, NY)),
        ],
        compiler_params=pltpu.CompilerParams(
            collective_id=0, has_side_effects=True, vmem_limit_bytes=60 * 2**20
        ),
        name="layer",
    )(x_rows, z_rows, b_rows.T, c_rows.T, step_raw.T, conv_x, conv_b, conv_c, decay_rate)
    return pl.pallas_call(
        scale,
        out_shape=jax.ShapeDtypeStruct((LENGTH, WIDTH), BF16),
        in_specs=[hbm, hbm, hbm],
        out_specs=hbm,
        scratch_shapes=[
            pltpu.VMEM((LENGTH, WIDTH), BF16),
            pltpu.VMEM((LENGTH, WIDTH), BF16),
            pltpu.VMEM((24, GROUP), F32),
            pltpu.VMEM((WIDTH,), F32),
            dma((BLOCKS // SCALED,)),
            dma((BLOCKS // SCALED,)),
            dma((2,)),
        ],
        compiler_params=pltpu.CompilerParams(vmem_limit_bytes=60 * 2**20),
        name="scale",
    )(g, totals, norm_gain)


def solution(mesh):
    placed = (
        P("seq", "head"),
        P("seq", "head"),
        P("seq", "head"),
        P("seq", "head"),
        P("seq", "head"),
        P(None, "head"),
        P(None, "head"),
        P(None, "head"),
        P("head"),
        P("head"),
    )
    return jax.shard_map(
        body, mesh=mesh, in_specs=placed, out_specs=P("seq", "head"), check_vma=False
    )
```

```python
import functools

import jax
import jax.numpy as jnp
from jax import lax
from jax.experimental import pallas as pl
from jax.experimental.pallas import tpu as pltpu
from jax.sharding import PartitionSpec as P

GROUP = 256
HALF = 128
HEADS = 6
WIDTH = 384
LENGTH = 5120
BLOCKS = 20
PAIRS = BLOCKS // 2
LOADS = 4
PER = BLOCKS // LOADS
FIRST = (0, 128)
SPANS = (((128, 384), (512, 384)), ((128, 384), (512, 384)))
SIDE = ((896, 384), (896, 384))
SCALED = 2
NSEQ = 8
NZ = 8
NY = 4
NHEAD = NZ * NY
STATE = 128
PART = STATE // NSEQ
HALO = 16
MASKED = -1e30
F32 = jnp.float32
BF16 = jnp.bfloat16


def remote(src, dst, send, recv, **where):
    return pltpu.make_async_remote_copy(
        src_ref=src,
        dst_ref=dst,
        send_sem=send,
        recv_sem=recv,
        device_id=where,
        device_id_type=pl.DeviceIdType.MESH,
    )


def loop(count, body):
    lax.fori_loop(0, count, lambda i, _: (body(i), 0)[1], 0)


def dot(a, b):
    return jnp.dot(a, b, preferred_element_type=F32)


def layer(
    x_hbm,
    z_hbm,
    b_ref,
    c_ref,
    raw_ref,
    taps_ref,
    taps_b_ref,
    taps_c_ref,
    rate_ref,
    g_hbm,
    total_ref,
    xbuf,
    zbuf,
    egate,
    xs_even,
    xs_odd,
    near,
    far,
    gath,
    cmat,
    bmat,
    ydiag,
    local_state,
    colq,
    rowq,
    bq,
    stepq,
    bcx,
    prec,
    state,
    gones,
    got_decay,
    got,
    back,
    carry_in,
    sums_row,
    sums_z,
    half_sums,
    sums_y,
    x_sem,
    z_sem,
    g_sem,
    halo_send,
    halo_recv,
    zs_send,
    zs_recv,
    ys_send,
    ys_recv,
    yf_send,
    yf_recv,
    st_send,
    st_recv,
    cb_send,
    cb_recv,
    tz_send,
    tz_recv,
    ty_send,
    ty_recv,
    sd_send,
    sd_recv,
    side_out,
    side_in,
    ring_out,
    ring_in,
    sz_send,
    sz_recv,
    sy_send,
    sy_recv,
):
    seq = lax.axis_index("seq")
    head = lax.axis_index("head")
    my_z = head // NY
    my_y = head % NY
    rows = LENGTH // LOADS

    def x_copy(c):
        part = pl.multiple_of(c * rows, rows)
        return pltpu.make_async_copy(
            x_hbm.at[pl.ds(part, rows)], xbuf.at[pl.ds(HALO + part, rows)], x_sem.at[c]
        )

    z_copy = pltpu.make_async_copy(z_hbm, zbuf, z_sem)

    barrier = pltpu.get_barrier_semaphore()

    def greet(**where):
        pl.semaphore_signal(
            barrier, inc=1, device_id=where, device_id_type=pl.DeviceIdType.MESH
        )

    for r in range(1, NZ):
        greet(head=lax.rem(my_z + r, NZ) * NY + my_y)
    for r in range(1, NY):
        greet(head=my_z * NY + lax.rem(my_y + r, NY))
    for r in range(1, NSEQ):
        greet(seq=lax.rem(seq + r, NSEQ))
    for c in range(LOADS):
        x_copy(c).start()
    z_copy.start()

    bcx[0:4, HALF:] = b_ref[...].astype(F32)
    bcx[4:8, HALF:] = c_ref[...].astype(F32)
    taps_bc = jnp.concatenate([taps_b_ref[...].astype(F32), taps_c_ref[...].astype(F32)], axis=1)
    taps_bc = taps_bc.T * 0.5
    head_row = lax.broadcasted_iota(jnp.int32, (8, GROUP), 0)
    rate = jnp.zeros((8, GROUP), F32)
    for h in range(HEADS):
        rate = jnp.where(head_row == h, rate_ref[h], rate)
    sums_row[...] = jnp.zeros_like(sums_row)

    def conv_bc(ext):
        acc = ext * taps_bc[:, 3:4]
        for back_by in (1, 2, 3):
            acc = acc + pltpu.roll(ext, back_by, axis=1) * taps_bc[:, 3 - back_by : 4 - back_by]
        return acc + acc * jnp.tanh(acc)

    def put_tile(kind, pair, quarters):
        tile = jnp.concatenate([q[4 * kind : 4 * kind + 4] for q in quarters], axis=0)
        gath[kind, my_y, my_z, :, HALF * pair : HALF * (pair + 1)] = tile.astype(BF16)

    acc = conv_bc(bcx[:, HALF:])
    quarters = [acc[:, HALF * k : HALF * (k + 1)] for k in range(4 * PAIRS)]
    for kind in range(2):
        for pair in range(1, PAIRS):
            put_tile(kind, pair, quarters[4 * pair : 4 * pair + 4])

    pl.semaphore_wait(barrier, NZ - 1 + NY - 1 + NSEQ - 1)

    def halo_bc():
        return remote(
            bcx.at[:, pl.ds(LENGTH, HALF)],
            bcx.at[:, pl.ds(0, HALF)],
            halo_send.at[0],
            halo_recv.at[0],
            seq=lax.rem(seq + 1, NSEQ),
        )

    def halo_x():
        return remote(
            x_hbm.at[pl.ds(LENGTH - HALO, HALO)],
            xbuf.at[pl.ds(0, HALO)],
            halo_send.at[1],
            halo_recv.at[1],
            seq=lax.rem(seq + 1, NSEQ),
        )

    @pl.when(seq < NSEQ - 1)
    def _():
        halo_bc().start()
        halo_x().start()

    def part(kind, y, z, span):
        return gath.at[kind, y, z, :, pl.ds(*span)]

    def z_send(kind, c, r):
        ref = part(kind, my_y, my_z, SPANS[kind][c])
        there = lax.rem(my_z + r, NZ) * NY + my_y
        return remote(ref, ref, zs_send.at[kind, c, r], zs_recv.at[kind, c, my_z], head=there)

    def z_arrive(kind, c, r):
        other = lax.rem(my_z + r, NZ)
        ref = part(kind, my_y, other, SPANS[kind][c])
        return remote(
            ref,
            ref,
            zs_send.at[kind, c, r],
            zs_recv.at[kind, c, other],
            head=other * NY + my_y,
        )

    order = (1, 7, 2, 6, 3, 5, 4)

    def side_send(kind, r):
        ref = part(kind, my_y, my_z, SIDE[kind])
        there = my_z * NY + lax.rem(my_y + r, NY)
        return remote(ref, ref, side_out.at[kind, r], side_in.at[kind, my_y], head=there)

    def side_arrive(kind, r):
        other = lax.rem(my_y + r, NY)
        ref = part(kind, other, my_z, SIDE[kind])
        return remote(
            ref, ref, side_out.at[kind, r], side_in.at[kind, other], head=my_z * NY + other
        )

    y_order = (1, 3, 2)

    def send_z(kind, c):
        for r in order:
            z_send(kind, c, r).start()

    send_z(0, 0)
    for r in y_order:
        side_send(0, r).start()
    send_z(0, 1)
    for r in y_order:
        side_send(1, r).start()

    raw = raw_ref[...]
    stepq[...] = jnp.ones_like(stepq)
    step_all = jnp.maximum(raw, 0.0) + jnp.log1p(jnp.exp(-jnp.abs(raw)))
    for i in range(BLOCKS):
        stepq[i, 0:HEADS, :] = step_all[:, GROUP * i : GROUP * (i + 1)]
    step = stepq[...]
    decay = -(step * rate[None])
    decay = decay.reshape(BLOCKS * 8, GROUP)
    row = lax.broadcasted_iota(jnp.int32, (GROUP, GROUP), 0)
    col = lax.broadcasted_iota(jnp.int32, (GROUP, GROUP), 1)
    upper = jnp.where(row <= col, 1.0, 0.0).astype(BF16)
    high = decay.astype(BF16)
    rest = decay - high.astype(F32)
    mid = rest.astype(BF16)
    low = (rest - mid.astype(F32)).astype(BF16)
    cum = dot(high, upper) + (dot(mid, upper) + dot(low, upper))
    last = cum[:, GROUP - 1 : GROUP]
    step2 = step.reshape(BLOCKS * 8, GROUP)
    rowq[:, 0:8, :] = cum.reshape(BLOCKS, 8, GROUP)
    rowq[:, 8:16, :] = (jnp.exp(last - cum) * step2).reshape(BLOCKS, 8, GROUP)
    rowq[:, 16:24, :] = jnp.exp(cum).reshape(BLOCKS, 8, GROUP)
    bq[...] = (cum - jnp.log(step2)).reshape(BLOCKS, 8, GROUP)

    above = lax.rem(my_y + 1, NY)
    below = lax.rem(my_y + NY - 1, NY)
    across = lax.rem(my_y + 2, NY)
    ups = my_z * NY + above
    downs = my_z * NY + below

    def y_copy(kind, c, slot, up):
        ref = gath.at[kind, slot, :, :, pl.ds(*SPANS[kind][c])]
        way = 0 if up else 1
        return remote(
            ref,
            ref,
            ys_send.at[kind, c, way],
            ys_recv.at[kind, c, way],
            head=ups if up else downs,
        )

    def f_copy(kind, c, slot, up):
        first = 0 if up else NZ // 2
        ref = gath.at[kind, slot, pl.ds(first, NZ // 2), :, pl.ds(*SPANS[kind][c])]
        way = 0 if up else 1
        return remote(
            ref,
            ref,
            yf_send.at[kind, c, way],
            yf_recv.at[kind, c, way],
            head=ups if up else downs,
        )

    z_above = lax.rem(my_z + 1, NZ) * NY + my_y
    z_below = lax.rem(my_z + NZ - 1, NZ) * NY + my_y

    def ring(kind, hop, up, block):
        half = NY // 2
        if hop < NZ // 2 - 1:
            ref = gath.at[kind, :, block, :, pl.ds(*SIDE[kind])]
        elif up:
            ref = gath.at[kind, pl.ds(0, half), block, :, pl.ds(*SIDE[kind])]
        else:
            ref = gath.at[kind, pl.ds(half, half), block, :, pl.ds(*SIDE[kind])]
        way = 0 if up else 1
        return remote(
            ref,
            ref,
            ring_out.at[kind, hop, way],
            ring_in.at[kind, hop, way],
            head=z_above if up else z_below,
        )

    def ring_send(kind, hop):
        ring(kind, hop, True, lax.rem(my_z + NZ - hop, NZ)).start()
        ring(kind, hop, False, lax.rem(my_z + hop, NZ)).start()

    def ring_arrive(kind, hop):
        ring(kind, hop, True, lax.rem(my_z + NZ - hop - 1, NZ)).wait_recv()
        ring(kind, hop, False, lax.rem(my_z + hop + 1, NZ)).wait_recv()

    def ring_done(kind, hop):
        ring(kind, hop, True, lax.rem(my_z + NZ - hop, NZ)).wait_send()
        ring(kind, hop, False, lax.rem(my_z + hop, NZ)).wait_send()

    def event_side(kind):
        for r in y_order:
            side_arrive(kind, r).wait_recv()
        ring_send(kind, 0)

    def event_ring(kind, hop):
        ring_arrive(kind, hop - 1)
        ring_send(kind, hop)

    def event_z(kind, c):
        for r in order:
            z_arrive(kind, c, r).wait_recv()
        y_copy(kind, c, my_y, True).start()
        y_copy(kind, c, my_y, False).start()

    def event_f(kind, c):
        y_copy(kind, c, below, True).wait_recv()
        f_copy(kind, c, below, True).start()
        y_copy(kind, c, above, False).wait_recv()
        f_copy(kind, c, above, False).start()

    def event_d(kind, c):
        f_copy(kind, c, across, True).wait_recv()
        f_copy(kind, c, across, False).wait_recv()

    def first_part(y, z):
        return gath.at[:, y, z, :, pl.ds(*FIRST)]

    def first_z(r):
        ref = first_part(my_y, my_z)
        there = lax.rem(my_z + r, NZ) * NY + my_y
        return remote(ref, ref, tz_send.at[r], tz_recv.at[my_z], head=there)

    def first_z_arrive(r):
        other = lax.rem(my_z + r, NZ)
        ref = first_part(my_y, other)
        return remote(ref, ref, tz_send.at[r], tz_recv.at[other], head=other * NY + my_y)

    def first_y(r):
        ref = gath.at[:, my_y, :, :, pl.ds(*FIRST)]
        there = my_z * NY + lax.rem(my_y + r, NY)
        return remote(ref, ref, ty_send.at[r], ty_recv.at[my_y], head=there)

    def first_y_arrive(r):
        other = lax.rem(my_y + r, NY)
        ref = gath.at[:, other, :, :, pl.ds(*FIRST)]
        return remote(ref, ref, ty_send.at[r], ty_recv.at[other], head=my_z * NY + other)

    def event_first():
        for r in order:
            first_z_arrive(r).wait_recv()
        for r in y_order:
            first_y(r).start()

    def event_first_done():
        for r in y_order:
            first_y_arrive(r).wait_recv()

    def event_halo():
        @pl.when(seq > 0)
        def _():
            halo_bc().wait_recv()
            halo_x().wait_recv()

        @pl.when(seq == 0)
        def _():
            bcx[:, 0:HALF] = jnp.zeros((8, HALF), F32)
            xbuf[0:HALO, :] = jnp.zeros((HALO, WIDTH), BF16)

        first = conv_bc(bcx[:, 0 : 2 * HALF])[:, HALF:]
        for kind in range(2):
            put_tile(kind, 0, [first] + quarters[1:4])
        for r in order:
            first_z(r).start()

    taps = taps_ref[...].astype(F32) * 0.5
    even = lax.broadcasted_iota(jnp.int32, (HALF, HALF), 1) < 64
    row1 = lax.broadcasted_iota(jnp.int32, (HALF, HALF), 0)
    col1 = lax.broadcasted_iota(jnp.int32, (HALF, HALF), 1)
    causal = row1 >= col1
    of_head = lax.broadcasted_iota(jnp.int32, (8, WIDTH), 1) >> 6

    def phase1(i):
        base = pl.multiple_of(i * GROUP, GROUP)
        for low in (0, HALF):
            for lane in range(0, WIDTH, HALF):
                span = slice(lane, lane + HALF)
                wide = xbuf[pl.ds(base + low, HALF + HALO), span].astype(F32)
                once = pltpu.roll(wide, 1, axis=0)
                older = pltpu.roll(wide * taps[1:2, span] + once * taps[0:1, span], 2, axis=0)
                half = (
                    wide[HALO:] * taps[3:4, span] + once[HALO:] * taps[2:3, span] + older[HALO:]
                )
                xs = (half + half * jnp.tanh(half)).astype(BF16)
                none = jnp.zeros_like(xs)
                xs_even[pl.ds(base + low, HALF), span] = jnp.where(even, xs, none)
                xs_odd[pl.ds(base + low, HALF), span] = jnp.where(even, none, xs)
        cols = rowq[i].T
        colq[i] = cols
        ends = cols[GROUP - 8 :, 16:24]
        gone = jnp.zeros((8, WIDTH), F32)
        for h in range(HEADS):
            gone = jnp.where(of_head == h, ends[7:8, h : h + 1], gone)
        gones[i] = gone
        b_all = bq[i]
        for h in range(HEADS):
            a = cols[:, h : h + 1]
            b = b_all[h : h + 1, :]
            gap1 = jnp.where(causal, a[:HALF] - b[:, :HALF], MASKED)
            gap2 = a[HALF:] - b[:, :HALF]
            gap3 = jnp.where(causal, a[HALF:] - b[:, HALF:], MASKED)
            near[i, h] = jnp.exp(gap1.astype(BF16))
            far[i, h, :, 0:HALF] = jnp.exp(gap2.astype(BF16))
            far[i, h, :, HALF:] = jnp.exp(gap3.astype(BF16))

    def step1(i):
        block = lax.rem(i + 1, BLOCKS)

        @pl.when((i == 0) | ((lax.rem(block, PER) == 0) & (block > 0)))
        def _():
            x_copy(block // PER).wait()

        phase1(block)

    def run(count, unit, before):
        def step(i):
            for when, events in before.items():

                @pl.when(i == when)
                def _(events=events):
                    for event, *which in events:
                        event(*which)

            unit(i)

        loop(count, step)

    run(
        BLOCKS,
        step1,
        {
            5: [(event_side, 0), (event_side, 1), (event_halo,), (send_z, 1, 0)],
            9: [(event_z, 0, 0)],
            12: [(event_ring, 0, 1), (event_z, 0, 1), (send_z, 1, 1)],
            14: [(event_ring, 1, 1), (event_first,)],
            15: [(event_f, 0, 0)],
            18: [(event_f, 0, 1), (event_ring, 0, 2)],
        },
    )

    spread_row = lax.broadcasted_iota(jnp.int32, (24, WIDTH), 0)
    spread_col = lax.broadcasted_iota(jnp.int32, (24, WIDTH), 1) >> 6
    spread_w = jnp.where(spread_row == spread_col + 8, 1.0, 0.0).astype(BF16)
    spread_e = jnp.where(spread_row == spread_col + 16, 1.0, 0.0).astype(BF16)
    upper4 = lax.broadcasted_iota(jnp.int32, (8, HALF), 0) < 4

    state[...] = jnp.zeros_like(state)

    so_far = jnp.ones((8, WIDTH), F32)
    prec[0] = so_far
    for i in range(BLOCKS):
        so_far = so_far * gones[i]
        prec[i + 1] = so_far
    got_decay[seq] = so_far

    def others(count, me, body):
        loop(count - 1, lambda r: body(lax.rem(me + 1 + r, count)))

    def sd_copy(j, slot):
        return remote(
            prec.at[BLOCKS], got_decay.at[slot], sd_send.at[j], sd_recv.at[slot], seq=j
        )

    others(NSEQ, seq, lambda j: sd_copy(j, seq).start())

    def assemble(kind, j):
        lane = pl.multiple_of(j * HALF, HALF)
        blocks = ([], [])
        for pair in range(NHEAD // 2):
            y, z = (2 * pair) // NZ, (2 * pair) % NZ
            first = gath[kind, y, z, :, pl.ds(lane, HALF)].astype(F32)
            second = gath[kind, y, z + 1, :, pl.ds(lane, HALF)].astype(F32)
            for e in range(2):
                one = first[8 * e : 8 * e + 8]
                two = second[8 * e : 8 * e + 8]
                left = jnp.where(upper4, one, pltpu.roll(two, 4, axis=0))
                right = jnp.where(upper4, pltpu.roll(one, 4, axis=0), two)
                blocks[e].append(jnp.concatenate([left, right], axis=1))
        return [jnp.concatenate(block, axis=0) for block in blocks]

    def phase2(j):
        blocks = (2 * j, 2 * j + 1)
        bases = [pl.multiple_of(i * GROUP, GROUP) for i in blocks]
        weights = [dot(colq[i].astype(BF16), spread_w) for i in blocks]
        b_ts = [b_t.astype(BF16) for b_t in assemble(0, j)]
        weighted = []
        for base, weight in zip(bases, weights):
            xs = (xs_even[pl.ds(base, GROUP), :] + xs_odd[pl.ds(base, GROUP), :]).astype(F32)
            weighted.append((weight * xs).astype(BF16))
        news = [dot(b_t, w) for b_t, w in zip(b_ts, weighted)]
        for i, b_t in zip(blocks, b_ts):
            bmat[i] = b_t
        goes = [gones[i] for i in blocks]
        old = state[...]
        local_state[2 * j] = old
        old = old * goes[0][0:1] + news[0]
        local_state[2 * j + 1] = old
        state[...] = old * goes[1][0:1] + news[1]

    def phase3(j):
        blocks = (2 * j, 2 * j + 1)
        bases = [pl.multiple_of(i * GROUP, GROUP) for i in blocks]
        c_is = [c_t.T.astype(BF16) for c_t in assemble(1, j)]
        scores = [dot(c_i, bmat[i]).astype(BF16) for i, c_i in zip(blocks, c_is)]
        for i, c_i in zip(blocks, c_is):
            cmat[i] = c_i
        for pair in range(HEADS // 2):
            span = slice(HALF * pair, HALF * (pair + 1))
            results = []
            for i, base, score in zip(blocks, bases, scores):
                top = score[:HALF, :HALF]
                low_rows = score[HALF:, :]
                xe = xs_even[pl.ds(base, GROUP), span]
                xo = xs_odd[pl.ds(base, GROUP), span]
                m1 = jnp.concatenate(
                    [top * near[i, 2 * pair], top * near[i, 2 * pair + 1]], axis=1
                )
                m2 = jnp.concatenate(
                    [low_rows * far[i, 2 * pair], low_rows * far[i, 2 * pair + 1]], axis=1
                )
                x1 = jnp.concatenate([xe[:HALF], xo[:HALF]], axis=0)
                x2 = jnp.concatenate([xe, xo], axis=0)
                results.append((dot(m1, x1), dot(m2, x2)))
            for base, (upper_rows, lower_rows) in zip(bases, results):
                gate = zbuf[pl.ds(base, GROUP), span].astype(F32)
                ydiag[pl.ds(base, HALF), span] = upper_rows * gate[:HALF]
                ydiag[pl.ds(base + HALF, HALF), span] = lower_rows * gate[HALF:]

    def gates(i):
        base = pl.multiple_of(i * GROUP, GROUP)
        half = zbuf[pl.ds(base, GROUP), :].astype(F32) * 0.5
        gate = half + half * jnp.tanh(half)
        zbuf[pl.ds(base, GROUP), :] = gate.astype(BF16)
        grown = dot(colq[i].astype(BF16), spread_e)
        egate[pl.ds(base, GROUP), :] = (gate * grown).astype(BF16)

    z_copy.wait()
    run(BLOCKS // 2, gates, {0: [(event_z, 1, 0)]})
    run(
        PAIRS,
        phase2,
        {
            0: [(event_ring, 1, 2), (event_first_done,)],
            1: [(event_d, 0, 0)],
            2: [(event_ring, 0, 3), (event_z, 1, 1)],
            4: [(event_d, 0, 1)],
            6: [(event_ring, 1, 3)],
            7: [(ring_arrive, 0, 3)],
            8: [(event_f, 1, 0)],
        },
    )

    def st_copy(j, slot):
        place = pl.multiple_of(j * PART, PART)
        return remote(
            state.at[pl.ds(place, PART)], got.at[slot], st_send.at[j], st_recv.at[slot], seq=j
        )

    def cb_copy(j, slot):
        place = pl.multiple_of(slot * PART, PART)
        return remote(
            back.at[j], carry_in.at[pl.ds(place, PART)], cb_send.at[j], cb_recv.at[slot], seq=j
        )

    others(NSEQ, seq, lambda j: st_copy(j, seq).start())
    got[seq] = state[pl.ds(pl.multiple_of(seq * PART, PART), PART), :]
    run(BLOCKS // 2, lambda i: gates(BLOCKS // 2 + i), {6: [(event_f, 1, 1)]})

    def event_states():
        others(NSEQ, seq, lambda j: sd_copy(j, j).wait_recv())
        others(NSEQ, seq, lambda j: st_copy(j, j).wait_recv())
        carry = jnp.zeros((PART, WIDTH), F32)
        for j in range(NSEQ):
            back[j] = carry
            carry = carry * got_decay[j, 0:1, :] + got[j]
        others(NSEQ, seq, lambda j: cb_copy(j, seq).start())
        carry_in[pl.ds(pl.multiple_of(seq * PART, PART), PART), :] = back[seq]

    run(
        PAIRS,
        lambda i: phase3(lax.rem(i + 7, PAIRS)),
        {
            0: [(ring_arrive, 1, 3)],
            4: [(event_d, 1, 0), (event_states,)],
            7: [(event_d, 1, 1)],
        },
    )
    others(NSEQ, seq, lambda j: cb_copy(j, j).wait_recv())

    ones = jnp.ones((8, WIDTH), BF16)

    def g_copy(i):
        base = pl.multiple_of(i * GROUP, GROUP)
        return pltpu.make_async_copy(
            xbuf.at[pl.ds(HALO + base, GROUP)], g_hbm.at[pl.ds(base, GROUP)], g_sem.at[i]
        )

    parts = (pl.ds(0, 16), pl.ds(16, 8))

    def sz_copy(p, r):
        there = lax.rem(my_z + r, NZ) * NY + my_y
        return remote(
            sums_row.at[parts[p]],
            sums_z.at[my_z, parts[p]],
            sz_send.at[p, r],
            sz_recv.at[p, my_z],
            head=there,
        )

    def sz_arrive(p, r):
        other = lax.rem(my_z + r, NZ)
        return remote(
            sums_row.at[parts[p]],
            sums_z.at[other, parts[p]],
            sz_send.at[p, r],
            sz_recv.at[p, other],
            head=other * NY + my_y,
        )

    def sy_copy(p, r):
        there = my_z * NY + lax.rem(my_y + r, NY)
        return remote(
            half_sums.at[parts[p]],
            sums_y.at[my_y, parts[p]],
            sy_send.at[p, r],
            sy_recv.at[p, my_y],
            head=there,
        )

    def sy_arrive(p, r):
        other = lax.rem(my_y + r, NY)
        return remote(
            half_sums.at[parts[p]],
            sums_y.at[other, parts[p]],
            sy_send.at[p, r],
            sy_recv.at[p, other],
            head=my_z * NY + other,
        )

    def sums_start(p):
        for r in order:
            sz_copy(p, r).start()
        sums_z[my_z, parts[p], :] = sums_row[parts[p], :]

    def sums_turn(p):
        for r in order:
            sz_arrive(p, r).wait_recv()
        added = sums_z[0, parts[p], :]
        for k in range(1, NZ):
            added = added + sums_z[k, parts[p], :]
        half_sums[parts[p], :] = added
        sums_y[my_y, parts[p], :] = added
        for r in (1, 3, 2):
            sy_copy(p, r).start()

    def sums_end(p):
        for r in (1, 3, 2):
            sy_arrive(p, r).wait_recv()
        added = sums_y[0, parts[p], :]
        for k in range(1, NY):
            added = added + sums_y[k, parts[p], :]
        total_ref[parts[p], :] = added

    def phase4(j):
        blocks = [4 * j + e for e in range(4)]
        bases = [pl.multiple_of(i * GROUP, GROUP) for i in blocks]
        operands = []
        for i in blocks:
            whole = local_state[i] + carry_in[...] * prec[i][0:1]
            whole_high = whole.astype(BF16)
            whole_low = (whole - whole_high.astype(F32)).astype(BF16)
            operands.append(jnp.concatenate([whole_high, whole_low], axis=0))
        products = []
        for i, operand in zip(blocks, operands):
            c_i = cmat[i]
            products.append(dot(jnp.concatenate([c_i, c_i], axis=1), operand))
        values = []
        for base, carried in zip(bases, products):
            factor = egate[pl.ds(base, GROUP), :].astype(F32)
            values.append((ydiag[pl.ds(base, GROUP), :] + carried * factor).astype(BF16))
        for i, base, g in zip(blocks, bases, values):
            sums = lax.dot_general(
                ones, g * g, (((1,), (1,)), ((), ())), preferred_element_type=F32
            )
            xbuf[pl.ds(HALO + base, GROUP), :] = g
            sums_row[pl.ds(jnp.where(i < 12, i, i + 4), 1), :] = sums[0:1]
        for i in blocks:
            g_copy(i).start()

        @pl.when(j == 2)
        def _():
            sums_start(0)

    loop(BLOCKS // 4, phase4)
    sums_start(1)
    sums_turn(0)
    sums_turn(1)
    sums_end(0)

    @pl.when(seq < NSEQ - 1)
    def _():
        halo_bc().wait_send()
        halo_x().wait_send()

    for r in order:
        first_z(r).wait_send()
    for r in y_order:
        first_y(r).wait_send()
    others(NSEQ, seq, lambda j: sd_copy(j, seq).wait_send())
    for kind in range(2):
        for c in range(2):
            for r in order:
                z_send(kind, c, r).wait_send()
            y_copy(kind, c, my_y, True).wait_send()
            y_copy(kind, c, my_y, False).wait_send()
            f_copy(kind, c, below, True).wait_send()
            f_copy(kind, c, above, False).wait_send()
        for r in y_order:
            side_send(kind, r).wait_send()
        for hop in range(NZ // 2):
            ring_done(kind, hop)
    others(NSEQ, seq, lambda j: st_copy(j, seq).wait_send())
    others(NSEQ, seq, lambda j: cb_copy(j, seq).wait_send())

    loop(BLOCKS, lambda i: g_copy(i).wait())
    for p in range(2):
        for r in order:
            sz_copy(p, r).wait_send()
    sums_end(1)
    for p in range(2):
        for r in (1, 3, 2):
            sy_copy(p, r).wait_send()


def scale(g_hbm, total_hbm, gain_hbm, out_hbm, g_in, g_out, total, gain_in, in_sem, out_sem, sem):
    rows = GROUP * SCALED

    def come(k):
        part = pl.ds(rows * k, rows)
        return pltpu.make_async_copy(g_hbm.at[part], g_in.at[part], in_sem.at[k])

    def go(k):
        part = pl.ds(rows * k, rows)
        return pltpu.make_async_copy(g_out.at[part], out_hbm.at[part], out_sem.at[k])

    total_copy = pltpu.make_async_copy(total_hbm, total, sem.at[0])
    gain_copy = pltpu.make_async_copy(gain_hbm, gain_in, sem.at[1])
    total_copy.start()
    gain_copy.start()
    for k in range(BLOCKS // SCALED):
        come(k).start()
    total_copy.wait()
    gain_copy.wait()
    gain = gain_in[...][None, :]
    factor = lax.rsqrt(total[...] * (1.0 / (NHEAD * WIDTH)) + 1e-05).T
    for k in range(BLOCKS // SCALED):
        come(k).wait()
        for j in range(SCALED * k, SCALED * (k + 1)):
            place = j if j < 12 else j + 4
            part = slice(GROUP * j, GROUP * (j + 1))
            g_out[part, :] = g_in[part, :] * (factor[:, place : place + 1] * gain).astype(BF16)
        go(k).start()
    for k in range(BLOCKS // SCALED):
        go(k).wait()


def body(x_rows, z_rows, b_rows, c_rows, step_raw, conv_x, conv_b, conv_c, decay_rate, norm_gain):
    vmem = pl.BlockSpec(memory_space=pltpu.VMEM)
    hbm = pl.BlockSpec(memory_space=pl.ANY)
    smem = pl.BlockSpec(memory_space=pltpu.SMEM)
    dma = pltpu.SemaphoreType.DMA
    g, totals = pl.pallas_call(
        layer,
        out_shape=(
            jax.ShapeDtypeStruct((LENGTH, WIDTH), BF16),
            jax.ShapeDtypeStruct((24, GROUP), F32),
        ),
        in_specs=[hbm, hbm, vmem, vmem, vmem, vmem, vmem, vmem, smem],
        out_specs=(hbm, vmem),
        scratch_shapes=[
            pltpu.VMEM((HALO + LENGTH, WIDTH), BF16),
            pltpu.VMEM((LENGTH, WIDTH), BF16),
            pltpu.VMEM((LENGTH, WIDTH), BF16),
            pltpu.VMEM((LENGTH, WIDTH), BF16),
            pltpu.VMEM((LENGTH, WIDTH), BF16),
            pltpu.VMEM((BLOCKS, HEADS, HALF, HALF), BF16),
            pltpu.VMEM((BLOCKS, HEADS, HALF, GROUP), BF16),
            pltpu.VMEM((2, NY, NZ, 16, HALF * PAIRS), BF16),
            pltpu.VMEM((BLOCKS, GROUP, STATE), BF16),
            pltpu.VMEM((BLOCKS, STATE, GROUP), BF16),
            pltpu.VMEM((LENGTH, WIDTH), F32),
            pltpu.VMEM((BLOCKS, STATE, WIDTH), F32),
            pltpu.VMEM((BLOCKS, GROUP, 24), F32),
            pltpu.VMEM((BLOCKS, 24, GROUP), F32),
            pltpu.VMEM((BLOCKS, 8, GROUP), F32),
            pltpu.VMEM((BLOCKS, 8, GROUP), F32),
            pltpu.VMEM((8, HALF + LENGTH), F32),
            pltpu.VMEM((BLOCKS + 1, 8, WIDTH), F32),
            pltpu.VMEM((STATE, WIDTH), F32),
            pltpu.VMEM((BLOCKS, 8, WIDTH), F32),
            pltpu.VMEM((NSEQ, 8, WIDTH), F32),
            pltpu.VMEM((NSEQ, PART, WIDTH), F32),
            pltpu.VMEM((NSEQ, PART, WIDTH), F32),
            pltpu.VMEM((STATE, WIDTH), F32),
            pltpu.VMEM((24, GROUP), F32),
            pltpu.VMEM((NZ, 24, GROUP), F32),
            pltpu.VMEM((24, GROUP), F32),
            pltpu.VMEM((NY, 24, GROUP), F32),
            dma((LOADS,)),
            dma,
            dma((BLOCKS,)),
            dma((2,)),
            dma((2,)),
            dma((2, 2, NZ)),
            dma((2, 2, NZ)),
            dma((2, 2, 2)),
            dma((2, 2, 2)),
            dma((2, 2, 2)),
            dma((2, 2, 2)),
            dma((NSEQ,)),
            dma((NSEQ,)),
            dma((NSEQ,)),
            dma((NSEQ,)),
            dma((NZ,)),
            dma((NZ,)),
            dma((NY,)),
            dma((NY,)),
            dma((NSEQ,)),
            dma((NSEQ,)),
            dma((2, NY)),
            dma((2, NY)),
            dma((2, NZ // 2, 2)),
            dma((2, NZ // 2, 2)),
            dma((2, NZ)),
            dma((2, NZ)),
            dma((2, NY)),
            dma((2, NY)),
        ],
        compiler_params=pltpu.CompilerParams(
            collective_id=0, has_side_effects=True, vmem_limit_bytes=60 * 2**20
        ),
        name="layer",
    )(x_rows, z_rows, b_rows.T, c_rows.T, step_raw.T, conv_x, conv_b, conv_c, decay_rate)
    return pl.pallas_call(
        scale,
        out_shape=jax.ShapeDtypeStruct((LENGTH, WIDTH), BF16),
        in_specs=[hbm, hbm, hbm],
        out_specs=hbm,
        scratch_shapes=[
            pltpu.VMEM((LENGTH, WIDTH), BF16),
            pltpu.VMEM((LENGTH, WIDTH), BF16),
            pltpu.VMEM((24, GROUP), F32),
            pltpu.VMEM((WIDTH,), F32),
            dma((BLOCKS // SCALED,)),
            dma((BLOCKS // SCALED,)),
            dma((2,)),
        ],
        compiler_params=pltpu.CompilerParams(vmem_limit_bytes=60 * 2**20),
        name="scale",
    )(g, totals, norm_gain)


def solution(mesh):
    placed = (
        P("seq", "head"),
        P("seq", "head"),
        P("seq", "head"),
        P("seq", "head"),
        P("seq", "head"),
        P(None, "head"),
        P(None, "head"),
        P(None, "head"),
        P("head"),
        P("head"),
    )
    return jax.shard_map(
        body, mesh=mesh, in_specs=placed, out_specs=P("seq", "head"), check_vma=False
    )
```

```python
import functools

import jax
import jax.numpy as jnp
from jax import lax
from jax.experimental import pallas as pl
from jax.experimental.pallas import tpu as pltpu
from jax.sharding import PartitionSpec as P

GROUP = 256
HALF = 128
HEADS = 6
WIDTH = 384
LENGTH = 5120
BLOCKS = 20
PAIRS = BLOCKS // 2
LOADS = 4
PER = BLOCKS // LOADS
FIRST = (0, 128)
SPANS = (((128, 384), (512, 384)), ((128, 384), (512, 384)))
SIDE = ((896, 384), (896, 384))
SCALED = 2
NSEQ = 8
NZ = 8
NY = 4
NHEAD = NZ * NY
STATE = 128
PART = STATE // NSEQ
HALO = 16
MASKED = -1e30
F32 = jnp.float32
BF16 = jnp.bfloat16


def remote(src, dst, send, recv, **where):
    return pltpu.make_async_remote_copy(
        src_ref=src,
        dst_ref=dst,
        send_sem=send,
        recv_sem=recv,
        device_id=where,
        device_id_type=pl.DeviceIdType.MESH,
    )


def loop(count, body):
    lax.fori_loop(0, count, lambda i, _: (body(i), 0)[1], 0)


def dot(a, b):
    return jnp.dot(a, b, preferred_element_type=F32)


def layer(
    x_hbm,
    z_hbm,
    b_ref,
    c_ref,
    raw_ref,
    taps_ref,
    taps_b_ref,
    taps_c_ref,
    rate_ref,
    g_hbm,
    total_ref,
    xbuf,
    zbuf,
    egate,
    xs_even,
    xs_odd,
    near,
    far,
    gath,
    cmat,
    bmat,
    ydiag,
    local_state,
    colq,
    rowq,
    bq,
    stepq,
    bcx,
    prec,
    state,
    gones,
    got_decay,
    got,
    back,
    carry_in,
    sums_row,
    sums_z,
    half_sums,
    sums_y,
    x_sem,
    z_sem,
    g_sem,
    halo_send,
    halo_recv,
    zs_send,
    zs_recv,
    ys_send,
    ys_recv,
    yf_send,
    yf_recv,
    st_send,
    st_recv,
    cb_send,
    cb_recv,
    tz_send,
    tz_recv,
    ty_send,
    ty_recv,
    sd_send,
    sd_recv,
    side_out,
    side_in,
    ring_out,
    ring_in,
    sz_send,
    sz_recv,
    sy_send,
    sy_recv,
):
    seq = lax.axis_index("seq")
    head = lax.axis_index("head")
    my_z = head // NY
    my_y = head % NY
    rows = LENGTH // LOADS

    def x_copy(c):
        part = pl.multiple_of(c * rows, rows)
        return pltpu.make_async_copy(
            x_hbm.at[pl.ds(part, rows)], xbuf.at[pl.ds(HALO + part, rows)], x_sem.at[c]
        )

    z_copy = pltpu.make_async_copy(z_hbm, zbuf, z_sem)

    barrier = pltpu.get_barrier_semaphore()

    def greet(**where):
        pl.semaphore_signal(
            barrier, inc=1, device_id=where, device_id_type=pl.DeviceIdType.MESH
        )

    for r in range(1, NZ):
        greet(head=lax.rem(my_z + r, NZ) * NY + my_y)
    for r in range(1, NY):
        greet(head=my_z * NY + lax.rem(my_y + r, NY))
    for r in range(1, NSEQ):
        greet(seq=lax.rem(seq + r, NSEQ))
    for c in range(LOADS):
        x_copy(c).start()
    z_copy.start()

    bcx[0:4, HALF:] = b_ref[...].astype(F32)
    bcx[4:8, HALF:] = c_ref[...].astype(F32)
    taps_bc = jnp.concatenate([taps_b_ref[...].astype(F32), taps_c_ref[...].astype(F32)], axis=1)
    taps_bc = taps_bc.T * 0.5
    head_row = lax.broadcasted_iota(jnp.int32, (8, GROUP), 0)
    rate = jnp.zeros((8, GROUP), F32)
    for h in range(HEADS):
        rate = jnp.where(head_row == h, rate_ref[h], rate)
    sums_row[...] = jnp.zeros_like(sums_row)

    def conv_bc(ext):
        acc = ext * taps_bc[:, 3:4]
        for back_by in (1, 2, 3):
            acc = acc + pltpu.roll(ext, back_by, axis=1) * taps_bc[:, 3 - back_by : 4 - back_by]
        return acc + acc * jnp.tanh(acc)

    def put_tile(kind, pair, quarters):
        tile = jnp.concatenate([q[4 * kind : 4 * kind + 4] for q in quarters], axis=0)
        gath[kind, my_y, my_z, :, HALF * pair : HALF * (pair + 1)] = tile.astype(BF16)

    acc = conv_bc(bcx[:, HALF:])
    quarters = [acc[:, HALF * k : HALF * (k + 1)] for k in range(4 * PAIRS)]
    for kind in range(2):
        for pair in range(1, PAIRS):
            put_tile(kind, pair, quarters[4 * pair : 4 * pair + 4])

    pl.semaphore_wait(barrier, NZ - 1 + NY - 1 + NSEQ - 1)

    def halo_bc():
        return remote(
            bcx.at[:, pl.ds(LENGTH, HALF)],
            bcx.at[:, pl.ds(0, HALF)],
            halo_send.at[0],
            halo_recv.at[0],
            seq=lax.rem(seq + 1, NSEQ),
        )

    def halo_x():
        return remote(
            x_hbm.at[pl.ds(LENGTH - HALO, HALO)],
            xbuf.at[pl.ds(0, HALO)],
            halo_send.at[1],
            halo_recv.at[1],
            seq=lax.rem(seq + 1, NSEQ),
        )

    @pl.when(seq < NSEQ - 1)
    def _():
        halo_bc().start()
        halo_x().start()

    def part(kind, y, z, span):
        return gath.at[kind, y, z, :, pl.ds(*span)]

    def z_send(kind, c, r):
        ref = part(kind, my_y, my_z, SPANS[kind][c])
        there = lax.rem(my_z + r, NZ) * NY + my_y
        return remote(ref, ref, zs_send.at[kind, c, r], zs_recv.at[kind, c, my_z], head=there)

    def z_arrive(kind, c, r):
        other = lax.rem(my_z + r, NZ)
        ref = part(kind, my_y, other, SPANS[kind][c])
        return remote(
            ref,
            ref,
            zs_send.at[kind, c, r],
            zs_recv.at[kind, c, other],
            head=other * NY + my_y,
        )

    order = (1, 7, 2, 6, 3, 5, 4)

    def side_send(kind, r):
        ref = part(kind, my_y, my_z, SIDE[kind])
        there = my_z * NY + lax.rem(my_y + r, NY)
        return remote(ref, ref, side_out.at[kind, r], side_in.at[kind, my_y], head=there)

    def side_arrive(kind, r):
        other = lax.rem(my_y + r, NY)
        ref = part(kind, other, my_z, SIDE[kind])
        return remote(
            ref, ref, side_out.at[kind, r], side_in.at[kind, other], head=my_z * NY + other
        )

    y_order = (1, 3, 2)

    def send_z(kind, c):
        for r in order:
            z_send(kind, c, r).start()

    send_z(0, 0)
    for r in y_order:
        side_send(0, r).start()
    send_z(0, 1)
    for r in y_order:
        side_send(1, r).start()

    raw = raw_ref[...]
    stepq[...] = jnp.ones_like(stepq)
    step_all = jnp.maximum(raw, 0.0) + jnp.log1p(jnp.exp(-jnp.abs(raw)))
    for i in range(BLOCKS):
        stepq[i, 0:HEADS, :] = step_all[:, GROUP * i : GROUP * (i + 1)]
    step = stepq[...]
    decay = -(step * rate[None])
    decay = decay.reshape(BLOCKS * 8, GROUP)
    row = lax.broadcasted_iota(jnp.int32, (GROUP, GROUP), 0)
    col = lax.broadcasted_iota(jnp.int32, (GROUP, GROUP), 1)
    upper = jnp.where(row <= col, 1.0, 0.0).astype(BF16)
    high = decay.astype(BF16)
    rest = decay - high.astype(F32)
    mid = rest.astype(BF16)
    low = (rest - mid.astype(F32)).astype(BF16)
    cum = dot(high, upper) + (dot(mid, upper) + dot(low, upper))
    last = cum[:, GROUP - 1 : GROUP]
    step2 = step.reshape(BLOCKS * 8, GROUP)
    cum_high = cum.astype(BF16).astype(F32)
    cum_mid = (cum - cum_high).astype(BF16).astype(F32)
    rowq[:, 0:8, :] = cum_high.reshape(BLOCKS, 8, GROUP)
    rowq[:, 8:16, :] = cum_mid.reshape(BLOCKS, 8, GROUP)
    rowq[:, 16:24, :] = (cum - cum_high - cum_mid).reshape(BLOCKS, 8, GROUP)
    rowq[:, 24:32, :] = (jnp.exp(last - cum) * step2).reshape(BLOCKS, 8, GROUP)
    rowq[:, 32:40, :] = jnp.exp(cum).reshape(BLOCKS, 8, GROUP)
    bq[...] = (cum - jnp.log(step2)).reshape(BLOCKS, 8, GROUP)

    above = lax.rem(my_y + 1, NY)
    below = lax.rem(my_y + NY - 1, NY)
    across = lax.rem(my_y + 2, NY)
    ups = my_z * NY + above
    downs = my_z * NY + below

    def y_copy(kind, c, slot, up):
        ref = gath.at[kind, slot, :, :, pl.ds(*SPANS[kind][c])]
        way = 0 if up else 1
        return remote(
            ref,
            ref,
            ys_send.at[kind, c, way],
            ys_recv.at[kind, c, way],
            head=ups if up else downs,
        )

    def f_copy(kind, c, slot, up):
        first = 0 if up else NZ // 2
        ref = gath.at[kind, slot, pl.ds(first, NZ // 2), :, pl.ds(*SPANS[kind][c])]
        way = 0 if up else 1
        return remote(
            ref,
            ref,
            yf_send.at[kind, c, way],
            yf_recv.at[kind, c, way],
            head=ups if up else downs,
        )

    z_above = lax.rem(my_z + 1, NZ) * NY + my_y
    z_below = lax.rem(my_z + NZ - 1, NZ) * NY + my_y

    def ring(kind, hop, up, block):
        half = NY // 2
        if hop < NZ // 2 - 1:
            ref = gath.at[kind, :, block, :, pl.ds(*SIDE[kind])]
        elif up:
            ref = gath.at[kind, pl.ds(0, half), block, :, pl.ds(*SIDE[kind])]
        else:
            ref = gath.at[kind, pl.ds(half, half), block, :, pl.ds(*SIDE[kind])]
        way = 0 if up else 1
        return remote(
            ref,
            ref,
            ring_out.at[kind, hop, way],
            ring_in.at[kind, hop, way],
            head=z_above if up else z_below,
        )

    def ring_send(kind, hop):
        ring(kind, hop, True, lax.rem(my_z + NZ - hop, NZ)).start()
        ring(kind, hop, False, lax.rem(my_z + hop, NZ)).start()

    def ring_arrive(kind, hop):
        ring(kind, hop, True, lax.rem(my_z + NZ - hop - 1, NZ)).wait_recv()
        ring(kind, hop, False, lax.rem(my_z + hop + 1, NZ)).wait_recv()

    def ring_done(kind, hop):
        ring(kind, hop, True, lax.rem(my_z + NZ - hop, NZ)).wait_send()
        ring(kind, hop, False, lax.rem(my_z + hop, NZ)).wait_send()

    def event_side(kind):
        for r in y_order:
            side_arrive(kind, r).wait_recv()
        ring_send(kind, 0)

    def event_ring(kind, hop):
        ring_arrive(kind, hop - 1)
        ring_send(kind, hop)

    def event_z(kind, c):
        for r in order:
            z_arrive(kind, c, r).wait_recv()
        y_copy(kind, c, my_y, True).start()
        y_copy(kind, c, my_y, False).start()

    def event_f(kind, c):
        y_copy(kind, c, below, True).wait_recv()
        f_copy(kind, c, below, True).start()
        y_copy(kind, c, above, False).wait_recv()
        f_copy(kind, c, above, False).start()

    def event_d(kind, c):
        f_copy(kind, c, across, True).wait_recv()
        f_copy(kind, c, across, False).wait_recv()

    def first_part(y, z):
        return gath.at[:, y, z, :, pl.ds(*FIRST)]

    def first_z(r):
        ref = first_part(my_y, my_z)
        there = lax.rem(my_z + r, NZ) * NY + my_y
        return remote(ref, ref, tz_send.at[r], tz_recv.at[my_z], head=there)

    def first_z_arrive(r):
        other = lax.rem(my_z + r, NZ)
        ref = first_part(my_y, other)
        return remote(ref, ref, tz_send.at[r], tz_recv.at[other], head=other * NY + my_y)

    def first_y(r):
        ref = gath.at[:, my_y, :, :, pl.ds(*FIRST)]
        there = my_z * NY + lax.rem(my_y + r, NY)
        return remote(ref, ref, ty_send.at[r], ty_recv.at[my_y], head=there)

    def first_y_arrive(r):
        other = lax.rem(my_y + r, NY)
        ref = gath.at[:, other, :, :, pl.ds(*FIRST)]
        return remote(ref, ref, ty_send.at[r], ty_recv.at[other], head=my_z * NY + other)

    def event_first():
        for r in order:
            first_z_arrive(r).wait_recv()
        for r in y_order:
            first_y(r).start()

    def event_first_done():
        for r in y_order:
            first_y_arrive(r).wait_recv()

    def event_halo():
        @pl.when(seq > 0)
        def _():
            halo_bc().wait_recv()
            halo_x().wait_recv()

        @pl.when(seq == 0)
        def _():
            bcx[:, 0:HALF] = jnp.zeros((8, HALF), F32)
            xbuf[0:HALO, :] = jnp.zeros((HALO, WIDTH), BF16)

        first = conv_bc(bcx[:, 0 : 2 * HALF])[:, HALF:]
        for kind in range(2):
            put_tile(kind, 0, [first] + quarters[1:4])
        for r in order:
            first_z(r).start()

    taps = taps_ref[...].astype(F32) * 0.5
    even = lax.broadcasted_iota(jnp.int32, (HALF, HALF), 1) < 64
    row1 = lax.broadcasted_iota(jnp.int32, (HALF, HALF), 0)
    col1 = lax.broadcasted_iota(jnp.int32, (HALF, HALF), 1)
    causal = row1 >= col1
    spread_row = lax.broadcasted_iota(jnp.int32, (40, HALF * HEADS), 0)
    spread_col = lax.broadcasted_iota(jnp.int32, (40, HALF * HEADS), 1) >> 7
    picked = (spread_row < 24) & ((spread_row & 7) == spread_col)
    spread_a = jnp.where(picked, 1.0, 0.0).astype(BF16)
    of_head = lax.broadcasted_iota(jnp.int32, (8, WIDTH), 1) >> 6

    def phase1(i):
        base = pl.multiple_of(i * GROUP, GROUP)
        for low in (0, HALF):
            for lane in range(0, WIDTH, HALF):
                span = slice(lane, lane + HALF)
                wide = xbuf[pl.ds(base + low, HALF + HALO), span].astype(F32)
                once = pltpu.roll(wide, 1, axis=0)
                older = pltpu.roll(wide * taps[1:2, span] + once * taps[0:1, span], 2, axis=0)
                half = (
                    wide[HALO:] * taps[3:4, span] + once[HALO:] * taps[2:3, span] + older[HALO:]
                )
                xs = (half + half * jnp.tanh(half)).astype(BF16)
                none = jnp.zeros_like(xs)
                xs_even[pl.ds(base + low, HALF), span] = jnp.where(even, xs, none)
                xs_odd[pl.ds(base + low, HALF), span] = jnp.where(even, none, xs)
        cols = rowq[i].T
        colb = cols.astype(BF16)
        colq[i] = colb
        ends = cols[GROUP - 8 :, 32:40]
        gone = jnp.zeros((8, WIDTH), F32)
        for h in range(HEADS):
            gone = jnp.where(of_head == h, ends[7:8, h : h + 1], gone)
        gones[i] = gone
        b_all = bq[i]
        for h in range(HEADS):
            if h % 2 == 0:
                two = dot(colb, spread_a[:, HALF * h : HALF * (h + 2)])
            a = two[:, HALF * (h % 2) : HALF * (h % 2 + 1)]
            b = b_all[h : h + 1, :]
            gap1 = jnp.where(causal, a[:HALF] - b[:, :HALF], MASKED)
            gap2 = a[HALF:] - b[:, :HALF]
            gap3 = jnp.where(causal, a[HALF:] - b[:, HALF:], MASKED)
            near[i, h] = jnp.exp(gap1.astype(BF16))
            far[i, h, :, 0:HALF] = jnp.exp(gap2.astype(BF16))
            far[i, h, :, HALF:] = jnp.exp(gap3.astype(BF16))

    def step1(i):
        block = lax.rem(i + 1, BLOCKS)

        @pl.when((i == 0) | ((lax.rem(block, PER) == 0) & (block > 0)))
        def _():
            x_copy(block // PER).wait()

        phase1(block)

    def run(count, unit, before):
        def step(i):
            for when, events in before.items():

                @pl.when(i == when)
                def _(events=events):
                    for event, *which in events:
                        event(*which)

            unit(i)

        loop(count, step)

    run(
        BLOCKS,
        step1,
        {
            5: [(event_side, 0), (event_side, 1), (event_halo,), (send_z, 1, 0)],
            9: [(event_z, 0, 0)],
            12: [(event_ring, 0, 1), (event_z, 0, 1), (send_z, 1, 1)],
            14: [(event_ring, 1, 1), (event_first,)],
            15: [(event_f, 0, 0)],
            18: [(event_f, 0, 1), (event_ring, 0, 2)],
        },
    )

    spread_row = lax.broadcasted_iota(jnp.int32, (40, WIDTH), 0)
    spread_col = lax.broadcasted_iota(jnp.int32, (40, WIDTH), 1) >> 6
    spread_w = jnp.where(spread_row == spread_col + 24, 1.0, 0.0).astype(BF16)
    spread_e = jnp.where(spread_row == spread_col + 32, 1.0, 0.0).astype(BF16)
    upper4 = lax.broadcasted_iota(jnp.int32, (8, HALF), 0) < 4

    state[...] = jnp.zeros_like(state)

    so_far = jnp.ones((8, WIDTH), F32)
    prec[0] = so_far
    for i in range(BLOCKS):
        so_far = so_far * gones[i]
        prec[i + 1] = so_far
    got_decay[seq] = so_far

    def others(count, me, body):
        loop(count - 1, lambda r: body(lax.rem(me + 1 + r, count)))

    def sd_copy(j, slot):
        return remote(
            prec.at[BLOCKS], got_decay.at[slot], sd_send.at[j], sd_recv.at[slot], seq=j
        )

    others(NSEQ, seq, lambda j: sd_copy(j, seq).start())

    def assemble(kind, j):
        lane = pl.multiple_of(j * HALF, HALF)
        blocks = ([], [])
        for pair in range(NHEAD // 2):
            y, z = (2 * pair) // NZ, (2 * pair) % NZ
            first = gath[kind, y, z, :, pl.ds(lane, HALF)].astype(F32)
            second = gath[kind, y, z + 1, :, pl.ds(lane, HALF)].astype(F32)
            for e in range(2):
                one = first[8 * e : 8 * e + 8]
                two = second[8 * e : 8 * e + 8]
                left = jnp.where(upper4, one, pltpu.roll(two, 4, axis=0))
                right = jnp.where(upper4, pltpu.roll(one, 4, axis=0), two)
                blocks[e].append(jnp.concatenate([left, right], axis=1))
        return [jnp.concatenate(block, axis=0) for block in blocks]

    def phase2(j):
        blocks = (2 * j, 2 * j + 1)
        bases = [pl.multiple_of(i * GROUP, GROUP) for i in blocks]
        weights = [dot(colq[i], spread_w) for i in blocks]
        b_ts = [b_t.astype(BF16) for b_t in assemble(0, j)]
        weighted = []
        for base, weight in zip(bases, weights):
            xs = (xs_even[pl.ds(base, GROUP), :] + xs_odd[pl.ds(base, GROUP), :]).astype(F32)
            weighted.append((weight * xs).astype(BF16))
        news = [dot(b_t, w) for b_t, w in zip(b_ts, weighted)]
        for i, b_t in zip(blocks, b_ts):
            bmat[i] = b_t
        goes = [gones[i] for i in blocks]
        old = state[...]
        local_state[2 * j] = old
        old = old * goes[0][0:1] + news[0]
        local_state[2 * j + 1] = old
        state[...] = old * goes[1][0:1] + news[1]

    def phase3(j):
        blocks = (2 * j, 2 * j + 1)
        bases = [pl.multiple_of(i * GROUP, GROUP) for i in blocks]
        c_is = [c_t.T.astype(BF16) for c_t in assemble(1, j)]
        scores = [dot(c_i, bmat[i]).astype(BF16) for i, c_i in zip(blocks, c_is)]
        for i, c_i in zip(blocks, c_is):
            cmat[i] = c_i
        for pair in range(HEADS // 2):
            span = slice(HALF * pair, HALF * (pair + 1))
            results = []
            for i, base, score in zip(blocks, bases, scores):
                top = score[:HALF, :HALF]
                low_rows = score[HALF:, :]
                xe = xs_even[pl.ds(base, GROUP), span]
                xo = xs_odd[pl.ds(base, GROUP), span]
                m1 = jnp.concatenate(
                    [top * near[i, 2 * pair], top * near[i, 2 * pair + 1]], axis=1
                )
                m2 = jnp.concatenate(
                    [low_rows * far[i, 2 * pair], low_rows * far[i, 2 * pair + 1]], axis=1
                )
                x1 = jnp.concatenate([xe[:HALF], xo[:HALF]], axis=0)
                x2 = jnp.concatenate([xe, xo], axis=0)
                results.append((dot(m1, x1), dot(m2, x2)))
            for base, (upper_rows, lower_rows) in zip(bases, results):
                gate = zbuf[pl.ds(base, GROUP), span].astype(F32)
                ydiag[pl.ds(base, HALF), span] = upper_rows * gate[:HALF]
                ydiag[pl.ds(base + HALF, HALF), span] = lower_rows * gate[HALF:]

    def gates(i):
        base = pl.multiple_of(i * GROUP, GROUP)
        half = zbuf[pl.ds(base, GROUP), :].astype(F32) * 0.5
        gate = half + half * jnp.tanh(half)
        zbuf[pl.ds(base, GROUP), :] = gate.astype(BF16)
        grown = dot(colq[i], spread_e)
        egate[pl.ds(base, GROUP), :] = (gate * grown).astype(BF16)

    z_copy.wait()
    run(BLOCKS // 2, gates, {0: [(event_z, 1, 0)]})
    run(
        PAIRS,
        phase2,
        {
            0: [(event_ring, 1, 2), (event_first_done,)],
            1: [(event_d, 0, 0)],
            2: [(event_ring, 0, 3), (event_z, 1, 1)],
            4: [(event_d, 0, 1)],
            6: [(event_ring, 1, 3)],
            7: [(ring_arrive, 0, 3)],
            8: [(event_f, 1, 0)],
        },
    )

    def st_copy(j, slot):
        place = pl.multiple_of(j * PART, PART)
        return remote(
            state.at[pl.ds(place, PART)], got.at[slot], st_send.at[j], st_recv.at[slot], seq=j
        )

    def cb_copy(j, slot):
        place = pl.multiple_of(slot * PART, PART)
        return remote(
            back.at[j], carry_in.at[pl.ds(place, PART)], cb_send.at[j], cb_recv.at[slot], seq=j
        )

    others(NSEQ, seq, lambda j: st_copy(j, seq).start())
    got[seq] = state[pl.ds(pl.multiple_of(seq * PART, PART), PART), :]
    run(BLOCKS // 2, lambda i: gates(BLOCKS // 2 + i), {6: [(event_f, 1, 1)]})

    def event_states():
        others(NSEQ, seq, lambda j: sd_copy(j, j).wait_recv())
        others(NSEQ, seq, lambda j: st_copy(j, j).wait_recv())
        carry = jnp.zeros((PART, WIDTH), F32)
        for j in range(NSEQ):
            back[j] = carry
            carry = carry * got_decay[j, 0:1, :] + got[j]
        others(NSEQ, seq, lambda j: cb_copy(j, seq).start())
        carry_in[pl.ds(pl.multiple_of(seq * PART, PART), PART), :] = back[seq]

    run(
        PAIRS,
        lambda i: phase3(lax.rem(i + 7, PAIRS)),
        {
            0: [(ring_arrive, 1, 3)],
            4: [(event_d, 1, 0), (event_states,)],
            7: [(event_d, 1, 1)],
        },
    )
    others(NSEQ, seq, lambda j: cb_copy(j, j).wait_recv())

    ones = jnp.ones((8, WIDTH), BF16)

    def g_copy(i):
        base = pl.multiple_of(i * GROUP, GROUP)
        return pltpu.make_async_copy(
            xbuf.at[pl.ds(HALO + base, GROUP)], g_hbm.at[pl.ds(base, GROUP)], g_sem.at[i]
        )

    parts = (pl.ds(0, 16), pl.ds(16, 8))

    def sz_copy(p, r):
        there = lax.rem(my_z + r, NZ) * NY + my_y
        return remote(
            sums_row.at[parts[p]],
            sums_z.at[my_z, parts[p]],
            sz_send.at[p, r],
            sz_recv.at[p, my_z],
            head=there,
        )

    def sz_arrive(p, r):
        other = lax.rem(my_z + r, NZ)
        return remote(
            sums_row.at[parts[p]],
            sums_z.at[other, parts[p]],
            sz_send.at[p, r],
            sz_recv.at[p, other],
            head=other * NY + my_y,
        )

    def sy_copy(p, r):
        there = my_z * NY + lax.rem(my_y + r, NY)
        return remote(
            half_sums.at[parts[p]],
            sums_y.at[my_y, parts[p]],
            sy_send.at[p, r],
            sy_recv.at[p, my_y],
            head=there,
        )

    def sy_arrive(p, r):
        other = lax.rem(my_y + r, NY)
        return remote(
            half_sums.at[parts[p]],
            sums_y.at[other, parts[p]],
            sy_send.at[p, r],
            sy_recv.at[p, other],
            head=my_z * NY + other,
        )

    def sums_start(p):
        for r in order:
            sz_copy(p, r).start()
        sums_z[my_z, parts[p], :] = sums_row[parts[p], :]

    def sums_turn(p):
        for r in order:
            sz_arrive(p, r).wait_recv()
        added = sums_z[0, parts[p], :]
        for k in range(1, NZ):
            added = added + sums_z[k, parts[p], :]
        half_sums[parts[p], :] = added
        sums_y[my_y, parts[p], :] = added
        for r in (1, 3, 2):
            sy_copy(p, r).start()

    def sums_end(p):
        for r in (1, 3, 2):
            sy_arrive(p, r).wait_recv()
        added = sums_y[0, parts[p], :]
        for k in range(1, NY):
            added = added + sums_y[k, parts[p], :]
        total_ref[parts[p], :] = added

    def phase4(j):
        blocks = [4 * j + e for e in range(4)]
        bases = [pl.multiple_of(i * GROUP, GROUP) for i in blocks]
        operands = []
        for i in blocks:
            whole = local_state[i] + carry_in[...] * prec[i][0:1]
            whole_high = whole.astype(BF16)
            whole_low = (whole - whole_high.astype(F32)).astype(BF16)
            operands.append(jnp.concatenate([whole_high, whole_low], axis=0))
        products = []
        for i, operand in zip(blocks, operands):
            c_i = cmat[i]
            products.append(dot(jnp.concatenate([c_i, c_i], axis=1), operand))
        values = []
        for base, carried in zip(bases, products):
            factor = egate[pl.ds(base, GROUP), :].astype(F32)
            values.append((ydiag[pl.ds(base, GROUP), :] + carried * factor).astype(BF16))
        for i, base, g in zip(blocks, bases, values):
            sums = lax.dot_general(
                ones, g * g, (((1,), (1,)), ((), ())), preferred_element_type=F32
            )
            xbuf[pl.ds(HALO + base, GROUP), :] = g
            sums_row[pl.ds(jnp.where(i < 12, i, i + 4), 1), :] = sums[0:1]
        for i in blocks:
            g_copy(i).start()

        @pl.when(j == 2)
        def _():
            sums_start(0)

    loop(BLOCKS // 4, phase4)
    sums_start(1)
    sums_turn(0)
    sums_turn(1)
    sums_end(0)

    @pl.when(seq < NSEQ - 1)
    def _():
        halo_bc().wait_send()
        halo_x().wait_send()

    for r in order:
        first_z(r).wait_send()
    for r in y_order:
        first_y(r).wait_send()
    others(NSEQ, seq, lambda j: sd_copy(j, seq).wait_send())
    for kind in range(2):
        for c in range(2):
            for r in order:
                z_send(kind, c, r).wait_send()
            y_copy(kind, c, my_y, True).wait_send()
            y_copy(kind, c, my_y, False).wait_send()
            f_copy(kind, c, below, True).wait_send()
            f_copy(kind, c, above, False).wait_send()
        for r in y_order:
            side_send(kind, r).wait_send()
        for hop in range(NZ // 2):
            ring_done(kind, hop)
    others(NSEQ, seq, lambda j: st_copy(j, seq).wait_send())
    others(NSEQ, seq, lambda j: cb_copy(j, seq).wait_send())

    loop(BLOCKS, lambda i: g_copy(i).wait())
    for p in range(2):
        for r in order:
            sz_copy(p, r).wait_send()
    sums_end(1)
    for p in range(2):
        for r in (1, 3, 2):
            sy_copy(p, r).wait_send()


def scale(g_hbm, total_hbm, gain_hbm, out_hbm, g_in, g_out, total, gain_in, in_sem, out_sem, sem):
    rows = GROUP * SCALED

    def come(k):
        part = pl.ds(rows * k, rows)
        return pltpu.make_async_copy(g_hbm.at[part], g_in.at[part], in_sem.at[k])

    def go(k):
        part = pl.ds(rows * k, rows)
        return pltpu.make_async_copy(g_out.at[part], out_hbm.at[part], out_sem.at[k])

    total_copy = pltpu.make_async_copy(total_hbm, total, sem.at[0])
    gain_copy = pltpu.make_async_copy(gain_hbm, gain_in, sem.at[1])
    total_copy.start()
    gain_copy.start()
    for k in range(BLOCKS // SCALED):
        come(k).start()
    total_copy.wait()
    gain_copy.wait()
    gain = gain_in[...][None, :]
    factor = lax.rsqrt(total[...] * (1.0 / (NHEAD * WIDTH)) + 1e-05).T
    for k in range(BLOCKS // SCALED):
        come(k).wait()
        for j in range(SCALED * k, SCALED * (k + 1)):
            place = j if j < 12 else j + 4
            part = slice(GROUP * j, GROUP * (j + 1))
            g_out[part, :] = g_in[part, :] * (factor[:, place : place + 1] * gain).astype(BF16)
        go(k).start()
    for k in range(BLOCKS // SCALED):
        go(k).wait()


def body(x_rows, z_rows, b_rows, c_rows, step_raw, conv_x, conv_b, conv_c, decay_rate, norm_gain):
    vmem = pl.BlockSpec(memory_space=pltpu.VMEM)
    hbm = pl.BlockSpec(memory_space=pl.ANY)
    smem = pl.BlockSpec(memory_space=pltpu.SMEM)
    dma = pltpu.SemaphoreType.DMA
    g, totals = pl.pallas_call(
        layer,
        out_shape=(
            jax.ShapeDtypeStruct((LENGTH, WIDTH), BF16),
            jax.ShapeDtypeStruct((24, GROUP), F32),
        ),
        in_specs=[hbm, hbm, vmem, vmem, vmem, vmem, vmem, vmem, smem],
        out_specs=(hbm, vmem),
        scratch_shapes=[
            pltpu.VMEM((HALO + LENGTH, WIDTH), BF16),
            pltpu.VMEM((LENGTH, WIDTH), BF16),
            pltpu.VMEM((LENGTH, WIDTH), BF16),
            pltpu.VMEM((LENGTH, WIDTH), BF16),
            pltpu.VMEM((LENGTH, WIDTH), BF16),
            pltpu.VMEM((BLOCKS, HEADS, HALF, HALF), BF16),
            pltpu.VMEM((BLOCKS, HEADS, HALF, GROUP), BF16),
            pltpu.VMEM((2, NY, NZ, 16, HALF * PAIRS), BF16),
            pltpu.VMEM((BLOCKS, GROUP, STATE), BF16),
            pltpu.VMEM((BLOCKS, STATE, GROUP), BF16),
            pltpu.VMEM((LENGTH, WIDTH), F32),
            pltpu.VMEM((BLOCKS, STATE, WIDTH), F32),
            pltpu.VMEM((BLOCKS, GROUP, 40), BF16),
            pltpu.VMEM((BLOCKS, 40, GROUP), F32),
            pltpu.VMEM((BLOCKS, 8, GROUP), F32),
            pltpu.VMEM((BLOCKS, 8, GROUP), F32),
            pltpu.VMEM((8, HALF + LENGTH), F32),
            pltpu.VMEM((BLOCKS + 1, 8, WIDTH), F32),
            pltpu.VMEM((STATE, WIDTH), F32),
            pltpu.VMEM((BLOCKS, 8, WIDTH), F32),
            pltpu.VMEM((NSEQ, 8, WIDTH), F32),
            pltpu.VMEM((NSEQ, PART, WIDTH), F32),
            pltpu.VMEM((NSEQ, PART, WIDTH), F32),
            pltpu.VMEM((STATE, WIDTH), F32),
            pltpu.VMEM((24, GROUP), F32),
            pltpu.VMEM((NZ, 24, GROUP), F32),
            pltpu.VMEM((24, GROUP), F32),
            pltpu.VMEM((NY, 24, GROUP), F32),
            dma((LOADS,)),
            dma,
            dma((BLOCKS,)),
            dma((2,)),
            dma((2,)),
            dma((2, 2, NZ)),
            dma((2, 2, NZ)),
            dma((2, 2, 2)),
            dma((2, 2, 2)),
            dma((2, 2, 2)),
            dma((2, 2, 2)),
            dma((NSEQ,)),
            dma((NSEQ,)),
            dma((NSEQ,)),
            dma((NSEQ,)),
            dma((NZ,)),
            dma((NZ,)),
            dma((NY,)),
            dma((NY,)),
            dma((NSEQ,)),
            dma((NSEQ,)),
            dma((2, NY)),
            dma((2, NY)),
            dma((2, NZ // 2, 2)),
            dma((2, NZ // 2, 2)),
            dma((2, NZ)),
            dma((2, NZ)),
            dma((2, NY)),
            dma((2, NY)),
        ],
        compiler_params=pltpu.CompilerParams(
            collective_id=0, has_side_effects=True, vmem_limit_bytes=60 * 2**20
        ),
        name="layer",
    )(x_rows, z_rows, b_rows.T, c_rows.T, step_raw.T, conv_x, conv_b, conv_c, decay_rate)
    return pl.pallas_call(
        scale,
        out_shape=jax.ShapeDtypeStruct((LENGTH, WIDTH), BF16),
        in_specs=[hbm, hbm, hbm],
        out_specs=hbm,
        scratch_shapes=[
            pltpu.VMEM((LENGTH, WIDTH), BF16),
            pltpu.VMEM((LENGTH, WIDTH), BF16),
            pltpu.VMEM((24, GROUP), F32),
            pltpu.VMEM((WIDTH,), F32),
            dma((BLOCKS // SCALED,)),
            dma((BLOCKS // SCALED,)),
            dma((2,)),
        ],
        compiler_params=pltpu.CompilerParams(vmem_limit_bytes=60 * 2**20),
        name="scale",
    )(g, totals, norm_gain)


def solution(mesh):
    placed = (
        P("seq", "head"),
        P("seq", "head"),
        P("seq", "head"),
        P("seq", "head"),
        P("seq", "head"),
        P(None, "head"),
        P(None, "head"),
        P(None, "head"),
        P("head"),
        P("head"),
    )
    return jax.shard_map(
        body, mesh=mesh, in_specs=placed, out_specs=P("seq", "head"), check_vma=False
    )
```

```python
import functools

import jax
import jax.numpy as jnp
from jax import lax
from jax.experimental import pallas as pl
from jax.experimental.pallas import tpu as pltpu
from jax.sharding import PartitionSpec as P

GROUP = 256
HALF = 128
HEADS = 6
WIDTH = 384
LENGTH = 5120
BLOCKS = 20
PAIRS = BLOCKS // 2
LOADS = 4
PER = BLOCKS // LOADS
FIRST = (0, 128)
SPANS = (((128, 384), (512, 384)), ((128, 384), (512, 384)))
SIDE = ((896, 384), (896, 384))
SCALED = 2
NSEQ = 8
NZ = 8
NY = 4
NHEAD = NZ * NY
STATE = 128
PART = STATE // NSEQ
HALO = 16
MASKED = -1e30
F32 = jnp.float32
BF16 = jnp.bfloat16


def remote(src, dst, send, recv, **where):
    return pltpu.make_async_remote_copy(
        src_ref=src,
        dst_ref=dst,
        send_sem=send,
        recv_sem=recv,
        device_id=where,
        device_id_type=pl.DeviceIdType.MESH,
    )


def loop(count, body):
    lax.fori_loop(0, count, lambda i, _: (body(i), 0)[1], 0)


def dot(a, b):
    return jnp.dot(a, b, preferred_element_type=F32)


def layer(
    x_hbm,
    z_hbm,
    b_ref,
    c_ref,
    raw_ref,
    taps_ref,
    taps_b_ref,
    taps_c_ref,
    rate_ref,
    g_hbm,
    total_ref,
    xbuf,
    zbuf,
    egate,
    xs_even,
    xs_odd,
    near,
    far,
    gath,
    cmat,
    bmat,
    ydiag,
    local_state,
    colq,
    rowq,
    bq,
    stepq,
    bcx,
    prec,
    state,
    gones,
    got_decay,
    got,
    back,
    carry_in,
    sums_row,
    sums_z,
    half_sums,
    sums_y,
    x_sem,
    z_sem,
    g_sem,
    halo_send,
    halo_recv,
    zs_send,
    zs_recv,
    ys_send,
    ys_recv,
    yf_send,
    yf_recv,
    st_send,
    st_recv,
    cb_send,
    cb_recv,
    tz_send,
    tz_recv,
    ty_send,
    ty_recv,
    sd_send,
    sd_recv,
    side_out,
    side_in,
    ring_out,
    ring_in,
    sz_send,
    sz_recv,
    sy_send,
    sy_recv,
):
    seq = lax.axis_index("seq")
    head = lax.axis_index("head")
    my_z = head // NY
    my_y = head % NY
    rows = LENGTH // LOADS

    def x_copy(c):
        part = pl.multiple_of(c * rows, rows)
        return pltpu.make_async_copy(
            x_hbm.at[pl.ds(part, rows)], xbuf.at[pl.ds(HALO + part, rows)], x_sem.at[c]
        )

    z_copy = pltpu.make_async_copy(z_hbm, zbuf, z_sem)

    barrier = pltpu.get_barrier_semaphore()

    def greet(**where):
        pl.semaphore_signal(
            barrier, inc=1, device_id=where, device_id_type=pl.DeviceIdType.MESH
        )

    for r in range(1, NZ):
        greet(head=lax.rem(my_z + r, NZ) * NY + my_y)
    for r in range(1, NY):
        greet(head=my_z * NY + lax.rem(my_y + r, NY))
    for r in range(1, NSEQ):
        greet(seq=lax.rem(seq + r, NSEQ))
    for c in range(LOADS):
        x_copy(c).start()
    z_copy.start()

    bcx[0:4, HALF:] = b_ref[...].astype(F32)
    bcx[4:8, HALF:] = c_ref[...].astype(F32)
    taps_bc = jnp.concatenate([taps_b_ref[...].astype(F32), taps_c_ref[...].astype(F32)], axis=1)
    taps_bc = taps_bc.T * 0.5
    head_row = lax.broadcasted_iota(jnp.int32, (8, GROUP), 0)
    rate = jnp.zeros((8, GROUP), F32)
    for h in range(HEADS):
        rate = jnp.where(head_row == h, rate_ref[h], rate)
    sums_row[...] = jnp.zeros_like(sums_row)

    def conv_bc(ext):
        acc = ext * taps_bc[:, 3:4]
        for back_by in (1, 2, 3):
            acc = acc + pltpu.roll(ext, back_by, axis=1) * taps_bc[:, 3 - back_by : 4 - back_by]
        return acc + acc * jnp.tanh(acc)

    def put_tile(kind, pair, quarters):
        tile = jnp.concatenate([q[4 * kind : 4 * kind + 4] for q in quarters], axis=0)
        gath[kind, my_y, my_z, :, HALF * pair : HALF * (pair + 1)] = tile.astype(BF16)

    acc = conv_bc(bcx[:, HALF:])
    quarters = [acc[:, HALF * k : HALF * (k + 1)] for k in range(4 * PAIRS)]
    for kind in range(2):
        for pair in range(1, PAIRS):
            put_tile(kind, pair, quarters[4 * pair : 4 * pair + 4])

    pl.semaphore_wait(barrier, NZ - 1 + NY - 1 + NSEQ - 1)

    def halo_bc():
        return remote(
            bcx.at[:, pl.ds(LENGTH, HALF)],
            bcx.at[:, pl.ds(0, HALF)],
            halo_send.at[0],
            halo_recv.at[0],
            seq=lax.rem(seq + 1, NSEQ),
        )

    def halo_x():
        return remote(
            x_hbm.at[pl.ds(LENGTH - HALO, HALO)],
            xbuf.at[pl.ds(0, HALO)],
            halo_send.at[1],
            halo_recv.at[1],
            seq=lax.rem(seq + 1, NSEQ),
        )

    @pl.when(seq < NSEQ - 1)
    def _():
        halo_bc().start()
        halo_x().start()

    def part(kind, y, z, span):
        return gath.at[kind, y, z, :, pl.ds(*span)]

    def z_send(kind, c, r):
        ref = part(kind, my_y, my_z, SPANS[kind][c])
        there = lax.rem(my_z + r, NZ) * NY + my_y
        return remote(ref, ref, zs_send.at[kind, c, r], zs_recv.at[kind, c, my_z], head=there)

    def z_arrive(kind, c, r):
        other = lax.rem(my_z + r, NZ)
        ref = part(kind, my_y, other, SPANS[kind][c])
        return remote(
            ref,
            ref,
            zs_send.at[kind, c, r],
            zs_recv.at[kind, c, other],
            head=other * NY + my_y,
        )

    order = (1, 7, 2, 6, 3, 5, 4)

    def side_send(kind, r):
        ref = part(kind, my_y, my_z, SIDE[kind])
        there = my_z * NY + lax.rem(my_y + r, NY)
        return remote(ref, ref, side_out.at[kind, r], side_in.at[kind, my_y], head=there)

    def side_arrive(kind, r):
        other = lax.rem(my_y + r, NY)
        ref = part(kind, other, my_z, SIDE[kind])
        return remote(
            ref, ref, side_out.at[kind, r], side_in.at[kind, other], head=my_z * NY + other
        )

    y_order = (1, 3, 2)

    def send_z(kind, c):
        for r in order:
            z_send(kind, c, r).start()

    send_z(0, 0)
    for r in y_order:
        side_send(0, r).start()
    send_z(0, 1)
    for r in y_order:
        side_send(1, r).start()

    raw = raw_ref[...]
    stepq[...] = jnp.ones_like(stepq)
    step_all = jnp.maximum(raw, 0.0) + jnp.log1p(jnp.exp(-jnp.abs(raw)))
    for i in range(BLOCKS):
        stepq[i, 0:HEADS, :] = step_all[:, GROUP * i : GROUP * (i + 1)]
    step = stepq[...]
    decay = -(step * rate[None])
    decay = decay.reshape(BLOCKS * 8, GROUP)
    row = lax.broadcasted_iota(jnp.int32, (GROUP, GROUP), 0)
    col = lax.broadcasted_iota(jnp.int32, (GROUP, GROUP), 1)
    upper = jnp.where(row <= col, 1.0, 0.0).astype(BF16)
    high = decay.astype(BF16)
    rest = decay - high.astype(F32)
    mid = rest.astype(BF16)
    low = (rest - mid.astype(F32)).astype(BF16)
    cum = dot(high, upper) + (dot(mid, upper) + dot(low, upper))
    last = cum[:, GROUP - 1 : GROUP]
    step2 = step.reshape(BLOCKS * 8, GROUP)
    cum_high = cum.astype(BF16).astype(F32)
    cum_mid = (cum - cum_high).astype(BF16).astype(F32)
    rowq[:, 0:8, :] = cum_high.reshape(BLOCKS, 8, GROUP)
    rowq[:, 8:16, :] = cum_mid.reshape(BLOCKS, 8, GROUP)
    rowq[:, 16:24, :] = (cum - cum_high - cum_mid).reshape(BLOCKS, 8, GROUP)
    rowq[:, 24:32, :] = (jnp.exp(last - cum) * step2).reshape(BLOCKS, 8, GROUP)
    rowq[:, 32:40, :] = jnp.exp(cum).reshape(BLOCKS, 8, GROUP)
    bq[...] = (cum - jnp.log(step2)).reshape(BLOCKS, 8, GROUP)

    above = lax.rem(my_y + 1, NY)
    below = lax.rem(my_y + NY - 1, NY)
    across = lax.rem(my_y + 2, NY)
    ups = my_z * NY + above
    downs = my_z * NY + below

    def y_copy(kind, c, slot, up):
        ref = gath.at[kind, slot, :, :, pl.ds(*SPANS[kind][c])]
        way = 0 if up else 1
        return remote(
            ref,
            ref,
            ys_send.at[kind, c, way],
            ys_recv.at[kind, c, way],
            head=ups if up else downs,
        )

    def f_copy(kind, c, slot, up):
        first = 0 if up else NZ // 2
        ref = gath.at[kind, slot, pl.ds(first, NZ // 2), :, pl.ds(*SPANS[kind][c])]
        way = 0 if up else 1
        return remote(
            ref,
            ref,
            yf_send.at[kind, c, way],
            yf_recv.at[kind, c, way],
            head=ups if up else downs,
        )

    z_above = lax.rem(my_z + 1, NZ) * NY + my_y
    z_below = lax.rem(my_z + NZ - 1, NZ) * NY + my_y

    def ring(kind, hop, up, block):
        half = NY // 2
        if hop < NZ // 2 - 1:
            ref = gath.at[kind, :, block, :, pl.ds(*SIDE[kind])]
        elif up:
            ref = gath.at[kind, pl.ds(0, half), block, :, pl.ds(*SIDE[kind])]
        else:
            ref = gath.at[kind, pl.ds(half, half), block, :, pl.ds(*SIDE[kind])]
        way = 0 if up else 1
        return remote(
            ref,
            ref,
            ring_out.at[kind, hop, way],
            ring_in.at[kind, hop, way],
            head=z_above if up else z_below,
        )

    def ring_send(kind, hop):
        ring(kind, hop, True, lax.rem(my_z + NZ - hop, NZ)).start()
        ring(kind, hop, False, lax.rem(my_z + hop, NZ)).start()

    def ring_arrive(kind, hop):
        ring(kind, hop, True, lax.rem(my_z + NZ - hop - 1, NZ)).wait_recv()
        ring(kind, hop, False, lax.rem(my_z + hop + 1, NZ)).wait_recv()

    def ring_done(kind, hop):
        ring(kind, hop, True, lax.rem(my_z + NZ - hop, NZ)).wait_send()
        ring(kind, hop, False, lax.rem(my_z + hop, NZ)).wait_send()

    def event_side(kind):
        for r in y_order:
            side_arrive(kind, r).wait_recv()
        ring_send(kind, 0)

    def event_ring(kind, hop):
        ring_arrive(kind, hop - 1)
        ring_send(kind, hop)

    def event_z(kind, c):
        for r in order:
            z_arrive(kind, c, r).wait_recv()
        y_copy(kind, c, my_y, True).start()
        y_copy(kind, c, my_y, False).start()

    def event_f(kind, c):
        y_copy(kind, c, below, True).wait_recv()
        f_copy(kind, c, below, True).start()
        y_copy(kind, c, above, False).wait_recv()
        f_copy(kind, c, above, False).start()

    def event_d(kind, c):
        f_copy(kind, c, across, True).wait_recv()
        f_copy(kind, c, across, False).wait_recv()

    def first_part(y, z):
        return gath.at[:, y, z, :, pl.ds(*FIRST)]

    def first_z(r):
        ref = first_part(my_y, my_z)
        there = lax.rem(my_z + r, NZ) * NY + my_y
        return remote(ref, ref, tz_send.at[r], tz_recv.at[my_z], head=there)

    def first_z_arrive(r):
        other = lax.rem(my_z + r, NZ)
        ref = first_part(my_y, other)
        return remote(ref, ref, tz_send.at[r], tz_recv.at[other], head=other * NY + my_y)

    def first_y(r):
        ref = gath.at[:, my_y, :, :, pl.ds(*FIRST)]
        there = my_z * NY + lax.rem(my_y + r, NY)
        return remote(ref, ref, ty_send.at[r], ty_recv.at[my_y], head=there)

    def first_y_arrive(r):
        other = lax.rem(my_y + r, NY)
        ref = gath.at[:, other, :, :, pl.ds(*FIRST)]
        return remote(ref, ref, ty_send.at[r], ty_recv.at[other], head=my_z * NY + other)

    def event_first():
        for r in order:
            first_z_arrive(r).wait_recv()
        for r in y_order:
            first_y(r).start()

    def event_first_done():
        for r in y_order:
            first_y_arrive(r).wait_recv()

    def event_halo():
        @pl.when(seq > 0)
        def _():
            halo_bc().wait_recv()
            halo_x().wait_recv()

        @pl.when(seq == 0)
        def _():
            bcx[:, 0:HALF] = jnp.zeros((8, HALF), F32)
            xbuf[0:HALO, :] = jnp.zeros((HALO, WIDTH), BF16)

        first = conv_bc(bcx[:, 0 : 2 * HALF])[:, HALF:]
        for kind in range(2):
            put_tile(kind, 0, [first] + quarters[1:4])
        for r in order:
            first_z(r).start()

    taps = taps_ref[...].astype(F32) * 0.5
    even = lax.broadcasted_iota(jnp.int32, (HALF, HALF), 1) < 64
    row1 = lax.broadcasted_iota(jnp.int32, (HALF, HALF), 0)
    col1 = lax.broadcasted_iota(jnp.int32, (HALF, HALF), 1)
    causal = row1 >= col1
    spread_row = lax.broadcasted_iota(jnp.int32, (40, HALF * HEADS), 0)
    spread_col = lax.broadcasted_iota(jnp.int32, (40, HALF * HEADS), 1) >> 7
    picked = (spread_row < 24) & ((spread_row & 7) == spread_col)
    spread_a = jnp.where(picked, 1.0, 0.0).astype(BF16)
    of_head = lax.broadcasted_iota(jnp.int32, (8, WIDTH), 1) >> 6

    def phase1(i):
        base = pl.multiple_of(i * GROUP, GROUP)
        for low in (0, HALF):
            for lane in range(0, WIDTH, HALF):
                span = slice(lane, lane + HALF)
                wide = xbuf[pl.ds(base + low, HALF + HALO), span].astype(F32)
                once = pltpu.roll(wide, 1, axis=0)
                older = pltpu.roll(wide * taps[1:2, span] + once * taps[0:1, span], 2, axis=0)
                half = (
                    wide[HALO:] * taps[3:4, span] + once[HALO:] * taps[2:3, span] + older[HALO:]
                )
                xs = (half + half * jnp.tanh(half)).astype(BF16)
                none = jnp.zeros_like(xs)
                xs_even[pl.ds(base + low, HALF), span] = jnp.where(even, xs, none)
                xs_odd[pl.ds(base + low, HALF), span] = jnp.where(even, none, xs)
        cols = rowq[i].T
        colb = cols.astype(BF16)
        colq[i] = colb
        ends = cols[GROUP - 8 :, 32:40]
        gone = jnp.zeros((8, WIDTH), F32)
        for h in range(HEADS):
            gone = jnp.where(of_head == h, ends[7:8, h : h + 1], gone)
        gones[i] = gone
        b_all = bq[i]
        for h in range(HEADS):
            if h % 2 == 0:
                two = dot(colb, spread_a[:, HALF * h : HALF * (h + 2)])
            a = two[:, HALF * (h % 2) : HALF * (h % 2 + 1)]
            b = b_all[h : h + 1, :]
            gap1 = jnp.where(causal, a[:HALF] - b[:, :HALF], MASKED)
            gap2 = a[HALF:] - b[:, :HALF]
            gap3 = jnp.where(causal, a[HALF:] - b[:, HALF:], MASKED)
            near[i, h] = jnp.exp(gap1.astype(BF16))
            far[i, h, :, 0:HALF] = jnp.exp(gap2.astype(BF16))
            far[i, h, :, HALF:] = jnp.exp(gap3.astype(BF16))

    def step1(i):
        block = lax.rem(i + 1, BLOCKS)

        @pl.when((i == 0) | ((lax.rem(block, PER) == 0) & (block > 0)))
        def _():
            x_copy(block // PER).wait()

        phase1(block)

    def run(count, unit, before):
        def step(i):
            for when, events in before.items():

                @pl.when(i == when)
                def _(events=events):
                    for event, *which in events:
                        event(*which)

            unit(i)

        loop(count, step)

    run(
        BLOCKS,
        step1,
        {
            5: [(event_side, 0), (event_side, 1), (event_halo,), (send_z, 1, 0)],
            10: [(event_z, 0, 0)],
            13: [(event_ring, 0, 1), (event_z, 0, 1), (send_z, 1, 1)],
            15: [(event_ring, 1, 1), (event_first,)],
            17: [(event_f, 0, 0)],
            19: [(event_f, 0, 1), (event_ring, 0, 2)],
        },
    )

    spread_row = lax.broadcasted_iota(jnp.int32, (40, WIDTH), 0)
    spread_col = lax.broadcasted_iota(jnp.int32, (40, WIDTH), 1) >> 6
    spread_w = jnp.where(spread_row == spread_col + 24, 1.0, 0.0).astype(BF16)
    spread_e = jnp.where(spread_row == spread_col + 32, 1.0, 0.0).astype(BF16)
    upper4 = lax.broadcasted_iota(jnp.int32, (8, HALF), 0) < 4

    state[...] = jnp.zeros_like(state)

    so_far = jnp.ones((8, WIDTH), F32)
    prec[0] = so_far
    for i in range(BLOCKS):
        so_far = so_far * gones[i]
        prec[i + 1] = so_far
    got_decay[seq] = so_far

    def others(count, me, body):
        loop(count - 1, lambda r: body(lax.rem(me + 1 + r, count)))

    def sd_copy(j, slot):
        return remote(
            prec.at[BLOCKS], got_decay.at[slot], sd_send.at[j], sd_recv.at[slot], seq=j
        )

    others(NSEQ, seq, lambda j: sd_copy(j, seq).start())

    def assemble(kind, j):
        lane = pl.multiple_of(j * HALF, HALF)
        blocks = ([], [])
        for pair in range(NHEAD // 2):
            y, z = (2 * pair) // NZ, (2 * pair) % NZ
            first = gath[kind, y, z, :, pl.ds(lane, HALF)].astype(F32)
            second = gath[kind, y, z + 1, :, pl.ds(lane, HALF)].astype(F32)
            for e in range(2):
                one = first[8 * e : 8 * e + 8]
                two = second[8 * e : 8 * e + 8]
                left = jnp.where(upper4, one, pltpu.roll(two, 4, axis=0))
                right = jnp.where(upper4, pltpu.roll(one, 4, axis=0), two)
                blocks[e].append(jnp.concatenate([left, right], axis=1))
        return [jnp.concatenate(block, axis=0) for block in blocks]

    def phase2(j):
        blocks = (2 * j, 2 * j + 1)
        bases = [pl.multiple_of(i * GROUP, GROUP) for i in blocks]
        weights = [dot(colq[i], spread_w) for i in blocks]
        b_ts = [b_t.astype(BF16) for b_t in assemble(0, j)]
        weighted = []
        for base, weight in zip(bases, weights):
            xs = (xs_even[pl.ds(base, GROUP), :] + xs_odd[pl.ds(base, GROUP), :]).astype(F32)
            weighted.append((weight * xs).astype(BF16))
        news = [dot(b_t, w) for b_t, w in zip(b_ts, weighted)]
        for i, b_t in zip(blocks, b_ts):
            bmat[i] = b_t
        goes = [gones[i] for i in blocks]
        old = state[...]
        local_state[2 * j] = old
        old = old * goes[0][0:1] + news[0]
        local_state[2 * j + 1] = old
        state[...] = old * goes[1][0:1] + news[1]

    def phase3(j):
        blocks = (2 * j, 2 * j + 1)
        bases = [pl.multiple_of(i * GROUP, GROUP) for i in blocks]
        c_is = [c_t.T.astype(BF16) for c_t in assemble(1, j)]
        scores = [dot(c_i, bmat[i]).astype(BF16) for i, c_i in zip(blocks, c_is)]
        for i, c_i in zip(blocks, c_is):
            cmat[i] = c_i
        for pair in range(HEADS // 2):
            span = slice(HALF * pair, HALF * (pair + 1))
            results = []
            for i, base, score in zip(blocks, bases, scores):
                top = score[:HALF, :HALF]
                low_rows = score[HALF:, :]
                xe = xs_even[pl.ds(base, GROUP), span]
                xo = xs_odd[pl.ds(base, GROUP), span]
                m1 = jnp.concatenate(
                    [top * near[i, 2 * pair], top * near[i, 2 * pair + 1]], axis=1
                )
                m2 = jnp.concatenate(
                    [low_rows * far[i, 2 * pair], low_rows * far[i, 2 * pair + 1]], axis=1
                )
                x1 = jnp.concatenate([xe[:HALF], xo[:HALF]], axis=0)
                x2 = jnp.concatenate([xe, xo], axis=0)
                results.append((dot(m1, x1), dot(m2, x2)))
            for base, (upper_rows, lower_rows) in zip(bases, results):
                gate = zbuf[pl.ds(base, GROUP), span].astype(F32)
                ydiag[pl.ds(base, HALF), span] = upper_rows * gate[:HALF]
                ydiag[pl.ds(base + HALF, HALF), span] = lower_rows * gate[HALF:]

    def gates(i):
        base = pl.multiple_of(i * GROUP, GROUP)
        half = zbuf[pl.ds(base, GROUP), :].astype(F32) * 0.5
        gate = half + half * jnp.tanh(half)
        zbuf[pl.ds(base, GROUP), :] = gate.astype(BF16)
        grown = dot(colq[i], spread_e)
        egate[pl.ds(base, GROUP), :] = (gate * grown).astype(BF16)

    z_copy.wait()
    run(BLOCKS // 2, gates, {0: [(event_z, 1, 0)]})
    run(
        PAIRS,
        phase2,
        {
            0: [(event_ring, 1, 2), (event_first_done,)],
            1: [(event_d, 0, 0)],
            2: [(event_ring, 0, 3), (event_z, 1, 1)],
            4: [(event_d, 0, 1)],
            6: [(event_ring, 1, 3)],
            7: [(ring_arrive, 0, 3)],
            8: [(event_f, 1, 0)],
        },
    )

    def st_copy(j, slot):
        place = pl.multiple_of(j * PART, PART)
        return remote(
            state.at[pl.ds(place, PART)], got.at[slot], st_send.at[j], st_recv.at[slot], seq=j
        )

    def cb_copy(j, slot):
        place = pl.multiple_of(slot * PART, PART)
        return remote(
            back.at[j], carry_in.at[pl.ds(place, PART)], cb_send.at[j], cb_recv.at[slot], seq=j
        )

    others(NSEQ, seq, lambda j: st_copy(j, seq).start())
    got[seq] = state[pl.ds(pl.multiple_of(seq * PART, PART), PART), :]
    run(BLOCKS // 2, lambda i: gates(BLOCKS // 2 + i), {6: [(event_f, 1, 1)]})

    def event_states():
        others(NSEQ, seq, lambda j: sd_copy(j, j).wait_recv())
        others(NSEQ, seq, lambda j: st_copy(j, j).wait_recv())
        carry = jnp.zeros((PART, WIDTH), F32)
        for j in range(NSEQ):
            back[j] = carry
            carry = carry * got_decay[j, 0:1, :] + got[j]
        others(NSEQ, seq, lambda j: cb_copy(j, seq).start())
        carry_in[pl.ds(pl.multiple_of(seq * PART, PART), PART), :] = back[seq]

    run(
        PAIRS,
        lambda i: phase3(lax.rem(i + 7, PAIRS)),
        {
            0: [(ring_arrive, 1, 3)],
            4: [(event_d, 1, 0), (event_states,)],
            7: [(event_d, 1, 1)],
        },
    )
    others(NSEQ, seq, lambda j: cb_copy(j, j).wait_recv())

    ones = jnp.ones((8, WIDTH), BF16)

    def g_copy(i):
        base = pl.multiple_of(i * GROUP, GROUP)
        return pltpu.make_async_copy(
            xbuf.at[pl.ds(HALO + base, GROUP)], g_hbm.at[pl.ds(base, GROUP)], g_sem.at[i]
        )

    parts = (pl.ds(0, 16), pl.ds(16, 8))

    def sz_copy(p, r):
        there = lax.rem(my_z + r, NZ) * NY + my_y
        return remote(
            sums_row.at[parts[p]],
            sums_z.at[my_z, parts[p]],
            sz_send.at[p, r],
            sz_recv.at[p, my_z],
            head=there,
        )

    def sz_arrive(p, r):
        other = lax.rem(my_z + r, NZ)
        return remote(
            sums_row.at[parts[p]],
            sums_z.at[other, parts[p]],
            sz_send.at[p, r],
            sz_recv.at[p, other],
            head=other * NY + my_y,
        )

    def sy_copy(p, r):
        there = my_z * NY + lax.rem(my_y + r, NY)
        return remote(
            half_sums.at[parts[p]],
            sums_y.at[my_y, parts[p]],
            sy_send.at[p, r],
            sy_recv.at[p, my_y],
            head=there,
        )

    def sy_arrive(p, r):
        other = lax.rem(my_y + r, NY)
        return remote(
            half_sums.at[parts[p]],
            sums_y.at[other, parts[p]],
            sy_send.at[p, r],
            sy_recv.at[p, other],
            head=my_z * NY + other,
        )

    def sums_start(p):
        for r in order:
            sz_copy(p, r).start()
        sums_z[my_z, parts[p], :] = sums_row[parts[p], :]

    def sums_turn(p):
        for r in order:
            sz_arrive(p, r).wait_recv()
        added = sums_z[0, parts[p], :]
        for k in range(1, NZ):
            added = added + sums_z[k, parts[p], :]
        half_sums[parts[p], :] = added
        sums_y[my_y, parts[p], :] = added
        for r in (1, 3, 2):
            sy_copy(p, r).start()

    def sums_end(p):
        for r in (1, 3, 2):
            sy_arrive(p, r).wait_recv()
        added = sums_y[0, parts[p], :]
        for k in range(1, NY):
            added = added + sums_y[k, parts[p], :]
        total_ref[parts[p], :] = added

    def phase4(j):
        blocks = [4 * j + e for e in range(4)]
        bases = [pl.multiple_of(i * GROUP, GROUP) for i in blocks]
        operands = []
        for i in blocks:
            whole = local_state[i] + carry_in[...] * prec[i][0:1]
            whole_high = whole.astype(BF16)
            whole_low = (whole - whole_high.astype(F32)).astype(BF16)
            operands.append(jnp.concatenate([whole_high, whole_low], axis=0))
        products = []
        for i, operand in zip(blocks, operands):
            c_i = cmat[i]
            products.append(dot(jnp.concatenate([c_i, c_i], axis=1), operand))
        values = []
        for base, carried in zip(bases, products):
            factor = egate[pl.ds(base, GROUP), :].astype(F32)
            values.append((ydiag[pl.ds(base, GROUP), :] + carried * factor).astype(BF16))
        for i, base, g in zip(blocks, bases, values):
            sums = lax.dot_general(
                ones, g * g, (((1,), (1,)), ((), ())), preferred_element_type=F32
            )
            xbuf[pl.ds(HALO + base, GROUP), :] = g
            sums_row[pl.ds(jnp.where(i < 12, i, i + 4), 1), :] = sums[0:1]
        for i in blocks:
            g_copy(i).start()

        @pl.when(j == 2)
        def _():
            sums_start(0)

    loop(BLOCKS // 4, phase4)
    sums_start(1)
    sums_turn(0)
    sums_turn(1)
    sums_end(0)

    @pl.when(seq < NSEQ - 1)
    def _():
        halo_bc().wait_send()
        halo_x().wait_send()

    for r in order:
        first_z(r).wait_send()
    for r in y_order:
        first_y(r).wait_send()
    others(NSEQ, seq, lambda j: sd_copy(j, seq).wait_send())
    for kind in range(2):
        for c in range(2):
            for r in order:
                z_send(kind, c, r).wait_send()
            y_copy(kind, c, my_y, True).wait_send()
            y_copy(kind, c, my_y, False).wait_send()
            f_copy(kind, c, below, True).wait_send()
            f_copy(kind, c, above, False).wait_send()
        for r in y_order:
            side_send(kind, r).wait_send()
        for hop in range(NZ // 2):
            ring_done(kind, hop)
    others(NSEQ, seq, lambda j: st_copy(j, seq).wait_send())
    others(NSEQ, seq, lambda j: cb_copy(j, seq).wait_send())

    loop(BLOCKS, lambda i: g_copy(i).wait())
    for p in range(2):
        for r in order:
            sz_copy(p, r).wait_send()
    sums_end(1)
    for p in range(2):
        for r in (1, 3, 2):
            sy_copy(p, r).wait_send()


def scale(g_hbm, total_hbm, gain_hbm, out_hbm, g_in, g_out, total, gain_in, in_sem, out_sem, sem):
    rows = GROUP * SCALED

    def come(k):
        part = pl.ds(rows * k, rows)
        return pltpu.make_async_copy(g_hbm.at[part], g_in.at[part], in_sem.at[k])

    def go(k):
        part = pl.ds(rows * k, rows)
        return pltpu.make_async_copy(g_out.at[part], out_hbm.at[part], out_sem.at[k])

    total_copy = pltpu.make_async_copy(total_hbm, total, sem.at[0])
    gain_copy = pltpu.make_async_copy(gain_hbm, gain_in, sem.at[1])
    total_copy.start()
    gain_copy.start()
    for k in range(BLOCKS // SCALED):
        come(k).start()
    total_copy.wait()
    gain_copy.wait()
    gain = gain_in[...][None, :]
    factor = lax.rsqrt(total[...] * (1.0 / (NHEAD * WIDTH)) + 1e-05).T
    for k in range(BLOCKS // SCALED):
        come(k).wait()
        for j in range(SCALED * k, SCALED * (k + 1)):
            place = j if j < 12 else j + 4
            part = slice(GROUP * j, GROUP * (j + 1))
            g_out[part, :] = g_in[part, :] * (factor[:, place : place + 1] * gain).astype(BF16)
        go(k).start()
    for k in range(BLOCKS // SCALED):
        go(k).wait()


def body(x_rows, z_rows, b_rows, c_rows, step_raw, conv_x, conv_b, conv_c, decay_rate, norm_gain):
    vmem = pl.BlockSpec(memory_space=pltpu.VMEM)
    hbm = pl.BlockSpec(memory_space=pl.ANY)
    smem = pl.BlockSpec(memory_space=pltpu.SMEM)
    dma = pltpu.SemaphoreType.DMA
    g, totals = pl.pallas_call(
        layer,
        out_shape=(
            jax.ShapeDtypeStruct((LENGTH, WIDTH), BF16),
            jax.ShapeDtypeStruct((24, GROUP), F32),
        ),
        in_specs=[hbm, hbm, vmem, vmem, vmem, vmem, vmem, vmem, smem],
        out_specs=(hbm, vmem),
        scratch_shapes=[
            pltpu.VMEM((HALO + LENGTH, WIDTH), BF16),
            pltpu.VMEM((LENGTH, WIDTH), BF16),
            pltpu.VMEM((LENGTH, WIDTH), BF16),
            pltpu.VMEM((LENGTH, WIDTH), BF16),
            pltpu.VMEM((LENGTH, WIDTH), BF16),
            pltpu.VMEM((BLOCKS, HEADS, HALF, HALF), BF16),
            pltpu.VMEM((BLOCKS, HEADS, HALF, GROUP), BF16),
            pltpu.VMEM((2, NY, NZ, 16, HALF * PAIRS), BF16),
            pltpu.VMEM((BLOCKS, GROUP, STATE), BF16),
            pltpu.VMEM((BLOCKS, STATE, GROUP), BF16),
            pltpu.VMEM((LENGTH, WIDTH), F32),
            pltpu.VMEM((BLOCKS, STATE, WIDTH), F32),
            pltpu.VMEM((BLOCKS, GROUP, 40), BF16),
            pltpu.VMEM((BLOCKS, 40, GROUP), F32),
            pltpu.VMEM((BLOCKS, 8, GROUP), F32),
            pltpu.VMEM((BLOCKS, 8, GROUP), F32),
            pltpu.VMEM((8, HALF + LENGTH), F32),
            pltpu.VMEM((BLOCKS + 1, 8, WIDTH), F32),
            pltpu.VMEM((STATE, WIDTH), F32),
            pltpu.VMEM((BLOCKS, 8, WIDTH), F32),
            pltpu.VMEM((NSEQ, 8, WIDTH), F32),
            pltpu.VMEM((NSEQ, PART, WIDTH), F32),
            pltpu.VMEM((NSEQ, PART, WIDTH), F32),
            pltpu.VMEM((STATE, WIDTH), F32),
            pltpu.VMEM((24, GROUP), F32),
            pltpu.VMEM((NZ, 24, GROUP), F32),
            pltpu.VMEM((24, GROUP), F32),
            pltpu.VMEM((NY, 24, GROUP), F32),
            dma((LOADS,)),
            dma,
            dma((BLOCKS,)),
            dma((2,)),
            dma((2,)),
            dma((2, 2, NZ)),
            dma((2, 2, NZ)),
            dma((2, 2, 2)),
            dma((2, 2, 2)),
            dma((2, 2, 2)),
            dma((2, 2, 2)),
            dma((NSEQ,)),
            dma((NSEQ,)),
            dma((NSEQ,)),
            dma((NSEQ,)),
            dma((NZ,)),
            dma((NZ,)),
            dma((NY,)),
            dma((NY,)),
            dma((NSEQ,)),
            dma((NSEQ,)),
            dma((2, NY)),
            dma((2, NY)),
            dma((2, NZ // 2, 2)),
            dma((2, NZ // 2, 2)),
            dma((2, NZ)),
            dma((2, NZ)),
            dma((2, NY)),
            dma((2, NY)),
        ],
        compiler_params=pltpu.CompilerParams(
            collective_id=0, has_side_effects=True, vmem_limit_bytes=60 * 2**20
        ),
        name="layer",
    )(x_rows, z_rows, b_rows.T, c_rows.T, step_raw.T, conv_x, conv_b, conv_c, decay_rate)
    return pl.pallas_call(
        scale,
        out_shape=jax.ShapeDtypeStruct((LENGTH, WIDTH), BF16),
        in_specs=[hbm, hbm, hbm],
        out_specs=hbm,
        scratch_shapes=[
            pltpu.VMEM((LENGTH, WIDTH), BF16),
            pltpu.VMEM((LENGTH, WIDTH), BF16),
            pltpu.VMEM((24, GROUP), F32),
            pltpu.VMEM((WIDTH,), F32),
            dma((BLOCKS // SCALED,)),
            dma((BLOCKS // SCALED,)),
            dma((2,)),
        ],
        compiler_params=pltpu.CompilerParams(vmem_limit_bytes=60 * 2**20),
        name="scale",
    )(g, totals, norm_gain)


def solution(mesh):
    placed = (
        P("seq", "head"),
        P("seq", "head"),
        P("seq", "head"),
        P("seq", "head"),
        P("seq", "head"),
        P(None, "head"),
        P(None, "head"),
        P(None, "head"),
        P("head"),
        P("head"),
    )
    return jax.shard_map(
        body, mesh=mesh, in_specs=placed, out_specs=P("seq", "head"), check_vma=False
    )
```
